32 devices in a mesh: req: 4 (over z), ctx: 8 (over y, x, core).
Axes of the slice: x: 2, y: 2, z: 4, core: 2. Of those that a mesh axis runs over, the one named last changes fastest.
Arguments:
- residual: bfloat16 [16, 7168], P('ctx', 'req'), may hold values from -6 to 6
- query: bfloat16 [16, 128, 576], P('req', 'ctx'), may hold values from -260 to 260
- latent_cache: bfloat16 [8, 4096, 576], P('req', 'ctx'), may hold values from -6 to 6
- lengths: int32 [8], P('req'), may hold values from 4 to 4096, as said below
- w_uv: bfloat16 [128, 512, 128], P('ctx'), may hold values from -6 to 6
- w_o: bfloat16 [16384, 7168], P('ctx', 'req'), may hold values from -0.046875 to 0.046875
- norm_gain: bfloat16 [7168], replicated, may hold values from 0.099609375 to 1.8984375
- routes: int32 [16, 4], replicated, may hold values from 0 to 15, all different within a row; in each aligned block of 16 rows (0 to 15, 16 to 31, ...) at most 8 rows name the same one
- route_weight: float32 [16, 4], replicated, may hold values from 0.2 to 1
- w_gate: bfloat16 [16, 2048, 7168], P('req', 'ctx'), may hold values from -0.0625 to 0.0625
- w_up: bfloat16 [16, 2048, 7168], P('req', 'ctx'), may hold values from -0.0625 to 0.0625
- w_down: bfloat16 [16, 2048, 7168], P('req', 'ctx'), may hold values from -0.125 to 0.125
Outputs:
- layer_out: bfloat16 [16, 7168], P('req', 'ctx')
The draws below stay inside these ranges and needn't reach their ends.
Inputs may be any that keep to these rules, and one draw needn't show every extreme that they name: `lengths`: some request has length exactly 4096. `routes`: each token names 4 different experts; over all 16 tokens no expert is named by more than 8 tokens, a bound that some block reaches.
All inputs are finite; a program needn't handle non-finite values.
Results may differ from the reference program's by a relative error of at most 0.035.
Values may be sent and summed in bfloat16 or wider, within the bound.
No kernel may reach another device: no remote copies, remote signals or barrier semaphores. Data moves between devices by JAX's collectives and lax.ppermute only.
A program may use at most 128 MiB of HBM per device.

```python
import math
import jax
import jax.numpy as jnp
import numpy as np
from jax import lax

D = 7168
H = 128
KV_LAT = 512
VD = 128
FF = 2048
EXPERTS = 16
TOP = 4
Q_TOK = 2
CTX_DEV = 512
LATW = 576
HV = 16384
REQUESTS = 8
CONTEXT = 4096
TOKENS = 16
CAP = 8
N_CTX = 8


def draw_latent_cache(key, part):
    base = jnp.clip(jax.random.normal(jax.random.fold_in(key, 12), (REQUESTS, CONTEXT, LATW), jnp.float32), -6.0, 6.0)
    return base.astype(jnp.bfloat16)


def draw_query(key, part):
    base = jnp.clip(jax.random.normal(jax.random.fold_in(key, 13), (TOKENS, H, LATW), jnp.float32), -6.0, 6.0)
    return base.astype(jnp.bfloat16)


def draw_lengths(key, part):
    drawn = jax.random.randint(jax.random.fold_in(key, 16), (REQUESTS,), 4, CONTEXT + 1)
    longest = jax.random.randint(jax.random.fold_in(key, 17), (), 0, REQUESTS)
    return jnp.where(jnp.arange(REQUESTS, dtype=jnp.int32) == longest, CONTEXT, drawn).astype(jnp.int32)


def steps_of(key, extent, pieces, low, high):
    loudness = 1.0
    for axis_at, blocks in pieces:
        heights = jax.random.uniform(jax.random.fold_in(jax.random.fold_in(key, 6), axis_at), (blocks,), jnp.float32, low / len(pieces), high / len(pieces))
        loudness = loudness * jnp.repeat(jnp.exp(heights), extent[axis_at] // blocks).reshape((-1,) + (1,) * (len(extent) - 1 - axis_at))
    return loudness


def shared_out(rng, own, number, rows, number_of, top, most, lean):
    order = jax.random.permutation(rng, number_of)
    heavy_load, usual = portions_of(number_of, rows * top, most, lean, True), portions_of(number_of, rows * top, most, lean, False)
    places = jnp.arange(number_of)

    def named(tallies, rotation):
        used = int((tallies > 0).sum())
        fixed = max(1, used // 4)
        moved = fixed + (places - fixed + rotation * (used - fixed)) % max(1, number_of - fixed)
        return jnp.zeros((number_of,), jnp.int32).at[order[jnp.where(places < fixed, places, moved)]].set(jnp.asarray(tallies, jnp.int32))

    tallies = jnp.where(number % 4 == 0, named(heavy_load, number // 4), named(usual, number - number // 4 - 1))
    mixed = jax.random.permutation(jax.random.fold_in(own, 3), number_of)
    donor, taker = mixed[0:number_of // 2 * 2:2], mixed[1:number_of // 2 * 2:2]
    room = jnp.minimum(tallies[donor] - 1, most - tallies[taker]) // 2
    room = jnp.where((donor == order[0]) | (taker == order[0]) | (tallies[taker] == 0), 0, jnp.maximum(room, 0))
    moved = jax.random.randint(jax.random.fold_in(own, 4), (number_of // 2,), 0, 1 << 20) % (room + 1)
    tallies = tallies.at[donor].add(-moved).at[taker].add(moved)
    members = jnp.searchsorted(jnp.cumsum(tallies), jnp.arange(rows * top), side="right").astype(jnp.int32)
    table = members.reshape(top, rows).T
    table = table[jax.random.permutation(jax.random.fold_in(own, 1), rows)]
    rotation = jax.random.randint(jax.random.fold_in(own, 2), (rows, 1), 0, top)
    return jnp.take_along_axis(table, (jnp.arange(top)[None, :] + rotation) % top, axis=1)


def portions_of(number_of, total, most, lean, full):
    weights = [(1 << 20) // math.isqrt(rank ** lean) + 1 for rank in range(1, number_of + 1)]
    largest = most if full else min(most, max(-(-total // number_of), total * weights[0] // sum(weights)))
    least = 1 if total - largest >= number_of - 1 else 0
    given, spare = [largest] + [least] * (number_of - 1), total - largest - least * (number_of - 1)
    while spare > 0:
        free = [i for i in range(1, number_of) if given[i] < largest] or [i for i in range(1, number_of) if given[i] < most]
        mass, budget = sum([weights[i] for i in free]), spare
        for i in free:
            extra = min(most - given[i], max(1, budget * weights[i] // mass), spare)
            given[i] = given[i] + extra
            spare = spare - extra
    return np.array(given)


def scatter_about(stream_key, dims, scale, reach, pieces=(), kind=jnp.bfloat16):
    result = jax.random.normal(stream_key, dims, jnp.float32) * scale
    if len(pieces) > 0:
        result = steps_of(stream_key, dims, pieces, -0.22, 0.18) * result
    return jnp.clip(result, min=-reach, max=reach).astype(kind)


def setup_inputs(seed: int = 0) -> dict:
    key_of = jax.random.split(jax.random.key(seed), 13)
    residual = scatter_about(key_of[0], (TOKENS, D), 1.0, 6.0, ((0, 8), (1, 4)))
    query = draw_query(jax.random.fold_in(key_of[12], 71), 0)
    latent_cache = draw_latent_cache(jax.random.fold_in(key_of[12], 71), 0)
    lengths = draw_lengths(jax.random.fold_in(key_of[12], 71), 0)
    w_uv = scatter_about(key_of[4], (H, KV_LAT, VD), 0.4, 6.0, ((0, 8),))
    w_o = scatter_about(key_of[5], (HV, D), HV ** -0.5, 0.046875, ((0, 8), (1, 4)))
    norm_gain = jnp.clip(1.0 + 0.18 * jax.random.normal(key_of[6], (D,), jnp.float32), 0.099609375, 1.8984375).astype(jnp.bfloat16)
    routes_keys = jax.random.split(jax.random.fold_in(key_of[7], 1), TOKENS // TOKENS)
    routes_turns = jax.random.permutation(jax.random.fold_in(key_of[7], 3), TOKENS // TOKENS)
    routes = jax.vmap(lambda own, number: shared_out(jax.random.fold_in(key_of[7], 2), own, number, TOKENS, EXPERTS, TOP, CAP, 1))(routes_keys, routes_turns).reshape((TOKENS, TOP))
    route_weight = jnp.clip(jax.random.uniform(key_of[8], (TOKENS, TOP), jnp.float32, 0.2, 1.0), 0.2, 1.0)
    w_gate = scatter_about(key_of[9], (EXPERTS, FF, D), D ** -0.5, 0.0625, ((0, 4), (1, 8)))
    w_up = scatter_about(key_of[10], (EXPERTS, FF, D), D ** -0.5, 0.0625, ((0, 4), (1, 8)))
    w_down = scatter_about(key_of[11], (EXPERTS, FF, D), FF ** -0.5, 0.125, ((0, 4), (1, 8)))
    return {"residual": residual, "query": query, "latent_cache": latent_cache, "lengths": lengths, "w_uv": w_uv, "w_o": w_o, "norm_gain": norm_gain, "routes": routes, "route_weight": route_weight, "w_gate": w_gate, "w_up": w_up, "w_down": w_down}


SOFTMAX_SCALE = 192.0 ** (-0.5)
NEG_FILL = -1e+30
NORM_EPS = 1e-06

def local_softmax(scores, visible, values):
    masked = jnp.where(visible, scores, -jnp.inf)
    peaks = lax.optimization_barrier(jnp.max(masked, axis=-1))
    peaks = jnp.where(jnp.any(visible, axis=-1), peaks, jnp.zeros_like(peaks))
    raised = jnp.exp(masked - peaks[..., None])
    totals = lax.optimization_barrier(jnp.sum(raised, axis=-1))
    probs = lax.optimization_barrier(raised.astype(jnp.bfloat16)).astype(jnp.float32)
    mixed = jnp.einsum('rqp,rpd->rqd', probs, values, precision=lax.Precision.HIGHEST)
    filled = totals > 0.0
    safe_totals = jnp.where(filled, totals, jnp.ones_like(totals))
    shard_out = jnp.where(filled[..., None], mixed / safe_totals[..., None], jnp.zeros_like(mixed)).astype(jnp.bfloat16)
    shard_log = jnp.where(filled, peaks + jnp.log(safe_totals), jnp.full_like(peaks, NEG_FILL))
    return (shard_out, shard_log)

def reference(residual, query, latent_cache, lengths, w_uv, w_o, norm_gain, routes, route_weight, w_gate, w_up, w_down):
    grouped = query.reshape(REQUESTS, Q_TOK * H, LATW).astype(jnp.float32)
    shards = latent_cache.reshape(REQUESTS, N_CTX, CTX_DEV, LATW)
    offsets = jnp.arange(Q_TOK * H, dtype=jnp.int32) // H
    limits = lengths[:, None] - Q_TOK + offsets[None, :]

    def one_shard(index):
        block = lax.dynamic_index_in_dim(shards, index, 1, keepdims=False).astype(jnp.float32)
        scores = jnp.einsum('rqd,rpd->rqp', grouped, block, precision=lax.Precision.HIGHEST) * SOFTMAX_SCALE
        positions = index * CTX_DEV + jnp.arange(CTX_DEV, dtype=jnp.int32)
        visible = positions[None, None, :] <= limits[:, :, None]
        return local_softmax(scores, visible, block[:, :, :KV_LAT])
    parts, logs = lax.map(one_shard, jnp.arange(N_CTX, dtype=jnp.int32))
    top_log = lax.optimization_barrier(jnp.max(logs, axis=0))
    factors = jnp.exp(logs - top_log[None])
    numer = lax.optimization_barrier(jnp.sum(factors[..., None] * parts.astype(jnp.float32), axis=0))
    denom = lax.optimization_barrier(jnp.sum(factors, axis=0))
    latent = (numer / denom[..., None]).astype(jnp.bfloat16).reshape(TOKENS, H, KV_LAT)
    projected = jnp.einsum('thd,hde->the', latent.astype(jnp.float32), w_uv.astype(jnp.float32), precision=lax.Precision.HIGHEST)
    head_value = projected.astype(jnp.bfloat16).reshape(TOKENS, HV)
    attention = jnp.dot(head_value, w_o, preferred_element_type=jnp.float32)
    mid = (residual.astype(jnp.float32) + attention).astype(jnp.bfloat16)
    widened = mid.astype(jnp.float32)
    scale_rows = lax.rsqrt(lax.optimization_barrier(jnp.mean(widened * widened, axis=-1, keepdims=True)) + NORM_EPS)
    normed = (widened * scale_rows * norm_gain.astype(jnp.float32)).astype(jnp.bfloat16)
    expert_ids = jnp.arange(EXPERTS, dtype=jnp.int32)
    coefs = lax.optimization_barrier(jnp.sum(jnp.where(routes[:, :, None] == expert_ids[None, None, :], route_weight[:, :, None], jnp.zeros_like(route_weight)[:, :, None]), axis=1))

    def expert_step(carry, items):
        gate_w, up_w, down_w, coef = items
        gate_vals = jnp.dot(normed, gate_w.T, preferred_element_type=jnp.float32)
        up_vals = jnp.dot(normed, up_w.T, preferred_element_type=jnp.float32)
        hidden = (jax.nn.silu(gate_vals) * up_vals * coef[:, None]).astype(jnp.bfloat16)
        return (carry + jnp.dot(hidden, down_w, preferred_element_type=jnp.float32), None)
    moe_out, _ = lax.scan(expert_step, jnp.zeros((TOKENS, D), jnp.float32), (w_gate, w_up, w_down, coefs.T))
    return (mid.astype(jnp.float32) + moe_out).astype(jnp.bfloat16)
```

```python
import jax
import jax.numpy as jnp
from jax import lax
from jax.sharding import PartitionSpec as P

SOFTMAX_SCALE = 192.0 ** (-0.5)
NEG_FILL = -1e30
NORM_EPS = 1e-06


def gather_all(x, axes, size):
    spread = jnp.broadcast_to(x[None], (size,) + x.shape)
    return lax.all_to_all(spread, axes, split_axis=0, concat_axis=0, tiled=True)


def local_softmax(scores, visible, values):
    masked = jnp.where(visible, scores, -jnp.inf)
    peaks = jnp.max(masked, axis=-1)
    peaks = jnp.where(jnp.any(visible, axis=-1), peaks, jnp.zeros_like(peaks))
    raised = jnp.exp(masked - peaks[..., None])
    totals = jnp.sum(raised, axis=-1)
    probs = raised.astype(jnp.bfloat16)
    mixed = jnp.einsum("rqp,rpd->rqd", probs, values, preferred_element_type=jnp.float32)
    filled = totals > 0.0
    safe_totals = jnp.where(filled, totals, jnp.ones_like(totals))
    shard_out = jnp.where(
        filled[..., None], mixed / safe_totals[..., None], jnp.zeros_like(mixed)
    ).astype(jnp.bfloat16)
    shard_log = jnp.where(filled, peaks + jnp.log(safe_totals), jnp.full_like(peaks, NEG_FILL))
    return (shard_out, shard_log)


def local(
    residual,
    query,
    latent_cache,
    lengths,
    w_uv,
    w_o,
    norm_gain,
    routes,
    route_weight,
    w_gate,
    w_up,
    w_down,
):
    n_ctx = lax.axis_size("ctx")
    n_req = lax.axis_size("req")
    req_local, ctx_local, _ = latent_cache.shape
    heads_local, lat_width, value_width = w_uv.shape
    tok_local = query.shape[0]
    q_tokens = tok_local // req_local
    queries = gather_all(query, "ctx", n_ctx)
    queries = queries.reshape(n_ctx, req_local, q_tokens * heads_local, query.shape[2])
    grouped = jnp.swapaxes(queries, 0, 1).reshape(req_local, -1, query.shape[2])
    scores = (
        jnp.einsum("rqd,rpd->rqp", grouped, latent_cache, preferred_element_type=jnp.float32)
        * SOFTMAX_SCALE
    )
    positions = lax.axis_index("ctx") * ctx_local + jnp.arange(ctx_local, dtype=jnp.int32)
    offsets = (jnp.arange(grouped.shape[1], dtype=jnp.int32) // heads_local) % q_tokens
    limits = lengths[:, None] - q_tokens + offsets[None, :]
    visible = positions[None, None, :] <= limits[:, :, None]
    shard_out, shard_log = local_softmax(scores, visible, latent_cache[:, :, :lat_width])
    rows = tok_local * heads_local

    def by_owner(x):
        x = x.reshape((req_local, n_ctx, q_tokens * heads_local) + x.shape[2:])
        return jnp.swapaxes(x, 0, 1).reshape((n_ctx, rows) + x.shape[3:])

    log_rows = by_owner(shard_log)
    log_high = lax.reduce_precision(log_rows, 8, 7)
    log_low = log_rows - log_high
    log_row = jnp.concatenate([log_high, log_low], axis=1).astype(jnp.bfloat16)
    log_row = jnp.pad(log_row, ((0, 0), (0, -2 * rows % lat_width))).reshape(n_ctx, -1, lat_width)
    packed = jnp.concatenate([by_owner(shard_out), log_row], axis=1)
    landed = lax.all_to_all(packed, "ctx", split_axis=0, concat_axis=0, tiled=True)
    outs_in = landed[:, :rows].astype(jnp.float32)
    logs_in = landed[:, rows:].reshape(n_ctx, -1).astype(jnp.float32)
    logs_in = logs_in[:, :rows] + logs_in[:, rows : 2 * rows]
    top_log = jnp.max(logs_in, axis=0)
    factors = jnp.exp(logs_in - top_log[None])
    numer = jnp.sum(factors[..., None] * outs_in, axis=0)
    denom = jnp.sum(factors, axis=0)
    latent = (numer / denom[..., None]).astype(jnp.bfloat16)
    latent = latent.reshape(tok_local, heads_local, lat_width)
    projected = jnp.einsum("nhd,hde->nhe", latent, w_uv, preferred_element_type=jnp.float32)
    head_values = projected.astype(jnp.bfloat16).reshape(tok_local, -1)
    token_values = gather_all(head_values, "req", n_req).reshape(n_req * tok_local, -1)
    partial_attn = jnp.dot(token_values, w_o, preferred_element_type=jnp.float32)
    partial_attn = partial_attn.astype(jnp.bfloat16).reshape((n_ctx,) + residual.shape)
    pieces = lax.all_to_all(partial_attn, "ctx", split_axis=0, concat_axis=0, tiled=True)
    attention = jnp.sum(pieces.astype(jnp.float32), axis=0)
    residual_mid = (residual.astype(jnp.float32) + attention).astype(jnp.bfloat16)
    mids = gather_all(residual_mid, ("ctx", "req"), n_ctx * n_req)
    mids = mids.reshape((n_ctx, n_req) + residual.shape)
    all_tokens = jnp.swapaxes(mids, 1, 2).reshape(n_ctx * residual.shape[0], -1)
    model_width = all_tokens.shape[1]
    widened = all_tokens.astype(jnp.float32)
    scale_rows = lax.rsqrt(jnp.mean(widened * widened, axis=-1, keepdims=True) + NORM_EPS)
    normed = (widened * scale_rows * norm_gain.astype(jnp.float32)).astype(jnp.bfloat16)
    local_experts = w_gate.shape[0]
    expert_ids = lax.axis_index("req") * local_experts + jnp.arange(local_experts, dtype=jnp.int32)
    matches = routes[:, :, None] == expert_ids[None, None, :]
    coefs = jnp.sum(
        jnp.where(matches, route_weight[:, :, None], jnp.zeros_like(route_weight)[:, :, None]),
        axis=1,
    )
    gate_vals = jnp.einsum("td,efd->etf", normed, w_gate, preferred_element_type=jnp.float32)
    up_vals = jnp.einsum("td,efd->etf", normed, w_up, preferred_element_type=jnp.float32)
    hidden = (jax.nn.silu(gate_vals) * up_vals * coefs.T[:, :, None]).astype(jnp.bfloat16)
    partial_sum = jnp.einsum("etf,efd->td", hidden, w_down, preferred_element_type=jnp.float32)
    rows_out = all_tokens.shape[0] // n_req
    slice_width = model_width // n_ctx
    blocks = partial_sum.astype(jnp.bfloat16).reshape(n_req, rows_out, n_ctx, slice_width)
    blocks = jnp.swapaxes(blocks, 1, 2).reshape(n_req * n_ctx, rows_out, slice_width)
    landed = lax.all_to_all(blocks, ("req", "ctx"), split_axis=0, concat_axis=0, tiled=True)
    moe_out = jnp.sum(landed.astype(jnp.float32), axis=0)
    kept = lax.dynamic_slice(
        all_tokens,
        (lax.axis_index("req") * rows_out, lax.axis_index("ctx") * slice_width),
        (rows_out, slice_width),
    )
    return (kept.astype(jnp.float32) + moe_out).astype(jnp.bfloat16)


def solution(mesh):
    in_specs = (
        P("ctx", "req"),
        P("req", "ctx", None),
        P("req", "ctx", None),
        P("req"),
        P("ctx", None, None),
        P("ctx", "req"),
        P(),
        P(),
        P(),
        P("req", "ctx", None),
        P("req", "ctx", None),
        P("req", "ctx", None),
    )
    out_specs = P("req", "ctx")
    return jax.shard_map(local, mesh=mesh, in_specs=in_specs, out_specs=out_specs, check_vma=False)
```

```python
import functools

import jax
import jax.numpy as jnp
from jax import lax
from jax.experimental import pallas as pl
from jax.experimental.pallas import tpu as pltpu
from jax.sharding import PartitionSpec as P

SOFTMAX_SCALE = 192.0 ** (-0.5)
NEG_FILL = -1e30
NORM_EPS = 1e-06
CORES = 2
LANES = 128
MIB = 1 << 20
NT = (((1,), (1,)), ((), ()))
VMEM = pl.BlockSpec(memory_space=pltpu.VMEM)
SMEM = pl.BlockSpec(memory_space=pltpu.SMEM)
ANY = pl.BlockSpec(memory_space=pl.ANY)


def gather_all(x, axes, size):
    spread = jnp.broadcast_to(x[None], (size,) + x.shape)
    return lax.all_to_all(spread, axes, split_axis=0, concat_axis=0, tiled=True)


def chip_shift(x, step, n_ctx):
    chips = n_ctx // CORES
    pairs = [
        (chip * CORES + core, (chip + step) % chips * CORES + core)
        for chip in range(chips)
        for core in range(CORES)
    ]
    return lax.ppermute(x, "ctx", pairs)


def core_swap(x, n_ctx):
    return lax.ppermute(x, "ctx", [(i, i ^ 1) for i in range(n_ctx)])


def axis_shift(x, axis, step, size):
    return lax.ppermute(x, axis, [(i, (i + step) % size) for i in range(size)])


def stack_rows(blocks):
    if len(blocks) == 1:
        return blocks[0]
    if all(b.shape[0] % 16 == 0 for b in blocks):
        return jnp.concatenate(blocks, axis=0)
    return jnp.concatenate([b.astype(jnp.float32) for b in blocks], axis=0).astype(blocks[0].dtype)


def attend_kernel(n_blocks, q_tokens, width, place, lengths, *refs):
    queries, caches, outs = refs[:n_blocks], refs[n_blocks : n_blocks + 2], refs[n_blocks + 2 :]
    req_local, rows, _ = queries[0].shape
    ctx_local = caches[0].shape[1]
    total_rows = n_blocks * rows
    heads_local = rows // q_tokens
    row = lax.broadcasted_iota(jnp.int32, (total_rows, ctx_local), 0)
    column = lax.broadcasted_iota(jnp.int32, (total_rows, ctx_local), 1)
    token = (row // heads_local) % q_tokens
    lane = lax.broadcasted_iota(jnp.int32, (total_rows, LANES), 1)
    for r in range(req_local):
        grouped = stack_rows([q[r] for q in queries])
        limit = lengths[r] - q_tokens + token
        masked = []
        for half, cache in enumerate(caches):
            score = lax.dot_general(grouped, cache[r], NT, preferred_element_type=jnp.float32)
            visible = column + place[half] <= limit
            masked.append(jnp.where(visible, score * SOFTMAX_SCALE, -jnp.inf))
        peak = jnp.maximum(
            jnp.max(masked[0], axis=-1, keepdims=True), jnp.max(masked[1], axis=-1, keepdims=True)
        )
        peak = jnp.where(peak > -jnp.inf, peak, 0.0)
        total = jnp.zeros((total_rows, 1), jnp.float32)
        mixed = jnp.zeros((total_rows, width), jnp.float32)
        for scores, cache in zip(masked, caches):
            raised = jnp.exp(scores - peak)
            total += jnp.sum(raised, axis=-1, keepdims=True)
            mixed += jnp.dot(
                raised.astype(jnp.bfloat16), cache[r, :, :width], preferred_element_type=jnp.float32
            )
        filled = total > 0.0
        safe = jnp.where(filled, total, 1.0)
        mean = jnp.where(filled, mixed / safe, 0.0).astype(jnp.bfloat16)
        log = jnp.where(filled, peak + jnp.log(safe), NEG_FILL)
        high = log.astype(jnp.bfloat16).astype(jnp.float32)
        tail = jnp.where(lane == 0, high, jnp.where(lane == 1, log - high, 0.0))
        tail = tail.astype(jnp.bfloat16)
        for s, out in enumerate(outs):
            out[r, :, :width] = mean[s * rows : (s + 1) * rows]
            out[r, :, width:] = tail[s * rows : (s + 1) * rows]


def attend(blocks, caches, lengths, place, width, q_tokens):
    req_local, rows, lat = blocks[0].shape
    n = len(blocks)
    ctx_local = caches[0].shape[1]
    flops = 2 * req_local * n * rows * 2 * ctx_local * (lat + width)
    shape = jax.ShapeDtypeStruct((req_local, rows, width + LANES), jnp.bfloat16)
    return pl.pallas_call(
        functools.partial(attend_kernel, n, q_tokens, width),
        out_shape=[shape] * n,
        in_specs=[SMEM, SMEM] + [VMEM] * (n + 2),
        out_specs=[VMEM] * n,
        compiler_params=pltpu.CompilerParams(vmem_limit_bytes=16 * MIB),
        cost_estimate=pl.CostEstimate(
            flops=flops,
            bytes_accessed=4 * req_local * ctx_local * lat,
            transcendentals=2 * req_local * n * rows * ctx_local,
        ),
        name="attend",
    )(place, lengths, *blocks, *caches)


def out_proj_kernel(n_blocks, place, *refs):
    blocks, w_o, out = refs[:n_blocks], refs[n_blocks], refs[n_blocks + 1]
    per = blocks[0].shape[0]
    tokens = n_blocks * per
    stacked = stack_rows([b[...] for b in blocks])
    to = lax.broadcasted_iota(jnp.int32, (tokens, tokens), 0)
    at = lax.broadcasted_iota(jnp.int32, (tokens, tokens), 1)
    origin = place[0] - at // per
    origin = jnp.where(origin < 0, origin + n_blocks, origin)
    picked = jnp.where(to == origin * per + at % per, 1.0, 0.0).astype(jnp.bfloat16)
    ordered = jnp.dot(picked, stacked, preferred_element_type=jnp.float32).astype(jnp.bfloat16)
    out[...] = jnp.dot(ordered, w_o[...], preferred_element_type=jnp.float32).astype(out.dtype)


def out_proj(blocks, w_o, place):
    n = len(blocks)
    tokens = n * blocks[0].shape[0]
    w_o = pltpu.with_memory_space_constraint(w_o, pltpu.VMEM)
    return pl.pallas_call(
        functools.partial(out_proj_kernel, n),
        out_shape=jax.ShapeDtypeStruct((tokens, w_o.shape[1]), jnp.bfloat16),
        in_specs=[SMEM] + [VMEM] * (n + 1),
        out_specs=VMEM,
        compiler_params=pltpu.CompilerParams(vmem_limit_bytes=16 * MIB),
        cost_estimate=pl.CostEstimate(
            flops=2 * tokens * w_o.size, bytes_accessed=2 * w_o.size, transcendentals=0
        ),
        name="out_proj",
    )(place, *blocks, w_o)


def experts_kernel(
    split, mids, gain, coefs, gate_hbm, up_hbm, down_hbm, out, rows, hidden, gate, up, down, sems
):
    n_exp, units, model = gate.shape
    tokens = rows.shape[0]
    n_slices, slice_width = split
    fetches = []
    for e in range(n_exp):
        fetches.append(pltpu.make_async_copy(gate_hbm.at[e], gate.at[e], sems.at[0, e]))
        fetches.append(pltpu.make_async_copy(up_hbm.at[e], up.at[e], sems.at[1, e]))
    n_chunks = down.shape[0]
    chunk = down.shape[3]
    for j in range(n_chunks):
        fetches.append(
            pltpu.make_async_copy(
                down_hbm.at[:, :, pl.ds(j * chunk, chunk)], down.at[j], sems.at[2, j]
            )
        )
    for fetch in fetches:
        fetch.start()
    if len(mids.shape) == 4:
        n_ctx, n_req, per, width = mids.shape
        for c in range(n_ctx):
            for q in range(n_req):
                rows[c * per : (c + 1) * per, q * width : (q + 1) * width] = mids[c, q].astype(
                    jnp.float32
                )
    else:
        rows[...] = mids[...].astype(jnp.float32)
    widened = rows[...]
    scale = lax.rsqrt(jnp.mean(widened * widened, axis=-1, keepdims=True) + NORM_EPS)
    normed = (widened * scale * gain[...].astype(jnp.float32)).astype(jnp.bfloat16)
    for e in range(n_exp):
        fetches[2 * e].wait()
        gate_vals = lax.dot_general(gate[e], normed, NT, preferred_element_type=jnp.float32)
        fetches[2 * e + 1].wait()
        up_vals = lax.dot_general(up[e], normed, NT, preferred_element_type=jnp.float32)
        active = jax.nn.silu(gate_vals) * up_vals * coefs[e : e + 1, :]
        hidden[:, e * units : (e + 1) * units] = active.T.astype(jnp.bfloat16)
    held = hidden[...]
    for j in range(n_chunks):
        fetches[2 * n_exp + j].wait()
        weights = down[j].reshape(n_exp * units, chunk)
        total = jnp.dot(held, weights, preferred_element_type=jnp.float32).astype(out.dtype)
        if len(out.shape) == 4:
            per = out.shape[2]
            for q in range(out.shape[0]):
                out[q, j] = total[q * per : (q + 1) * per]
        else:
            out[:, j * chunk : (j + 1) * chunk] = total


def experts(mids, gain, coefs, w_gate, w_up, w_down, n_req, n_ctx):
    n_exp, units, model = w_gate.shape
    tokens = coefs.shape[1]
    slice_width = model // n_ctx
    aligned = slice_width % LANES == 0
    chunk = slice_width if aligned else model // 8
    if mids.shape[-1] % LANES:
        mids = jnp.swapaxes(mids, 1, 2).reshape(tokens, model)
    shape = (n_req, n_ctx, tokens // n_req, slice_width) if aligned else (tokens, model)
    return pl.pallas_call(
        functools.partial(experts_kernel, (n_ctx, slice_width)),
        out_shape=jax.ShapeDtypeStruct(shape, jnp.bfloat16),
        in_specs=[VMEM] * 3 + [ANY] * 3,
        out_specs=VMEM,
        scratch_shapes=[
            pltpu.VMEM((tokens, model), jnp.float32),
            pltpu.VMEM((tokens, n_exp * units), jnp.bfloat16),
            pltpu.VMEM((n_exp, units, model), jnp.bfloat16),
            pltpu.VMEM((n_exp, units, model), jnp.bfloat16),
            pltpu.VMEM((model // chunk, n_exp, units, chunk), jnp.bfloat16),
            pltpu.SemaphoreType.DMA((3, max(n_exp, model // chunk))),
        ],
        compiler_params=pltpu.CompilerParams(vmem_limit_bytes=54 * MIB),
        cost_estimate=pl.CostEstimate(
            flops=6 * tokens * w_gate.size,
            bytes_accessed=6 * w_gate.size,
            transcendentals=n_exp * units * tokens,
        ),
        name="experts",
    )(mids, gain, coefs, w_gate, w_up, w_down)


def local(
    residual,
    query,
    latent_cache,
    lengths,
    w_uv,
    w_o,
    norm_gain,
    routes,
    route_weight,
    w_gate,
    w_up,
    w_down,
):
    n_ctx = lax.axis_size("ctx")
    n_req = lax.axis_size("req")
    at_ctx = lax.axis_index("ctx").astype(jnp.int32)
    at_req = lax.axis_index("req").astype(jnp.int32)
    n_chips = n_ctx // CORES
    req_local, ctx_local, _ = latent_cache.shape
    heads_local, lat_width, _ = w_uv.shape
    tok_local = query.shape[0]
    q_tokens = tok_local // req_local

    other_cache = core_swap(latent_cache, n_ctx)
    query = query.reshape(req_local, q_tokens * heads_local, query.shape[2])
    blocks = [query] + [chip_shift(query, s, n_ctx) for s in range(1, n_chips)]
    place = jnp.stack([at_ctx * ctx_local, (at_ctx ^ 1) * ctx_local])
    outs = attend(blocks, (latent_cache, other_cache), lengths, place, lat_width, q_tokens)
    outs = [outs[0]] + [chip_shift(outs[s], -s, n_ctx) for s in range(1, n_chips)]

    logs_in = [
        o[..., lat_width].astype(jnp.float32) + o[..., lat_width + 1].astype(jnp.float32)
        for o in outs
    ]
    top_log = functools.reduce(jnp.maximum, logs_in)
    factors = [jnp.exp(log - top_log) for log in logs_in]
    numer = sum(f[..., None] * o[..., :lat_width].astype(jnp.float32) for f, o in zip(factors, outs))
    latent = (numer / sum(factors)[..., None]).astype(jnp.bfloat16)
    latent = latent.reshape(tok_local, heads_local, lat_width)
    projected = jnp.einsum("nhd,hde->nhe", latent, w_uv, preferred_element_type=jnp.float32)
    head_values = projected.astype(jnp.bfloat16).reshape(tok_local, -1)
    blocks = [head_values] + [axis_shift(head_values, "req", s, n_req) for s in range(1, n_req)]
    partial_attn = out_proj(blocks, w_o, at_req[None])
    partial_attn = partial_attn.reshape((n_ctx,) + residual.shape)
    pieces = lax.all_to_all(partial_attn, "ctx", split_axis=0, concat_axis=0, tiled=True)
    attention = jnp.sum(pieces.astype(jnp.float32), axis=0)
    residual_mid = (residual.astype(jnp.float32) + attention).astype(jnp.bfloat16)
    mids = gather_all(residual_mid, ("ctx", "req"), n_ctx * n_req)
    mids = mids.reshape((n_ctx, n_req) + residual.shape)

    local_experts = w_gate.shape[0]
    model_width = w_gate.shape[2]
    expert_ids = at_req * local_experts + jnp.arange(local_experts, dtype=jnp.int32)
    matches = routes[None, :, :] == expert_ids[:, None, None]
    coefs = jnp.sum(
        jnp.where(matches, route_weight[None], jnp.zeros_like(route_weight)[None]), axis=-1
    )
    partial_sum = experts(
        mids, norm_gain.reshape(1, -1), coefs, w_gate, w_up, w_down, n_req, n_ctx
    )
    rows_out = coefs.shape[1] // n_req
    slice_width = model_width // n_ctx
    if partial_sum.ndim == 2:
        partial_sum = partial_sum.reshape(n_req, rows_out, n_ctx, slice_width)
        partial_sum = jnp.swapaxes(partial_sum, 1, 2)
    partial_sum = partial_sum.reshape(n_req * n_ctx, rows_out, slice_width)
    landed = lax.all_to_all(partial_sum, ("req", "ctx"), split_axis=0, concat_axis=0, tiled=True)
    moe_out = jnp.sum(landed.astype(jnp.float32), axis=0)
    all_tokens = jnp.swapaxes(mids, 1, 2).reshape(coefs.shape[1], model_width)
    kept = lax.dynamic_slice(
        all_tokens, (at_req * rows_out, at_ctx * slice_width), (rows_out, slice_width)
    )
    return (kept.astype(jnp.float32) + moe_out).astype(jnp.bfloat16)


def solution(mesh):
    in_specs = (
        P("ctx", "req"),
        P("req", "ctx", None),
        P("req", "ctx", None),
        P("req"),
        P("ctx", None, None),
        P("ctx", "req"),
        P(),
        P(),
        P(),
        P("req", "ctx", None),
        P("req", "ctx", None),
        P("req", "ctx", None),
    )
    out_specs = P("req", "ctx")
    return jax.shard_map(local, mesh=mesh, in_specs=in_specs, out_specs=out_specs, check_vma=False)
```

```python
import functools

import jax
import jax.numpy as jnp
from jax import lax
from jax.experimental import pallas as pl
from jax.experimental.pallas import tpu as pltpu
from jax.sharding import PartitionSpec as P

SOFTMAX_SCALE = 192.0 ** (-0.5)
NEG_FILL = -1e30
NORM_EPS = 1e-06
CORES = 2
LANES = 128
MIB = 1 << 20
NT = (((1,), (1,)), ((), ()))
VMEM = pl.BlockSpec(memory_space=pltpu.VMEM)
SMEM = pl.BlockSpec(memory_space=pltpu.SMEM)
ANY = pl.BlockSpec(memory_space=pl.ANY)


def swap(x, axis, step, size):
    return lax.ppermute(x, axis, [(i, i ^ step) for i in range(size)])


def stack_rows(blocks):
    if len(blocks) == 1:
        return blocks[0]
    if all(b.shape[0] % 16 == 0 for b in blocks):
        return jnp.concatenate(blocks, axis=0)
    return jnp.concatenate([b.astype(jnp.float32) for b in blocks], axis=0).astype(blocks[0].dtype)


def attend_kernel(n_blocks, q_tokens, width, place, lengths, *refs):
    queries, caches, outs = refs[:n_blocks], refs[n_blocks : n_blocks + 2], refs[n_blocks + 2 :]
    req_local, rows, _ = queries[0].shape
    ctx_local = caches[0].shape[2]
    total_rows = n_blocks * rows
    heads_local = rows // q_tokens
    row = lax.broadcasted_iota(jnp.int32, (total_rows, ctx_local), 0)
    column = lax.broadcasted_iota(jnp.int32, (total_rows, ctx_local), 1)
    token = (row // heads_local) % q_tokens
    lane = lax.broadcasted_iota(jnp.int32, (total_rows, LANES), 1)
    for r in range(req_local):
        grouped = stack_rows([q[r] for q in queries])
        limit = lengths[r] - q_tokens + token
        masked = []
        for half, cache in enumerate(caches):
            score = jnp.dot(grouped, cache[r], preferred_element_type=jnp.float32)
            visible = column + (place[0] ^ half) * ctx_local <= limit
            masked.append(jnp.where(visible, score * SOFTMAX_SCALE, -jnp.inf))
        peak = jnp.maximum(
            jnp.max(masked[0], axis=-1, keepdims=True), jnp.max(masked[1], axis=-1, keepdims=True)
        )
        peak = jnp.where(peak > -jnp.inf, peak, 0.0)
        total = jnp.zeros((total_rows, 1), jnp.float32)
        mixed = jnp.zeros((total_rows, width), jnp.float32)
        for scores, cache in zip(masked, caches):
            raised = jnp.exp(scores - peak)
            total += jnp.sum(raised, axis=-1, keepdims=True)
            mixed += lax.dot_general(
                raised.astype(jnp.bfloat16),
                cache[r, :width, :],
                NT,
                preferred_element_type=jnp.float32,
            )
        filled = total > 0.0
        safe = jnp.where(filled, total, 1.0)
        mean = jnp.where(filled, mixed / safe, 0.0).astype(jnp.bfloat16)
        log = jnp.where(filled, peak + jnp.log(safe), NEG_FILL)
        high = log.astype(jnp.bfloat16).astype(jnp.float32)
        tail = jnp.where(lane == 0, high, jnp.where(lane == 1, log - high, 0.0))
        tail = tail.astype(jnp.bfloat16)
        for s, out in enumerate(outs):
            out[r, :, :width] = mean[s * rows : (s + 1) * rows]
            out[r, :, width:] = tail[s * rows : (s + 1) * rows]


def attend(blocks, caches, lengths, place, width, q_tokens):
    req_local, rows, lat = blocks[0].shape
    n = len(blocks)
    ctx_local = caches[0].shape[2]
    shape = jax.ShapeDtypeStruct((req_local, rows, width + LANES), jnp.bfloat16)
    return pl.pallas_call(
        functools.partial(attend_kernel, n, q_tokens, width),
        out_shape=[shape] * n,
        in_specs=[SMEM, SMEM] + [VMEM] * (n + 2),
        out_specs=[VMEM] * n,
        compiler_params=pltpu.CompilerParams(vmem_limit_bytes=16 * MIB),
        cost_estimate=pl.CostEstimate(
            flops=4 * req_local * n * rows * ctx_local * (lat + width),
            bytes_accessed=4 * req_local * ctx_local * lat,
            transcendentals=2 * req_local * n * rows * ctx_local,
        ),
        name="attend",
    )(place, lengths, *blocks, *caches)


def one_hot(shape, target):
    at = lax.broadcasted_iota(jnp.int32, shape, 1)
    return jnp.where(at == target(lax.broadcasted_iota(jnp.int32, shape, 0)), 1.0, 0.0).astype(
        jnp.bfloat16
    )


def out_proj_kernel(n_blocks, place, *refs):
    blocks, (w_o, residual, out) = refs[:n_blocks], refs[n_blocks:]
    per = blocks[0].shape[0]
    tokens = n_blocks * per
    stacked = stack_rows([b[...] for b in blocks])
    order = one_hot((tokens, tokens), lambda row: (row // per ^ place[1]) * per + row % per)
    ordered = jnp.dot(order, stacked, preferred_element_type=jnp.float32).astype(jnp.bfloat16)
    own = residual.shape[0]
    owner = one_hot((tokens, own), lambda row: row - place[0] * own)
    total = jnp.dot(ordered, w_o[...], preferred_element_type=jnp.float32)
    total += jnp.dot(owner, residual[...], preferred_element_type=jnp.float32)
    out[...] = total.astype(out.dtype)


def out_proj(blocks, w_o, residual, place):
    n = len(blocks)
    tokens = n * blocks[0].shape[0]
    w_o = pltpu.with_memory_space_constraint(w_o, pltpu.VMEM)
    return pl.pallas_call(
        functools.partial(out_proj_kernel, n),
        out_shape=jax.ShapeDtypeStruct((tokens, w_o.shape[1]), jnp.bfloat16),
        in_specs=[SMEM] + [VMEM] * (n + 2),
        out_specs=VMEM,
        compiler_params=pltpu.CompilerParams(vmem_limit_bytes=16 * MIB),
        cost_estimate=pl.CostEstimate(
            flops=2 * tokens * w_o.size, bytes_accessed=2 * w_o.size, transcendentals=0
        ),
        name="out_proj",
    )(place, *blocks, w_o, residual)


def experts_kernel(n_blocks, place, *refs):
    blocks = refs[:n_blocks]
    gain, routes, weights, gate_hbm, up_hbm, down_hbm = refs[n_blocks : n_blocks + 6]
    out, kept, rows, hidden, gate, up, down, sems = refs[n_blocks + 6 :]
    n_exp, units, model = gate.shape
    tokens = rows.shape[0]
    fetches = []
    for e in range(n_exp):
        fetches.append(pltpu.make_async_copy(gate_hbm.at[e], gate.at[e], sems.at[0, e]))
        fetches.append(pltpu.make_async_copy(up_hbm.at[e], up.at[e], sems.at[1, e]))
    n_chunks = down.shape[0]
    chunk = down.shape[3]
    for j in range(n_chunks):
        fetches.append(
            pltpu.make_async_copy(
                down_hbm.at[:, :, pl.ds(j * chunk, chunk)], down.at[j], sems.at[2, j]
            )
        )
    for fetch in fetches:
        fetch.start()
    width = blocks[0].shape[1]
    for s, block in enumerate(blocks):
        if n_blocks == 1:
            rows[...] = block[...]
        else:
            offset = pl.multiple_of((place[1] ^ s) * width, LANES)
            rows[:, pl.ds(offset, width)] = block[...]
    widened = rows[...].astype(jnp.float32)
    scale = lax.rsqrt(jnp.mean(widened * widened, axis=-1, keepdims=True) + NORM_EPS)
    normed = (widened * scale * gain[...].astype(jnp.float32)).astype(jnp.bfloat16)
    eye = lax.broadcasted_iota(jnp.int32, (tokens, tokens), 0) == lax.broadcasted_iota(
        jnp.int32, (tokens, tokens), 1
    )
    for e in range(n_exp):
        named = jnp.where(routes[...] == place[1] * n_exp + e, weights[...], 0.0)
        coef = jnp.sum(named, axis=0, keepdims=True)
        coef = jnp.sum(jnp.where(eye, coef, 0.0), axis=1, keepdims=True)
        fetches[2 * e].wait()
        gate_vals = lax.dot_general(normed, gate[e], NT, preferred_element_type=jnp.float32)
        fetches[2 * e + 1].wait()
        up_vals = lax.dot_general(normed, up[e], NT, preferred_element_type=jnp.float32)
        active = jax.nn.silu(gate_vals) * up_vals * coef
        hidden[:, e * units : (e + 1) * units] = active.astype(jnp.bfloat16)
    if len(out.shape) == 4:
        per = out.shape[2]
        columns = pl.ds(pl.multiple_of(place[0] * chunk, LANES), chunk)
        own = one_hot((per, tokens), lambda row: row + place[1] * per)
        kept[...] = jnp.dot(own, rows[:, columns], preferred_element_type=jnp.float32)
    else:
        kept[...] = rows[...].astype(jnp.float32)
    held = hidden[...]
    for j in range(n_chunks):
        fetches[2 * n_exp + j].wait()
        total = jnp.dot(
            held, down[j].reshape(n_exp * units, chunk), preferred_element_type=jnp.float32
        ).astype(out.dtype)
        if len(out.shape) == 4:
            for q in range(out.shape[0]):
                out[q, j] = total[q * per : (q + 1) * per]
        else:
            out[:, j * chunk : (j + 1) * chunk] = total


def experts(blocks, gain, routes, route_weight, w_gate, w_up, w_down, place, n_req, n_ctx):
    n_exp, units, model = w_gate.shape
    tokens = blocks[0].shape[0]
    slice_width = model // n_ctx
    aligned = slice_width % LANES == 0
    chunk = slice_width if aligned else model // 8
    shape = (n_req, n_ctx, tokens // n_req, slice_width) if aligned else (tokens, model)
    kept = (tokens // n_req, slice_width) if aligned else (tokens, model)
    return pl.pallas_call(
        functools.partial(experts_kernel, len(blocks)),
        out_shape=[
            jax.ShapeDtypeStruct(shape, jnp.bfloat16),
            jax.ShapeDtypeStruct(kept, jnp.float32),
        ],
        in_specs=[SMEM] + [VMEM] * (len(blocks) + 3) + [ANY] * 3,
        out_specs=[VMEM, VMEM],
        scratch_shapes=[
            pltpu.VMEM((tokens, model), jnp.bfloat16),
            pltpu.VMEM((tokens, n_exp * units), jnp.bfloat16),
            pltpu.VMEM((n_exp, units, model), jnp.bfloat16),
            pltpu.VMEM((n_exp, units, model), jnp.bfloat16),
            pltpu.VMEM((model // chunk, n_exp, units, chunk), jnp.bfloat16),
            pltpu.SemaphoreType.DMA((3, max(n_exp, model // chunk))),
        ],
        compiler_params=pltpu.CompilerParams(vmem_limit_bytes=52 * MIB),
        cost_estimate=pl.CostEstimate(
            flops=6 * tokens * w_gate.size,
            bytes_accessed=6 * w_gate.size,
            transcendentals=n_exp * units * tokens,
        ),
        name="experts",
    )(place, *blocks, gain, routes, route_weight, w_gate, w_up, w_down)


def local(
    residual,
    query,
    latent_cache,
    lengths,
    w_uv,
    w_o,
    norm_gain,
    routes,
    route_weight,
    w_gate,
    w_up,
    w_down,
):
    n_ctx = lax.axis_size("ctx")
    n_req = lax.axis_size("req")
    at_ctx = lax.axis_index("ctx").astype(jnp.int32)
    at_req = lax.axis_index("req").astype(jnp.int32)
    place = jnp.stack([at_ctx, at_req])
    chip_steps = range(CORES, n_ctx, CORES)
    req_steps = range(1, n_req)
    req_local = latent_cache.shape[0]
    heads_local, lat_width, _ = w_uv.shape
    tok_local = query.shape[0]
    q_tokens = tok_local // req_local

    cache = jnp.swapaxes(latent_cache, 1, 2)
    other_cache = swap(cache, "ctx", 1, n_ctx)
    query = query.reshape(req_local, q_tokens * heads_local, query.shape[2])
    blocks = [query] + [swap(query, "ctx", s, n_ctx) for s in chip_steps]
    outs = attend(blocks, (cache, other_cache), lengths, place, lat_width, q_tokens)
    outs = [outs[0]] + [swap(o, "ctx", s, n_ctx) for o, s in zip(outs[1:], chip_steps)]

    logs_in = [
        o[..., lat_width].astype(jnp.float32) + o[..., lat_width + 1].astype(jnp.float32)
        for o in outs
    ]
    top_log = functools.reduce(jnp.maximum, logs_in)
    factors = [jnp.exp(log - top_log) for log in logs_in]
    numer = sum(f[..., None] * o[..., :lat_width].astype(jnp.float32) for f, o in zip(factors, outs))
    latent = (numer / sum(factors)[..., None]).astype(jnp.bfloat16)
    latent = latent.reshape(tok_local, heads_local, lat_width)
    projected = jnp.einsum("nhd,hde->nhe", latent, w_uv, preferred_element_type=jnp.float32)
    head_values = projected.astype(jnp.bfloat16).reshape(tok_local, -1)
    blocks = [head_values] + [swap(head_values, "req", s, n_req) for s in req_steps]
    partial_mid = out_proj(blocks, w_o, residual, place)

    other = swap(partial_mid, "ctx", 1, n_ctx)
    chip_mid = (partial_mid.astype(jnp.float32) + other.astype(jnp.float32)).astype(jnp.bfloat16)
    parts = [chip_mid] + [swap(chip_mid, "ctx", s, n_ctx) for s in chip_steps]
    mid = sum(p.astype(jnp.float32) for p in parts).astype(jnp.bfloat16)
    if mid.shape[1] % LANES == 0:
        blocks = [mid] + [swap(mid, "req", s, n_req) for s in req_steps]
    else:
        blocks = [lax.all_gather(mid, "req", axis=1, tiled=True)]

    partial_sum, kept = experts(
        blocks,
        norm_gain.reshape(1, -1),
        routes.T,
        route_weight.T,
        w_gate,
        w_up,
        w_down,
        place,
        n_req,
        n_ctx,
    )
    tokens = mid.shape[0]
    model_width = w_gate.shape[2]
    rows_out = tokens // n_req
    slice_width = model_width // n_ctx
    if partial_sum.ndim == 2:
        partial_sum = partial_sum.reshape(n_req, rows_out, n_ctx, slice_width)
        partial_sum = jnp.swapaxes(partial_sum, 1, 2)
        kept = lax.dynamic_slice(
            kept, (at_req * rows_out, at_ctx * slice_width), (rows_out, slice_width)
        )
    partial_sum = partial_sum.reshape(n_req * n_ctx, rows_out, slice_width)
    landed = lax.all_to_all(partial_sum, ("req", "ctx"), split_axis=0, concat_axis=0, tiled=True)
    return (kept + jnp.sum(landed.astype(jnp.float32), axis=0)).astype(jnp.bfloat16)


def solution(mesh):
    in_specs = (
        P("ctx", "req"),
        P("req", "ctx", None),
        P("req", "ctx", None),
        P("req"),
        P("ctx", None, None),
        P("ctx", "req"),
        P(),
        P(),
        P(),
        P("req", "ctx", None),
        P("req", "ctx", None),
        P("req", "ctx", None),
    )
    out_specs = P("req", "ctx")
    return jax.shard_map(local, mesh=mesh, in_specs=in_specs, out_specs=out_specs, check_vma=False)
```

```python
import functools

import jax
import jax.numpy as jnp
from jax import lax
from jax.experimental import pallas as pl
from jax.experimental.pallas import tpu as pltpu
from jax.sharding import PartitionSpec as P

SOFTMAX_SCALE = 192.0 ** (-0.5)
NEG_FILL = -1e30
NORM_EPS = 1e-06
CORES = 2
OVERLAP = 800
LANES = 128
MIB = 1 << 20
NT = (((1,), (1,)), ((), ()))
VMEM = pl.BlockSpec(memory_space=pltpu.VMEM)
SMEM = pl.BlockSpec(memory_space=pltpu.SMEM)
HBM = pl.BlockSpec(memory_space=pltpu.HBM)


def swap(x, axis, step, size):
    return lax.ppermute(x, axis, [(i, i ^ step) for i in range(size)])


def stack_rows(blocks):
    if len(blocks) == 1:
        return blocks[0]
    if all(b.shape[0] % 16 == 0 for b in blocks):
        return jnp.concatenate(blocks, axis=0)
    return jnp.concatenate([b.astype(jnp.float32) for b in blocks], axis=0).astype(blocks[0].dtype)


def attend_kernel(n_blocks, q_tokens, width, place, lengths, *refs):
    queries, caches, outs = refs[:n_blocks], refs[n_blocks : n_blocks + 2], refs[n_blocks + 2 :]
    req_local, rows, _ = queries[0].shape
    ctx_local = caches[0].shape[2]
    total_rows = n_blocks * rows
    heads_local = rows // q_tokens
    row = lax.broadcasted_iota(jnp.int32, (total_rows, ctx_local), 0)
    column = lax.broadcasted_iota(jnp.int32, (total_rows, ctx_local), 1)
    token = (row // heads_local) % q_tokens
    lane = lax.broadcasted_iota(jnp.int32, (total_rows, LANES), 1)
    for r in range(req_local):
        grouped = stack_rows([q[r] for q in queries])
        limit = lengths[r] - q_tokens + token
        masked = []
        for half, cache in enumerate(caches):
            score = jnp.dot(grouped, cache[r], preferred_element_type=jnp.float32)
            visible = column + (place[0] ^ half) * ctx_local <= limit
            masked.append(jnp.where(visible, score * SOFTMAX_SCALE, -jnp.inf))
        peak = jnp.maximum(
            jnp.max(masked[0], axis=-1, keepdims=True), jnp.max(masked[1], axis=-1, keepdims=True)
        )
        peak = jnp.where(peak > -jnp.inf, peak, 0.0)
        total = jnp.zeros((total_rows, 1), jnp.float32)
        mixed = jnp.zeros((total_rows, width), jnp.float32)
        for scores, cache in zip(masked, caches):
            raised = jnp.exp(scores - peak)
            total += jnp.sum(raised, axis=-1, keepdims=True)
            mixed += lax.dot_general(
                raised.astype(jnp.bfloat16),
                cache[r, :width, :],
                NT,
                preferred_element_type=jnp.float32,
            )
        filled = total > 0.0
        safe = jnp.where(filled, total, 1.0)
        mean = jnp.where(filled, mixed / safe, 0.0).astype(jnp.bfloat16)
        log = jnp.where(filled, peak + jnp.log(safe), NEG_FILL)
        high = log.astype(jnp.bfloat16).astype(jnp.float32)
        tail = jnp.where(lane == 0, high, jnp.where(lane == 1, log - high, 0.0))
        tail = tail.astype(jnp.bfloat16)
        for s, out in enumerate(outs):
            out[r, :, :width] = mean[s * rows : (s + 1) * rows]
            out[r, :, width:] = tail[s * rows : (s + 1) * rows]


def attend(blocks, caches, lengths, place, width, q_tokens):
    req_local, rows, lat = blocks[0].shape
    n = len(blocks)
    ctx_local = caches[0].shape[2]
    shape = jax.ShapeDtypeStruct((req_local, rows, width + LANES), jnp.bfloat16)
    return pl.pallas_call(
        functools.partial(attend_kernel, n, q_tokens, width),
        out_shape=[shape] * n,
        in_specs=[SMEM, SMEM] + [VMEM] * (n + 2),
        out_specs=[VMEM] * n,
        compiler_params=pltpu.CompilerParams(vmem_limit_bytes=16 * MIB),
        cost_estimate=pl.CostEstimate(
            flops=4 * req_local * n * rows * ctx_local * (lat + width),
            bytes_accessed=4 * req_local * ctx_local * lat,
            transcendentals=2 * req_local * n * rows * ctx_local,
        ),
        name="attend",
    )(place, lengths, *blocks, *caches)


def stage_kernel(*refs):
    n = len(refs) // 2
    sems = refs[-1]
    copies = [
        pltpu.make_async_copy(source, target, sems.at[i])
        for i, (source, target) in enumerate(zip(refs[:n], refs[n : 2 * n]))
    ]
    for copy in copies:
        copy.start()
    for copy in copies:
        copy.wait()


def stage(arrays):
    return pl.pallas_call(
        stage_kernel,
        out_shape=[pltpu.VMEM(x.shape, x.dtype) for x in arrays],
        in_specs=[HBM] * len(arrays),
        out_specs=[VMEM] * len(arrays),
        scratch_shapes=[pltpu.SemaphoreType.DMA((len(arrays),))],
        compiler_params=pltpu.CompilerParams(vmem_limit_bytes=16 * MIB),
        cost_estimate=pl.CostEstimate(
            flops=0, bytes_accessed=sum(x.size * 2 for x in arrays), transcendentals=0
        ),
        name="stage",
    )(*[pltpu.with_memory_space_constraint(x, pltpu.HBM) for x in arrays])


def one_hot(shape, target):
    at = lax.broadcasted_iota(jnp.int32, shape, 1)
    return jnp.where(at == target(lax.broadcasted_iota(jnp.int32, shape, 0)), 1.0, 0.0).astype(
        jnp.bfloat16
    )


def out_proj_kernel(n_blocks, place, *refs):
    blocks, (w_o, residual, out) = refs[:n_blocks], refs[n_blocks:]
    per = blocks[0].shape[0]
    tokens = n_blocks * per
    stacked = stack_rows([b[...] for b in blocks])
    order = one_hot((tokens, tokens), lambda row: (row // per ^ place[1]) * per + row % per)
    ordered = jnp.dot(order, stacked, preferred_element_type=jnp.float32).astype(jnp.bfloat16)
    own = residual.shape[0]
    owner = one_hot((tokens, own), lambda row: row - place[0] * own)
    total = jnp.dot(ordered, w_o[...], preferred_element_type=jnp.float32)
    total += jnp.dot(owner, residual[...], preferred_element_type=jnp.float32)
    out[...] = total.astype(out.dtype)


def out_proj(blocks, w_o, residual, place):
    n = len(blocks)
    tokens = n * blocks[0].shape[0]
    return pl.pallas_call(
        functools.partial(out_proj_kernel, n),
        out_shape=jax.ShapeDtypeStruct((tokens, w_o.shape[1]), jnp.bfloat16),
        in_specs=[SMEM] + [VMEM] * (n + 2),
        out_specs=VMEM,
        compiler_params=pltpu.CompilerParams(vmem_limit_bytes=4 * MIB),
        cost_estimate=pl.CostEstimate(
            flops=OVERLAP * tokens * w_o.size, bytes_accessed=2 * w_o.size, transcendentals=0
        ),
        name="out_proj",
    )(place, *blocks, w_o, residual)


def experts_kernel(n_blocks, place, *refs):
    blocks = refs[:n_blocks]
    gain, routes, weights, gate, up, down_hbm = refs[n_blocks : n_blocks + 6]
    out, kept, rows, hidden, down, sems = refs[n_blocks + 6 :]
    n_exp, units, model = gate.shape
    tokens = rows.shape[0]
    n_chunks, _, _, chunk = down.shape
    fetches = [
        pltpu.make_async_copy(down_hbm.at[:, :, pl.ds(j * chunk, chunk)], down.at[j], sems.at[j])
        for j in range(n_chunks)
    ]
    for fetch in fetches:
        fetch.start()
    width = blocks[0].shape[1]
    for s, block in enumerate(blocks):
        if n_blocks == 1:
            rows[...] = block[...]
        else:
            offset = pl.multiple_of((place[1] ^ s) * width, LANES)
            rows[:, pl.ds(offset, width)] = block[...]
    widened = rows[...].astype(jnp.float32)
    scale = lax.rsqrt(jnp.mean(widened * widened, axis=-1, keepdims=True) + NORM_EPS)
    normed = (widened * scale * gain[...].astype(jnp.float32)).astype(jnp.bfloat16)
    eye = lax.broadcasted_iota(jnp.int32, (tokens, tokens), 0) == lax.broadcasted_iota(
        jnp.int32, (tokens, tokens), 1
    )
    for e in range(n_exp):
        named = jnp.where(routes[...] == place[1] * n_exp + e, weights[...], 0.0)
        coef = jnp.sum(named, axis=0, keepdims=True)
        coef = jnp.sum(jnp.where(eye, coef, 0.0), axis=1, keepdims=True)
        gate_vals = lax.dot_general(normed, gate[e], NT, preferred_element_type=jnp.float32)
        up_vals = lax.dot_general(normed, up[e], NT, preferred_element_type=jnp.float32)
        active = jax.nn.silu(gate_vals) * up_vals * coef
        hidden[:, e * units : (e + 1) * units] = active.astype(jnp.bfloat16)
    if len(out.shape) == 4:
        per = out.shape[2]
        columns = pl.ds(pl.multiple_of(place[0] * chunk, LANES), chunk)
        own = one_hot((per, tokens), lambda row: row + place[1] * per)
        kept[...] = jnp.dot(own, rows[:, columns], preferred_element_type=jnp.float32)
    else:
        kept[...] = rows[...].astype(jnp.float32)
    held = hidden[...]
    for j in range(n_chunks):
        fetches[j].wait()
        part = down[j].reshape(n_exp * units, chunk)
        total = jnp.dot(held, part, preferred_element_type=jnp.float32).astype(out.dtype)
        if len(out.shape) == 4:
            for q in range(out.shape[0]):
                out[q, j] = total[q * per : (q + 1) * per]
        else:
            out[:, j * chunk : (j + 1) * chunk] = total


def experts(blocks, gain, routes, route_weight, w_gate, w_up, w_down, place, n_req, n_ctx):
    n_exp, units, model = w_gate.shape
    tokens = blocks[0].shape[0]
    slice_width = model // n_ctx
    aligned = slice_width % LANES == 0
    chunk = slice_width if aligned else model // 8
    w_gate, w_up = [pltpu.with_memory_space_constraint(w, pltpu.VMEM) for w in (w_gate, w_up)]
    w_down = pltpu.with_memory_space_constraint(w_down, pltpu.HBM)
    shape = (n_req, n_ctx, tokens // n_req, slice_width) if aligned else (tokens, model)
    kept = (tokens // n_req, slice_width) if aligned else (tokens, model)
    return pl.pallas_call(
        functools.partial(experts_kernel, len(blocks)),
        out_shape=[
            jax.ShapeDtypeStruct(shape, jnp.bfloat16),
            jax.ShapeDtypeStruct(kept, jnp.float32),
        ],
        in_specs=[SMEM] + [VMEM] * (len(blocks) + 5) + [HBM],
        out_specs=[VMEM, VMEM],
        scratch_shapes=[
            pltpu.VMEM((tokens, model), jnp.bfloat16),
            pltpu.VMEM((tokens, n_exp * units), jnp.bfloat16),
            pltpu.VMEM((model // chunk, n_exp, units, chunk), jnp.bfloat16),
            pltpu.SemaphoreType.DMA((model // chunk,)),
        ],
        compiler_params=pltpu.CompilerParams(vmem_limit_bytes=20 * MIB),
        cost_estimate=pl.CostEstimate(
            flops=6 * tokens * w_gate.size,
            bytes_accessed=6 * w_gate.size,
            transcendentals=n_exp * units * tokens,
        ),
        name="experts",
    )(place, *blocks, gain, routes, route_weight, w_gate, w_up, w_down)


def local(
    residual,
    query,
    latent_cache,
    lengths,
    w_uv,
    w_o,
    norm_gain,
    routes,
    route_weight,
    w_gate,
    w_up,
    w_down,
):
    n_ctx = lax.axis_size("ctx")
    n_req = lax.axis_size("req")
    at_ctx = lax.axis_index("ctx").astype(jnp.int32)
    at_req = lax.axis_index("req").astype(jnp.int32)
    place = jnp.stack([at_ctx, at_req])
    chip_steps = range(CORES, n_ctx, CORES)
    req_steps = range(1, n_req)
    req_local = latent_cache.shape[0]
    heads_local, lat_width, _ = w_uv.shape
    tok_local = query.shape[0]
    q_tokens = tok_local // req_local

    cache = jnp.swapaxes(latent_cache, 1, 2)
    other_cache = swap(cache, "ctx", 1, n_ctx)
    query = query.reshape(req_local, q_tokens * heads_local, query.shape[2])
    received = [swap(query, "ctx", s, n_ctx) for s in chip_steps]
    cache, query, w_o = stage([cache, query, w_o])
    blocks = [query] + received
    outs = attend(blocks, (cache, other_cache), lengths, place, lat_width, q_tokens)
    outs = [outs[0]] + [swap(o, "ctx", s, n_ctx) for o, s in zip(outs[1:], chip_steps)]

    logs_in = [
        o[..., lat_width].astype(jnp.float32) + o[..., lat_width + 1].astype(jnp.float32)
        for o in outs
    ]
    top_log = functools.reduce(jnp.maximum, logs_in)
    factors = [jnp.exp(log - top_log) for log in logs_in]
    numer = sum(f[..., None] * o[..., :lat_width].astype(jnp.float32) for f, o in zip(factors, outs))
    latent = (numer / sum(factors)[..., None]).astype(jnp.bfloat16)
    latent = latent.reshape(tok_local, heads_local, lat_width)
    projected = jnp.einsum("nhd,hde->nhe", latent, w_uv, preferred_element_type=jnp.float32)
    head_values = projected.astype(jnp.bfloat16).reshape(tok_local, -1)
    blocks = [head_values] + [swap(head_values, "req", s, n_req) for s in req_steps]
    partial_mid = out_proj(blocks, w_o, residual, place)

    other = swap(partial_mid, "ctx", 1, n_ctx)
    chip_mid = (partial_mid.astype(jnp.float32) + other.astype(jnp.float32)).astype(jnp.bfloat16)
    parts = [chip_mid] + [swap(chip_mid, "ctx", s, n_ctx) for s in chip_steps]
    mid = sum(p.astype(jnp.float32) for p in parts).astype(jnp.bfloat16)
    if mid.shape[1] % LANES == 0:
        blocks = [mid] + [swap(mid, "req", s, n_req) for s in req_steps]
    else:
        blocks = [lax.all_gather(mid, "req", axis=1, tiled=True)]

    partial_sum, kept = experts(
        blocks,
        norm_gain.reshape(1, -1),
        routes.T,
        route_weight.T,
        w_gate,
        w_up,
        w_down,
        place,
        n_req,
        n_ctx,
    )
    tokens = mid.shape[0]
    model_width = w_gate.shape[2]
    rows_out = tokens // n_req
    slice_width = model_width // n_ctx
    if partial_sum.ndim == 2:
        partial_sum = partial_sum.reshape(n_req, rows_out, n_ctx, slice_width)
        partial_sum = jnp.swapaxes(partial_sum, 1, 2)
        kept = lax.dynamic_slice(
            kept, (at_req * rows_out, at_ctx * slice_width), (rows_out, slice_width)
        )
    partial_sum = partial_sum.reshape(n_req * n_ctx, rows_out, slice_width)
    landed = lax.all_to_all(partial_sum, ("req", "ctx"), split_axis=0, concat_axis=0, tiled=True)
    return (kept + jnp.sum(landed.astype(jnp.float32), axis=0)).astype(jnp.bfloat16)


def solution(mesh):
    in_specs = (
        P("ctx", "req"),
        P("req", "ctx", None),
        P("req", "ctx", None),
        P("req"),
        P("ctx", None, None),
        P("ctx", "req"),
        P(),
        P(),
        P(),
        P("req", "ctx", None),
        P("req", "ctx", None),
        P("req", "ctx", None),
    )
    out_specs = P("req", "ctx")
    return jax.shard_map(local, mesh=mesh, in_specs=in_specs, out_specs=out_specs, check_vma=False)
```

```python
import functools

import jax
import jax.numpy as jnp
from jax import lax
from jax.experimental import pallas as pl
from jax.experimental.pallas import tpu as pltpu
from jax.sharding import PartitionSpec as P

SOFTMAX_SCALE = 192.0 ** (-0.5)
NEG_FILL = -1e30
NORM_EPS = 1e-06
CORES = 2
OVERLAP = 800
LANES = 128
MIB = 1 << 20
NT = (((1,), (1,)), ((), ()))
VMEM = pl.BlockSpec(memory_space=pltpu.VMEM)
SMEM = pl.BlockSpec(memory_space=pltpu.SMEM)
HBM = pl.BlockSpec(memory_space=pltpu.HBM)


def swap(x, axis, step, size):
    return lax.ppermute(x, axis, [(i, i ^ step) for i in range(size)])


def stack_rows(blocks):
    if len(blocks) == 1:
        return blocks[0]
    if all(b.shape[0] % 16 == 0 for b in blocks):
        return jnp.concatenate(blocks, axis=0)
    return jnp.concatenate([b.astype(jnp.float32) for b in blocks], axis=0).astype(blocks[0].dtype)


def attend_kernel(n_blocks, q_tokens, width, place, lengths, *refs):
    queries, caches, outs = refs[:n_blocks], refs[n_blocks : n_blocks + 2], refs[n_blocks + 2 :]
    req_local, rows, _ = queries[0].shape
    ctx_local = caches[0].shape[2]
    total_rows = n_blocks * rows
    heads_local = rows // q_tokens
    row = lax.broadcasted_iota(jnp.int32, (total_rows, ctx_local), 0)
    column = lax.broadcasted_iota(jnp.int32, (total_rows, ctx_local), 1)
    token = (row // heads_local) % q_tokens
    lane = lax.broadcasted_iota(jnp.int32, (total_rows, LANES), 1)
    for r in range(req_local):
        grouped = stack_rows([q[r] for q in queries])
        limit = lengths[r] - q_tokens + token
        masked = []
        for half, cache in enumerate(caches):
            score = jnp.dot(grouped, cache[r], preferred_element_type=jnp.float32)
            visible = column + (place[0] ^ half) * ctx_local <= limit
            masked.append(jnp.where(visible, score * SOFTMAX_SCALE, -jnp.inf))
        peak = jnp.maximum(
            jnp.max(masked[0], axis=-1, keepdims=True), jnp.max(masked[1], axis=-1, keepdims=True)
        )
        peak = jnp.where(peak > -jnp.inf, peak, 0.0)
        total = jnp.zeros((total_rows, 1), jnp.float32)
        mixed = jnp.zeros((total_rows, width), jnp.float32)
        for scores, cache in zip(masked, caches):
            raised = jnp.exp(scores - peak)
            total += jnp.sum(raised, axis=-1, keepdims=True)
            mixed += lax.dot_general(
                raised.astype(jnp.bfloat16),
                cache[r, :width, :],
                NT,
                preferred_element_type=jnp.float32,
            )
        filled = total > 0.0
        safe = jnp.where(filled, total, 1.0)
        mean = jnp.where(filled, mixed / safe, 0.0).astype(jnp.bfloat16)
        log = jnp.where(filled, peak + jnp.log(safe), NEG_FILL)
        high = log.astype(jnp.bfloat16).astype(jnp.float32)
        tail = jnp.where(lane == 0, high, jnp.where(lane == 1, log - high, 0.0))
        tail = tail.astype(jnp.bfloat16)
        for s, out in enumerate(outs):
            out[r, :, :width] = mean[s * rows : (s + 1) * rows]
            out[r, :, width:] = tail[s * rows : (s + 1) * rows]


def attend(blocks, caches, lengths, place, width, q_tokens):
    req_local, rows, lat = blocks[0].shape
    n = len(blocks)
    ctx_local = caches[0].shape[2]
    shape = jax.ShapeDtypeStruct((req_local, rows, width + LANES), jnp.bfloat16)
    return pl.pallas_call(
        functools.partial(attend_kernel, n, q_tokens, width),
        out_shape=[shape] * n,
        in_specs=[SMEM, SMEM] + [VMEM] * (n + 2),
        out_specs=[VMEM] * n,
        compiler_params=pltpu.CompilerParams(vmem_limit_bytes=16 * MIB),
        cost_estimate=pl.CostEstimate(
            flops=4 * req_local * n * rows * ctx_local * (lat + width),
            bytes_accessed=4 * req_local * ctx_local * lat,
            transcendentals=2 * req_local * n * rows * ctx_local,
        ),
        name="attend",
    )(place, lengths, *blocks, *caches)


def stage_kernel(place, *refs):
    n = len(refs) // 2
    sems = refs[-1]
    copies = [
        pltpu.make_async_copy(source, target, sems.at[i])
        for i, (source, target) in enumerate(zip(refs[:n], refs[n : 2 * n]))
    ]
    for copy in copies:
        copy.start()
    for copy in copies:
        copy.wait()


def stage(place, arrays):
    return pl.pallas_call(
        stage_kernel,
        out_shape=[pltpu.VMEM(x.shape, x.dtype) for x in arrays],
        in_specs=[SMEM] + [HBM] * len(arrays),
        out_specs=[VMEM] * len(arrays),
        scratch_shapes=[pltpu.SemaphoreType.DMA((len(arrays),))],
        compiler_params=pltpu.CompilerParams(vmem_limit_bytes=16 * MIB),
        cost_estimate=pl.CostEstimate(
            flops=0, bytes_accessed=sum(x.size * 2 for x in arrays), transcendentals=0
        ),
        name="stage",
    )(place, *[pltpu.with_memory_space_constraint(x, pltpu.HBM) for x in arrays])


def one_hot(shape, target):
    at = lax.broadcasted_iota(jnp.int32, shape, 1)
    return jnp.where(at == target(lax.broadcasted_iota(jnp.int32, shape, 0)), 1.0, 0.0).astype(
        jnp.bfloat16
    )


def out_proj_kernel(n_blocks, place, *refs):
    blocks, (w_o, residual, out) = refs[:n_blocks], refs[n_blocks:]
    per = blocks[0].shape[0]
    tokens = n_blocks * per
    stacked = stack_rows([b[...] for b in blocks])
    order = one_hot((tokens, tokens), lambda row: (row // per ^ place[1]) * per + row % per)
    ordered = jnp.dot(order, stacked, preferred_element_type=jnp.float32).astype(jnp.bfloat16)
    own = residual.shape[0]
    owner = one_hot((tokens, own), lambda row: row - place[0] * own)
    total = jnp.dot(ordered, w_o[...], preferred_element_type=jnp.float32)
    total += jnp.dot(owner, residual[...], preferred_element_type=jnp.float32)
    out[...] = total.astype(out.dtype)


def out_proj(blocks, w_o, residual, place):
    n = len(blocks)
    tokens = n * blocks[0].shape[0]
    return pl.pallas_call(
        functools.partial(out_proj_kernel, n),
        out_shape=jax.ShapeDtypeStruct((tokens, w_o.shape[1]), jnp.bfloat16),
        in_specs=[SMEM] + [VMEM] * (n + 2),
        out_specs=VMEM,
        compiler_params=pltpu.CompilerParams(vmem_limit_bytes=12 * MIB),
        cost_estimate=pl.CostEstimate(
            flops=OVERLAP * tokens * w_o.size, bytes_accessed=2 * w_o.size, transcendentals=0
        ),
        name="out_proj",
    )(place, *blocks, w_o, residual)


def add_products(totals, n_exp, place, steps, blocks, gain, gate, up):
    whole = blocks[0].shape[1] == gate.shape[2]
    units = gate.shape[1]
    width = blocks[0].shape[1]
    for step, block in zip(steps, blocks):
        columns = pl.ds(0, width)
        if not whole:
            columns = pl.ds(pl.multiple_of((place[1] ^ step) * width, LANES), width)
        rows = block[...].astype(jnp.float32) * gain[:, columns].astype(jnp.float32)
        rows = rows.astype(jnp.bfloat16)
        for m, weights in enumerate((gate, up)):
            for e in range(n_exp):
                product = lax.dot_general(
                    weights[e, :, columns], rows, NT, preferred_element_type=jnp.float32
                )
                at = m * n_exp + e
                totals[at] = product if totals[at] is None else totals[at] + product
    return totals


def part_kernel(steps, place, block, gain, gate, up, *refs):
    n_exp = gate.shape[0]
    fetch = None
    if len(refs) > 1:
        down_hbm, out, down, sem = refs
        fetch = pltpu.make_async_copy(down_hbm.at[pl.ds(0, down.shape[0])], down, sem)
        fetch.start()
    else:
        (out,) = refs
    totals = add_products([None] * (2 * n_exp), n_exp, place, steps, [block], gain, gate, up)
    for at, total in enumerate(totals):
        out[at] = total
    if fetch is not None:
        fetch.wait()


def part(step, held, place, block, gain, w_gate, w_up, w_down):
    n_exp, units, model = w_gate.shape
    tokens, width = block.shape
    shapes = [pltpu.VMEM((2 * n_exp, units, tokens), jnp.float32)]
    if held:
        shapes.append(pltpu.VMEM((held, units, model), jnp.bfloat16))
    more = bool(held)
    return pl.pallas_call(
        functools.partial(part_kernel, [step]),
        out_shape=shapes,
        in_specs=[SMEM] + [VMEM] * 4 + [HBM] * more,
        out_specs=[VMEM] * len(shapes),
        scratch_shapes=[pltpu.SemaphoreType.DMA(())] * more,
        compiler_params=pltpu.CompilerParams(vmem_limit_bytes=12 * MIB),
        cost_estimate=pl.CostEstimate(
            flops=4 * tokens * n_exp * units * width,
            bytes_accessed=2 * held * units * model,
            transcendentals=0,
        ),
        name="part",
    )(place, block, gain, w_gate, w_up, *[w_down] * more)


def experts_kernel(n_blocks, n_parts, n_held, place, *refs):
    blocks, refs = refs[:n_blocks], refs[n_blocks:]
    parts, refs = refs[:n_parts], refs[n_parts:]
    held, refs = refs[:n_held], refs[n_held:]
    gain, routes, weights, gate, up, down_hbm, out, kept, rows, hidden, down, sem = refs
    n_exp, units, model = gate.shape
    first = n_exp - down.shape[0]
    fetch = pltpu.make_async_copy(down_hbm.at[pl.ds(first, n_exp - first)], down, sem)
    fetch.start()
    downs = list(held) + [down]
    tokens = rows.shape[0]
    width = blocks[0].shape[1]
    totals = [None] * (2 * n_exp)
    for done in parts:
        totals = [done[at] if t is None else t + done[at] for at, t in enumerate(totals)]
    steps = range(n_parts, n_blocks)
    totals = add_products(totals, n_exp, place, steps, blocks[n_parts:], gain, gate, up)
    for s, block in enumerate(blocks):
        if n_blocks == 1:
            rows[...] = block[...]
        else:
            offset = pl.multiple_of((place[1] ^ s) * width, LANES)
            rows[:, pl.ds(offset, width)] = block[...]
    squares = sum(
        jnp.sum(jnp.square(b[...].astype(jnp.float32)), axis=-1, keepdims=True) for b in blocks
    )
    scale = lax.rsqrt(squares / model + NORM_EPS)
    eye = lax.broadcasted_iota(jnp.int32, (tokens, tokens), 0) == lax.broadcasted_iota(
        jnp.int32, (tokens, tokens), 1
    )
    scale = jnp.sum(jnp.where(eye, scale, 0.0), axis=0, keepdims=True)
    for e in range(n_exp):
        named = jnp.where(routes[...] == place[1] * n_exp + e, weights[...], 0.0)
        coef = jnp.sum(named, axis=0, keepdims=True)
        active = jax.nn.silu(totals[e] * scale) * (totals[n_exp + e] * scale) * coef
        hidden[:, e * units : (e + 1) * units] = active.T.astype(jnp.bfloat16)
    sliced = len(out.shape) == 4
    if sliced:
        n_chunks, per, chunk = out.shape[1:]
        columns = pl.ds(pl.multiple_of(place[0] * chunk, LANES), chunk)
        own = one_hot((per, tokens), lambda row: row + place[1] * per)
        kept[...] = jnp.dot(own, rows[:, columns], preferred_element_type=jnp.float32)
    else:
        n_chunks, chunk = 8, model // 8
        kept[...] = rows[...].astype(jnp.float32)
    split = [0, first * units, n_exp * units] if n_held else [0, n_exp * units]
    fetch.wait()
    for j in range(n_chunks):
        columns = slice(j * chunk, (j + 1) * chunk)
        total = sum(
            jnp.dot(
                hidden[:, start:end],
                part_down[:, :, columns].reshape(end - start, chunk),
                preferred_element_type=jnp.float32,
            )
            for start, end, part_down in zip(split, split[1:], downs)
        ).astype(out.dtype)
        if sliced:
            for q in range(out.shape[0]):
                out[q, j] = total[q * per : (q + 1) * per]
        else:
            out[:, columns] = total


def experts(blocks, gain, routes, route_weight, w_gate, w_up, w_down, place, n_req, n_ctx):
    n_exp, units, model = w_gate.shape
    tokens = blocks[0].shape[0]
    slice_width = model // n_ctx
    aligned = slice_width % LANES == 0
    w_gate, w_up = [pltpu.with_memory_space_constraint(w, pltpu.VMEM) for w in (w_gate, w_up)]
    w_down = pltpu.with_memory_space_constraint(w_down, pltpu.HBM)
    parts, held = [], []
    if len(blocks) > 2:
        (first, *held), (second,) = [
            part(s, n, place, blocks[s], gain, w_gate, w_up, w_down)
            for s, n in ((0, n_exp // 2), (1, 0))
        ]
        parts = [first, second]
    rest = n_exp - sum(w.shape[0] for w in held)
    shape = (n_req, n_ctx, tokens // n_req, slice_width) if aligned else (tokens, model)
    kept = (tokens // n_req, slice_width) if aligned else (tokens, model)
    return pl.pallas_call(
        functools.partial(experts_kernel, len(blocks), len(parts), len(held)),
        out_shape=[
            jax.ShapeDtypeStruct(shape, jnp.bfloat16),
            jax.ShapeDtypeStruct(kept, jnp.float32),
        ],
        in_specs=[SMEM] + [VMEM] * (len(blocks) + len(parts) + len(held) + 5) + [HBM],
        out_specs=[VMEM, VMEM],
        scratch_shapes=[
            pltpu.VMEM((tokens, model), jnp.bfloat16),
            pltpu.VMEM((tokens, n_exp * units), jnp.bfloat16),
            pltpu.VMEM((rest, units, model), jnp.bfloat16),
            pltpu.SemaphoreType.DMA(()),
        ],
        compiler_params=pltpu.CompilerParams(vmem_limit_bytes=12 * MIB),
        cost_estimate=pl.CostEstimate(
            flops=6 * tokens * w_gate.size,
            bytes_accessed=6 * w_gate.size,
            transcendentals=n_exp * units * tokens,
        ),
        name="experts",
    )(place, *blocks, *parts, *held, gain, routes, route_weight, w_gate, w_up, w_down)


def local(
    residual,
    query,
    latent_cache,
    lengths,
    w_uv,
    w_o,
    norm_gain,
    routes,
    route_weight,
    w_gate,
    w_up,
    w_down,
):
    n_ctx = lax.axis_size("ctx")
    n_req = lax.axis_size("req")
    at_ctx = lax.axis_index("ctx").astype(jnp.int32)
    at_req = lax.axis_index("req").astype(jnp.int32)
    place = jnp.stack([at_ctx, at_req])
    chip_steps = range(CORES, n_ctx, CORES)
    req_steps = range(1, n_req)
    req_local = latent_cache.shape[0]
    heads_local, lat_width, _ = w_uv.shape
    tok_local = query.shape[0]
    q_tokens = tok_local // req_local

    cache = jnp.swapaxes(latent_cache, 1, 2)
    other_cache = swap(cache, "ctx", 1, n_ctx)
    query = query.reshape(req_local, q_tokens * heads_local, query.shape[2])
    received = [swap(query, "ctx", s, n_ctx) for s in chip_steps]
    cache, query, w_uv, w_o = stage(place, [cache, query, w_uv, w_o])
    blocks = [query] + received
    outs = attend(blocks, (cache, other_cache), lengths, place, lat_width, q_tokens)
    outs = [outs[0]] + [swap(o, "ctx", s, n_ctx) for o, s in zip(outs[1:], chip_steps)]

    logs_in = [
        o[..., lat_width].astype(jnp.float32) + o[..., lat_width + 1].astype(jnp.float32)
        for o in outs
    ]
    top_log = functools.reduce(jnp.maximum, logs_in)
    factors = [jnp.exp(log - top_log) for log in logs_in]
    numer = sum(f[..., None] * o[..., :lat_width].astype(jnp.float32) for f, o in zip(factors, outs))
    latent = (numer / sum(factors)[..., None]).astype(jnp.bfloat16)
    latent = latent.reshape(tok_local, heads_local, lat_width)
    projected = jnp.einsum("nhd,hde->nhe", latent, w_uv, preferred_element_type=jnp.float32)
    head_values = projected.astype(jnp.bfloat16).reshape(tok_local, -1)
    blocks = [head_values] + [swap(head_values, "req", s, n_req) for s in req_steps]
    partial_mid = out_proj(blocks, w_o, residual, place)

    other = swap(partial_mid, "ctx", 1, n_ctx)
    chip_mid = (partial_mid.astype(jnp.float32) + other.astype(jnp.float32)).astype(jnp.bfloat16)
    parts = [chip_mid] + [swap(chip_mid, "ctx", s, n_ctx) for s in chip_steps]
    mid = sum(p.astype(jnp.float32) for p in parts).astype(jnp.bfloat16)
    if mid.shape[1] % LANES == 0:
        blocks = [mid] + [swap(mid, "req", s, n_req) for s in req_steps]
    else:
        blocks = [lax.all_gather(mid, "req", axis=1, tiled=True)]

    partial_sum, kept = experts(
        blocks,
        norm_gain.reshape(1, -1),
        routes.T,
        route_weight.T,
        w_gate,
        w_up,
        w_down,
        place,
        n_req,
        n_ctx,
    )
    tokens = mid.shape[0]
    model_width = w_gate.shape[2]
    rows_out = tokens // n_req
    slice_width = model_width // n_ctx
    if partial_sum.ndim == 2:
        partial_sum = partial_sum.reshape(n_req, rows_out, n_ctx, slice_width)
        partial_sum = jnp.swapaxes(partial_sum, 1, 2)
        kept = lax.dynamic_slice(
            kept, (at_req * rows_out, at_ctx * slice_width), (rows_out, slice_width)
        )
    partial_sum = partial_sum.reshape(n_req * n_ctx, rows_out, slice_width)
    landed = lax.all_to_all(partial_sum, ("req", "ctx"), split_axis=0, concat_axis=0, tiled=True)
    return (kept + jnp.sum(landed.astype(jnp.float32), axis=0)).astype(jnp.bfloat16)


def solution(mesh):
    in_specs = (
        P("ctx", "req"),
        P("req", "ctx", None),
        P("req", "ctx", None),
        P("req"),
        P("ctx", None, None),
        P("ctx", "req"),
        P(),
        P(),
        P(),
        P("req", "ctx", None),
        P("req", "ctx", None),
        P("req", "ctx", None),
    )
    out_specs = P("req", "ctx")
    return jax.shard_map(local, mesh=mesh, in_specs=in_specs, out_specs=out_specs, check_vma=False)
```

```python
import functools

import jax
import jax.numpy as jnp
from jax import lax
from jax.experimental import pallas as pl
from jax.experimental.pallas import tpu as pltpu
from jax.sharding import PartitionSpec as P

SOFTMAX_SCALE = 192.0 ** (-0.5)
NEG_FILL = -1e30
NORM_EPS = 1e-06
CORES = 2
OVERLAP = 800
LANES = 128
DEPTH = 256
MIB = 1 << 20
NT = (((1,), (1,)), ((), ()))
VMEM = pl.BlockSpec(memory_space=pltpu.VMEM)
SMEM = pl.BlockSpec(memory_space=pltpu.SMEM)
HBM = pl.BlockSpec(memory_space=pltpu.HBM)


def swap(x, axis, step, size):
    return lax.ppermute(x, axis, [(i, i ^ step) for i in range(size)])


def stack_rows(blocks):
    if len(blocks) == 1:
        return blocks[0]
    if all(b.shape[0] % 16 == 0 for b in blocks):
        return jnp.concatenate(blocks, axis=0)
    return jnp.concatenate([b.astype(jnp.float32) for b in blocks], axis=0).astype(blocks[0].dtype)


def attend_kernel(n_blocks, q_tokens, width, place, lengths, *refs):
    queries, caches, outs = refs[:n_blocks], refs[n_blocks : n_blocks + 2], refs[n_blocks + 2 :]
    req_local, rows, _ = queries[0].shape
    ctx_local = caches[0].shape[2]
    total_rows = n_blocks * rows
    heads_local = rows // q_tokens
    row = lax.broadcasted_iota(jnp.int32, (total_rows, ctx_local), 0)
    column = lax.broadcasted_iota(jnp.int32, (total_rows, ctx_local), 1)
    token = (row // heads_local) % q_tokens
    lane = lax.broadcasted_iota(jnp.int32, (total_rows, LANES), 1)
    for r in range(req_local):
        grouped = stack_rows([q[r] for q in queries])
        limit = lengths[r] - q_tokens + token
        masked = []
        for half, cache in enumerate(caches):
            score = jnp.dot(grouped, cache[r], preferred_element_type=jnp.float32)
            visible = column + (place[0] ^ half) * ctx_local <= limit
            masked.append(jnp.where(visible, score * SOFTMAX_SCALE, -jnp.inf))
        peak = jnp.maximum(
            jnp.max(masked[0], axis=-1, keepdims=True), jnp.max(masked[1], axis=-1, keepdims=True)
        )
        peak = jnp.where(peak > -jnp.inf, peak, 0.0)
        total = jnp.zeros((total_rows, 1), jnp.float32)
        mixed = jnp.zeros((total_rows, width), jnp.float32)
        for scores, cache in zip(masked, caches):
            raised = jnp.exp(scores - peak)
            total += jnp.sum(raised, axis=-1, keepdims=True)
            mixed += lax.dot_general(
                raised.astype(jnp.bfloat16),
                cache[r, :width, :],
                NT,
                preferred_element_type=jnp.float32,
            )
        filled = total > 0.0
        safe = jnp.where(filled, total, 1.0)
        mean = jnp.where(filled, mixed / safe, 0.0).astype(jnp.bfloat16)
        log = jnp.where(filled, peak + jnp.log(safe), NEG_FILL)
        high = log.astype(jnp.bfloat16).astype(jnp.float32)
        tail = jnp.where(lane == 0, high, jnp.where(lane == 1, log - high, 0.0))
        tail = tail.astype(jnp.bfloat16)
        for s, out in enumerate(outs):
            out[r, :, :width] = mean[s * rows : (s + 1) * rows]
            out[r, :, width:] = tail[s * rows : (s + 1) * rows]


def attend(blocks, caches, lengths, place, width, q_tokens):
    req_local, rows, lat = blocks[0].shape
    n = len(blocks)
    ctx_local = caches[0].shape[2]
    shape = jax.ShapeDtypeStruct((req_local, rows, width + LANES), jnp.bfloat16)
    return pl.pallas_call(
        functools.partial(attend_kernel, n, q_tokens, width),
        out_shape=[shape] * n,
        in_specs=[SMEM, SMEM] + [VMEM] * (n + 2),
        out_specs=[VMEM] * n,
        compiler_params=pltpu.CompilerParams(vmem_limit_bytes=16 * MIB),
        cost_estimate=pl.CostEstimate(
            flops=4 * req_local * n * rows * ctx_local * (lat + width),
            bytes_accessed=4 * req_local * ctx_local * lat,
            transcendentals=2 * req_local * n * rows * ctx_local,
        ),
        name="attend",
    )(place, lengths, *blocks, *caches)


def stage_kernel(place, *refs):
    n = len(refs) // 2
    sems = refs[-1]
    copies = [
        pltpu.make_async_copy(source, target, sems.at[i])
        for i, (source, target) in enumerate(zip(refs[:n], refs[n : 2 * n]))
    ]
    for copy in copies:
        copy.start()
    for copy in copies:
        copy.wait()


def stage(place, arrays):
    return pl.pallas_call(
        stage_kernel,
        out_shape=[pltpu.VMEM(x.shape, x.dtype) for x in arrays],
        in_specs=[SMEM] + [HBM] * len(arrays),
        out_specs=[VMEM] * len(arrays),
        scratch_shapes=[pltpu.SemaphoreType.DMA((len(arrays),))],
        compiler_params=pltpu.CompilerParams(vmem_limit_bytes=16 * MIB),
        cost_estimate=pl.CostEstimate(
            flops=0, bytes_accessed=sum(x.size * 2 for x in arrays), transcendentals=0
        ),
        name="stage",
    )(place, *[pltpu.with_memory_space_constraint(x, pltpu.HBM) for x in arrays])


def one_hot(shape, target):
    at = lax.broadcasted_iota(jnp.int32, shape, 1)
    return jnp.where(at == target(lax.broadcasted_iota(jnp.int32, shape, 0)), 1.0, 0.0).astype(
        jnp.bfloat16
    )


def out_proj_kernel(n_blocks, place, *refs):
    blocks, (w_o, residual, out) = refs[:n_blocks], refs[n_blocks:]
    per = blocks[0].shape[0]
    tokens = n_blocks * per
    stacked = stack_rows([b[...] for b in blocks])
    order = one_hot((tokens, tokens), lambda row: (row // per ^ place[1]) * per + row % per)
    ordered = jnp.dot(order, stacked, preferred_element_type=jnp.float32).astype(jnp.bfloat16)
    total = jnp.dot(ordered, w_o[...], preferred_element_type=jnp.float32)
    own = residual.shape[0]
    row = lax.broadcasted_iota(jnp.int32, total.shape, 0) - place[0] * own
    rows = residual[...].astype(jnp.float32)
    for i in range(own):
        total += jnp.where(row == i, rows[i : i + 1], 0.0)
    out[...] = total.astype(out.dtype)


def out_proj(blocks, w_o, residual, place):
    n = len(blocks)
    tokens = n * blocks[0].shape[0]
    return pl.pallas_call(
        functools.partial(out_proj_kernel, n),
        out_shape=jax.ShapeDtypeStruct((tokens, w_o.shape[1]), jnp.bfloat16),
        in_specs=[SMEM] + [VMEM] * (n + 2),
        out_specs=VMEM,
        compiler_params=pltpu.CompilerParams(vmem_limit_bytes=8 * MIB),
        cost_estimate=pl.CostEstimate(
            flops=OVERLAP * tokens * w_o.size, bytes_accessed=2 * w_o.size, transcendentals=0
        ),
        name="out_proj",
    )(place, *blocks, w_o, residual)


def add_products(gates, ups, place, steps, blocks, gain, gate, up):
    n_exp = gate.shape[0]
    width = blocks[0].shape[1]
    for step, block in zip(steps, blocks):
        offset, columns = None, pl.ds(0, width)
        if width < gate.shape[2]:
            offset = (place[1] ^ step) * width
            columns = pl.ds(pl.multiple_of(offset, LANES), width)
        rows = block[...].astype(jnp.float32) * gain[:, columns].astype(jnp.float32)
        rows = rows.astype(jnp.bfloat16)
        for e in range(n_exp):
            for k in range(0, width, DEPTH):
                deep = min(DEPTH, width - k)
                part_columns = pl.ds(pl.multiple_of(offset + k, LANES) if offset is not None else k, deep)
                left = lax.dot_general(
                    rows[:, k : k + deep],
                    gate[e, :, part_columns],
                    NT,
                    preferred_element_type=jnp.float32,
                )
                gates[e] = left if gates[e] is None else gates[e] + left
            right = lax.dot_general(up[e, :, columns], rows, NT, preferred_element_type=jnp.float32)
            ups[e] = right if ups[e] is None else ups[e] + right
    return gates, ups


def part_kernel(steps, first, place, block, gain, gate, up, *refs):
    n_exp = gate.shape[0]
    fetch = None
    if len(refs) > 2:
        down_hbm, gates_out, ups_out, down, sem = refs
        fetch = pltpu.make_async_copy(down_hbm.at[pl.ds(first, down.shape[0])], down, sem)
        fetch.start()
    else:
        gates_out, ups_out = refs
    none = [None] * n_exp
    gates, ups = add_products(none[:], none[:], place, steps, [block], gain, gate, up)
    for e in range(n_exp):
        gates_out[e] = gates[e]
        ups_out[e] = ups[e]
    if fetch is not None:
        fetch.wait()


def part(step, first, held, place, block, gain, w_gate, w_up, w_down):
    n_exp, units, model = w_gate.shape
    tokens, width = block.shape
    shapes = [
        pltpu.VMEM((n_exp, tokens, units), jnp.float32),
        pltpu.VMEM((n_exp, units, tokens), jnp.float32),
    ]
    if held:
        shapes.append(pltpu.VMEM((held, units, model), jnp.bfloat16))
    more = bool(held)
    return pl.pallas_call(
        functools.partial(part_kernel, [step], first),
        out_shape=shapes,
        in_specs=[SMEM] + [VMEM] * 4 + [HBM] * more,
        out_specs=[VMEM] * len(shapes),
        scratch_shapes=[pltpu.SemaphoreType.DMA(())] * more,
        compiler_params=pltpu.CompilerParams(vmem_limit_bytes=8 * MIB),
        cost_estimate=pl.CostEstimate(
            flops=4 * tokens * n_exp * units * width,
            bytes_accessed=2 * held * units * model,
            transcendentals=0,
        ),
        name="part",
    )(place, block, gain, w_gate, w_up, *[w_down] * more)


def experts_kernel(n_blocks, n_parts, n_held, place, *refs):
    blocks, refs = refs[:n_blocks], refs[n_blocks:]
    parts, refs = refs[: 2 * n_parts], refs[2 * n_parts :]
    held, refs = refs[:n_held], refs[n_held:]
    gain, routes, weights, gate, up, down_hbm, out, kept, rows, hidden, down, sem = refs
    n_exp, units, model = gate.shape
    first = sum(w.shape[0] for w in held)
    fetch = pltpu.make_async_copy(down_hbm.at[pl.ds(first, n_exp - first)], down, sem)
    fetch.start()
    downs = list(held) + [down]
    tokens = rows.shape[0]
    width = blocks[0].shape[1]
    steps = range(n_parts, n_blocks)
    gates, ups = add_products(
        [None] * n_exp, [None] * n_exp, place, steps, blocks[n_parts:], gain, gate, up
    )
    for e in range(n_exp):
        gates[e] = sum([done[e] for done in parts[::2]], gates[e])
        ups[e] = sum([done[e] for done in parts[1::2]], ups[e])
    for s, block in enumerate(blocks):
        if n_blocks == 1:
            rows[...] = block[...]
        else:
            offset = pl.multiple_of((place[1] ^ s) * width, LANES)
            rows[:, pl.ds(offset, width)] = block[...]
    squares = sum(
        jnp.sum(jnp.square(b[...].astype(jnp.float32)), axis=-1, keepdims=True) for b in blocks
    )
    scale = lax.rsqrt(squares / model + NORM_EPS)
    eye = lax.broadcasted_iota(jnp.int32, (tokens, tokens), 0) == lax.broadcasted_iota(
        jnp.int32, (tokens, tokens), 1
    )
    for e in range(n_exp):
        named = jnp.where(routes[...] == place[1] * n_exp + e, weights[...], 0.0)
        coef = jnp.sum(named, axis=0, keepdims=True)
        coef = jnp.sum(jnp.where(eye, coef, 0.0), axis=1, keepdims=True)
        active = jax.nn.silu(gates[e] * scale) * (ups[e].T * scale) * coef
        hidden[:, e * units : (e + 1) * units] = active.astype(jnp.bfloat16)
    sliced = len(out.shape) == 4
    if sliced:
        n_chunks, per, chunk = out.shape[1:]
        columns = pl.ds(pl.multiple_of(place[0] * chunk, LANES), chunk)
        own = one_hot((per, tokens), lambda row: row + place[1] * per)
        kept[...] = jnp.dot(own, rows[:, columns], preferred_element_type=jnp.float32)
    else:
        n_chunks, chunk = 8, model // 8
        kept[...] = rows[...].astype(jnp.float32)
    split = [0]
    for weights in downs:
        split.append(split[-1] + weights.shape[0] * units)
    fetch.wait()
    for j in range(n_chunks):
        columns = slice(j * chunk, (j + 1) * chunk)
        total = sum(
            jnp.dot(
                hidden[:, start:end],
                part_down[:, :, columns].reshape(end - start, chunk),
                preferred_element_type=jnp.float32,
            )
            for start, end, part_down in zip(split, split[1:], downs)
        ).astype(out.dtype)
        if sliced:
            for q in range(out.shape[0]):
                out[q, j] = total[q * per : (q + 1) * per]
        else:
            out[:, columns] = total


def experts(blocks, gain, routes, route_weight, w_gate, w_up, w_down, place, n_req, n_ctx):
    n_exp, units, model = w_gate.shape
    tokens = blocks[0].shape[0]
    slice_width = model // n_ctx
    aligned = slice_width % LANES == 0
    w_gate, w_up = [pltpu.with_memory_space_constraint(w, pltpu.VMEM) for w in (w_gate, w_up)]
    w_down = pltpu.with_memory_space_constraint(w_down, pltpu.HBM)
    parts, held = [], []
    if len(blocks) > 2:
        for s, (first, number) in enumerate(((0, n_exp // 2), (n_exp // 2, n_exp // 4))):
            made = part(s, first, number, place, blocks[s], gain, w_gate, w_up, w_down)
            parts += made[:2]
            held += made[2:]
    rest = n_exp - sum(w.shape[0] for w in held)
    shape = (n_req, n_ctx, tokens // n_req, slice_width) if aligned else (tokens, model)
    kept = (tokens // n_req, slice_width) if aligned else (tokens, model)
    return pl.pallas_call(
        functools.partial(experts_kernel, len(blocks), len(parts) // 2, len(held)),
        out_shape=[
            jax.ShapeDtypeStruct(shape, jnp.bfloat16),
            jax.ShapeDtypeStruct(kept, jnp.float32),
        ],
        in_specs=[SMEM] + [VMEM] * (len(blocks) + len(parts) + len(held) + 5) + [HBM],
        out_specs=[VMEM, VMEM],
        scratch_shapes=[
            pltpu.VMEM((tokens, model), jnp.bfloat16),
            pltpu.VMEM((tokens, n_exp * units), jnp.bfloat16),
            pltpu.VMEM((rest, units, model), jnp.bfloat16),
            pltpu.SemaphoreType.DMA(()),
        ],
        compiler_params=pltpu.CompilerParams(vmem_limit_bytes=8 * MIB),
        cost_estimate=pl.CostEstimate(
            flops=6 * tokens * w_gate.size,
            bytes_accessed=6 * w_gate.size,
            transcendentals=n_exp * units * tokens,
        ),
        name="experts",
    )(place, *blocks, *parts, *held, gain, routes, route_weight, w_gate, w_up, w_down)


def local(
    residual,
    query,
    latent_cache,
    lengths,
    w_uv,
    w_o,
    norm_gain,
    routes,
    route_weight,
    w_gate,
    w_up,
    w_down,
):
    n_ctx = lax.axis_size("ctx")
    n_req = lax.axis_size("req")
    at_ctx = lax.axis_index("ctx").astype(jnp.int32)
    at_req = lax.axis_index("req").astype(jnp.int32)
    place = jnp.stack([at_ctx, at_req])
    chip_steps = range(CORES, n_ctx, CORES)
    req_steps = range(1, n_req)
    req_local = latent_cache.shape[0]
    heads_local, lat_width, _ = w_uv.shape
    tok_local = query.shape[0]
    q_tokens = tok_local // req_local

    cache = jnp.swapaxes(latent_cache, 1, 2)
    other_cache = swap(cache, "ctx", 1, n_ctx)
    query = query.reshape(req_local, q_tokens * heads_local, query.shape[2])
    received = [swap(query, "ctx", s, n_ctx) for s in chip_steps]
    cache, query, w_uv, w_o = stage(place, [cache, query, w_uv, w_o])
    blocks = [query] + received
    outs = attend(blocks, (cache, other_cache), lengths, place, lat_width, q_tokens)
    outs = [outs[0]] + [swap(o, "ctx", s, n_ctx) for o, s in zip(outs[1:], chip_steps)]

    logs_in = [
        o[..., lat_width].astype(jnp.float32) + o[..., lat_width + 1].astype(jnp.float32)
        for o in outs
    ]
    top_log = functools.reduce(jnp.maximum, logs_in)
    factors = [jnp.exp(log - top_log) for log in logs_in]
    numer = sum(f[..., None] * o[..., :lat_width].astype(jnp.float32) for f, o in zip(factors, outs))
    latent = (numer / sum(factors)[..., None]).astype(jnp.bfloat16)
    latent = latent.reshape(tok_local, heads_local, lat_width)
    projected = jnp.einsum("nhd,hde->nhe", latent, w_uv, preferred_element_type=jnp.float32)
    head_values = projected.astype(jnp.bfloat16).reshape(tok_local, -1)
    blocks = [head_values] + [swap(head_values, "req", s, n_req) for s in req_steps]
    partial_mid = out_proj(blocks, w_o, residual, place)

    mid = partial_mid
    step = 1
    while step < n_ctx:
        other = swap(mid, "ctx", step, n_ctx)
        mid = (mid.astype(jnp.float32) + other.astype(jnp.float32)).astype(jnp.bfloat16)
        step *= 2
    if mid.shape[1] % LANES == 0:
        blocks = [mid] + [swap(mid, "req", s, n_req) for s in req_steps]
    else:
        blocks = [lax.all_gather(mid, "req", axis=1, tiled=True)]

    partial_sum, kept = experts(
        blocks,
        norm_gain.reshape(1, -1),
        routes.T,
        route_weight.T,
        w_gate,
        w_up,
        w_down,
        place,
        n_req,
        n_ctx,
    )
    tokens = mid.shape[0]
    model_width = w_gate.shape[2]
    rows_out = tokens // n_req
    slice_width = model_width // n_ctx
    if partial_sum.ndim == 2:
        partial_sum = partial_sum.reshape(n_req, rows_out, n_ctx, slice_width)
        partial_sum = jnp.swapaxes(partial_sum, 1, 2)
        kept = lax.dynamic_slice(
            kept, (at_req * rows_out, at_ctx * slice_width), (rows_out, slice_width)
        )
    partial_sum = partial_sum.reshape(n_req * n_ctx, rows_out, slice_width)
    landed = lax.all_to_all(partial_sum, ("req", "ctx"), split_axis=0, concat_axis=0, tiled=True)
    return (kept + jnp.sum(landed.astype(jnp.float32), axis=0)).astype(jnp.bfloat16)


def solution(mesh):
    in_specs = (
        P("ctx", "req"),
        P("req", "ctx", None),
        P("req", "ctx", None),
        P("req"),
        P("ctx", None, None),
        P("ctx", "req"),
        P(),
        P(),
        P(),
        P("req", "ctx", None),
        P("req", "ctx", None),
        P("req", "ctx", None),
    )
    out_specs = P("req", "ctx")
    return jax.shard_map(local, mesh=mesh, in_specs=in_specs, out_specs=out_specs, check_vma=False)
```

```python
import functools

import jax
import jax.numpy as jnp
from jax import lax
from jax.experimental import pallas as pl
from jax.experimental.pallas import tpu as pltpu
from jax.sharding import PartitionSpec as P

SOFTMAX_SCALE = 192.0 ** (-0.5)
NEG_FILL = -1e30
NORM_EPS = 1e-06
CORES = 2
OVERLAP = 800
LANES = 128
MIB = 1 << 20
NT = (((1,), (1,)), ((), ()))
VMEM = pl.BlockSpec(memory_space=pltpu.VMEM)
HBM = pl.BlockSpec(memory_space=pltpu.HBM)


def swap(x, axis, step, size):
    return lax.ppermute(x, axis, [(i, i ^ step) for i in range(size)])


def stack_rows(blocks):
    if len(blocks) == 1:
        return blocks[0]
    if all(b.shape[0] % 16 == 0 for b in blocks):
        return jnp.concatenate(blocks, axis=0)
    return jnp.concatenate([b.astype(jnp.float32) for b in blocks], axis=0).astype(blocks[0].dtype)


def attend_kernel(n_blocks, q_tokens, width, lengths, *refs):
    queries, caches, outs = refs[:n_blocks], refs[n_blocks : n_blocks + 2], refs[n_blocks + 2 :]
    req_local, rows, _ = queries[0].shape
    ctx_local = caches[0].shape[2]
    total_rows = n_blocks * rows
    heads_local = rows // q_tokens
    row = lax.broadcasted_iota(jnp.int32, (total_rows, ctx_local), 0)
    column = lax.broadcasted_iota(jnp.int32, (total_rows, ctx_local), 1)
    token = (row // heads_local) % q_tokens
    lane = lax.broadcasted_iota(jnp.int32, (total_rows, LANES), 1)
    for r in range(req_local):
        grouped = stack_rows([q[r] for q in queries])
        limit = lengths[:, r : r + 1] - q_tokens + token
        masked = []
        for half, cache in enumerate(caches):
            score = jnp.dot(grouped, cache[r], preferred_element_type=jnp.float32)
            visible = column + (lax.axis_index("ctx") ^ half) * ctx_local <= limit
            masked.append(jnp.where(visible, score * SOFTMAX_SCALE, -jnp.inf))
        peak = jnp.maximum(
            jnp.max(masked[0], axis=-1, keepdims=True), jnp.max(masked[1], axis=-1, keepdims=True)
        )
        peak = jnp.where(peak > -jnp.inf, peak, 0.0)
        total = jnp.zeros((total_rows, 1), jnp.float32)
        mixed = jnp.zeros((total_rows, width), jnp.float32)
        for scores, cache in zip(masked, caches):
            raised = jnp.exp(scores - peak)
            total += jnp.sum(raised, axis=-1, keepdims=True)
            mixed += lax.dot_general(
                raised.astype(jnp.bfloat16),
                cache[r, :width, :],
                NT,
                preferred_element_type=jnp.float32,
            )
        filled = total > 0.0
        safe = jnp.where(filled, total, 1.0)
        mean = jnp.where(filled, mixed / safe, 0.0).astype(jnp.bfloat16)
        log = jnp.where(filled, peak + jnp.log(safe), NEG_FILL)
        high = log.astype(jnp.bfloat16).astype(jnp.float32)
        tail = jnp.where(lane == 0, high, jnp.where(lane == 1, log - high, 0.0))
        tail = tail.astype(jnp.bfloat16)
        for s, out in enumerate(outs):
            out[r, :, :width] = mean[s * rows : (s + 1) * rows]
            out[r, :, width:] = tail[s * rows : (s + 1) * rows]


def attend(blocks, caches, lengths, width, q_tokens):
    req_local, rows, lat = blocks[0].shape
    n = len(blocks)
    ctx_local = caches[0].shape[2]
    shape = jax.ShapeDtypeStruct((req_local, rows, width + LANES), jnp.bfloat16)
    return pl.pallas_call(
        functools.partial(attend_kernel, n, q_tokens, width),
        out_shape=[shape] * n,
        in_specs=[VMEM] * (n + 3),
        out_specs=[VMEM] * n,
        compiler_params=pltpu.CompilerParams(vmem_limit_bytes=16 * MIB),
        cost_estimate=pl.CostEstimate(
            flops=4 * req_local * n * rows * ctx_local * (lat + width),
            bytes_accessed=4 * req_local * ctx_local * lat,
            transcendentals=2 * req_local * n * rows * ctx_local,
        ),
        name="attend",
    )(lengths.reshape(1, -1), *blocks, *caches)


def stage_kernel(*refs):
    n = len(refs) // 2
    sems = refs[-1]
    copies = [
        pltpu.make_async_copy(source, target, sems.at[i])
        for i, (source, target) in enumerate(zip(refs[:n], refs[n : 2 * n]))
    ]
    for copy in copies:
        copy.start()
    for copy in copies:
        copy.wait()


def stage(arrays):
    return pl.pallas_call(
        stage_kernel,
        out_shape=[pltpu.VMEM(x.shape, x.dtype) for x in arrays],
        in_specs=[HBM] * len(arrays),
        out_specs=[VMEM] * len(arrays),
        scratch_shapes=[pltpu.SemaphoreType.DMA((len(arrays),))],
        compiler_params=pltpu.CompilerParams(vmem_limit_bytes=16 * MIB),
        cost_estimate=pl.CostEstimate(
            flops=0, bytes_accessed=sum(x.size * 2 for x in arrays), transcendentals=0
        ),
        name="stage",
    )(*[pltpu.with_memory_space_constraint(x, pltpu.HBM) for x in arrays])


def one_hot(shape, target):
    at = lax.broadcasted_iota(jnp.int32, shape, 1)
    return jnp.where(at == target(lax.broadcasted_iota(jnp.int32, shape, 0)), 1.0, 0.0).astype(
        jnp.bfloat16
    )


def out_proj_kernel(n_blocks, *refs):
    blocks, (w_o, residual, out) = refs[:n_blocks], refs[n_blocks:]
    per = blocks[0].shape[0]
    tokens = n_blocks * per
    stacked = stack_rows([b[...] for b in blocks])
    at_ctx, at_req = lax.axis_index("ctx"), lax.axis_index("req")
    order = one_hot((tokens, tokens), lambda row: (row // per ^ at_req) * per + row % per)
    ordered = jnp.dot(order, stacked, preferred_element_type=jnp.float32).astype(jnp.bfloat16)
    total = jnp.dot(ordered, w_o[...], preferred_element_type=jnp.float32)
    own = residual.shape[0]
    row = lax.broadcasted_iota(jnp.int32, total.shape, 0) - at_ctx * own
    rows = residual[...].astype(jnp.float32)
    for i in range(own):
        total += jnp.where(row == i, rows[i : i + 1], 0.0)
    out[...] = total.astype(out.dtype)


def out_proj(blocks, w_o, residual):
    n = len(blocks)
    tokens = n * blocks[0].shape[0]
    return pl.pallas_call(
        functools.partial(out_proj_kernel, n),
        out_shape=jax.ShapeDtypeStruct((tokens, w_o.shape[1]), jnp.bfloat16),
        in_specs=[VMEM] * (n + 2),
        out_specs=VMEM,
        compiler_params=pltpu.CompilerParams(vmem_limit_bytes=8 * MIB),
        cost_estimate=pl.CostEstimate(
            flops=OVERLAP * tokens * w_o.size, bytes_accessed=2 * w_o.size, transcendentals=0
        ),
        name="out_proj",
    )(*blocks, w_o, residual)


def add_products(totals, steps, blocks, gain, gate, up):
    n_exp = gate.shape[0]
    width = blocks[0].shape[1]
    for step, block in zip(steps, blocks):
        columns = pl.ds(0, width)
        if width < gate.shape[2]:
            columns = pl.ds(pl.multiple_of((lax.axis_index("req") ^ step) * width, LANES), width)
        rows = block[...].astype(jnp.float32) * gain[:, columns].astype(jnp.float32)
        rows = rows.astype(jnp.bfloat16)
        for m, weights in enumerate((gate, up)):
            for e in range(n_exp):
                product = lax.dot_general(
                    weights[e, :, columns], rows, NT, preferred_element_type=jnp.float32
                )
                at = m * n_exp + e
                totals[at] = product if totals[at] is None else totals[at] + product
    return totals


def part_kernel(steps, first, block, gain, gate, up, *refs):
    n_exp = gate.shape[0]
    fetch = None
    if len(refs) > 1:
        down_hbm, out, down, sem = refs
        fetch = pltpu.make_async_copy(down_hbm.at[pl.ds(first, down.shape[0])], down, sem)
        fetch.start()
    else:
        (out,) = refs
    totals = add_products([None] * (2 * n_exp), steps, [block], gain, gate, up)
    for at, total in enumerate(totals):
        out[at] = total
    if fetch is not None:
        fetch.wait()


def part(step, first, held, block, gain, w_gate, w_up, w_down):
    n_exp, units, model = w_gate.shape
    tokens, width = block.shape
    shapes = [pltpu.VMEM((2 * n_exp, units, tokens), jnp.float32)]
    if held:
        shapes.append(pltpu.VMEM((held, units, model), jnp.bfloat16))
    more = bool(held)
    return pl.pallas_call(
        functools.partial(part_kernel, [step], first),
        out_shape=shapes,
        in_specs=[VMEM] * 4 + [HBM] * more,
        out_specs=[VMEM] * len(shapes),
        scratch_shapes=[pltpu.SemaphoreType.DMA(())] * more,
        compiler_params=pltpu.CompilerParams(vmem_limit_bytes=8 * MIB),
        cost_estimate=pl.CostEstimate(
            flops=4 * tokens * n_exp * units * width,
            bytes_accessed=2 * held * units * model,
            transcendentals=0,
        ),
        name="part",
    )(block, gain, w_gate, w_up, *[w_down] * more)


def experts_kernel(n_blocks, n_parts, n_held, *refs):
    blocks, refs = refs[:n_blocks], refs[n_blocks:]
    parts, refs = refs[:n_parts], refs[n_parts:]
    held, refs = refs[:n_held], refs[n_held:]
    gain, routes, weights, gate, up, down_hbm, out, kept, rows, hidden, down, sem = refs
    at_ctx, at_req = lax.axis_index("ctx"), lax.axis_index("req")
    n_exp, units, model = gate.shape
    first = sum(w.shape[0] for w in held)
    fetch = pltpu.make_async_copy(down_hbm.at[pl.ds(first, n_exp - first)], down, sem)
    fetch.start()
    downs = list(held) + [down]
    tokens = rows.shape[0]
    width = blocks[0].shape[1]
    steps = range(n_parts, n_blocks)
    totals = [None] * (2 * n_exp)
    for done in parts:
        totals = [done[at] if t is None else t + done[at] for at, t in enumerate(totals)]
    totals = add_products(totals, steps, blocks[n_parts:], gain, gate, up)
    totals = [t.T for t in totals]
    for s, block in enumerate(blocks):
        if n_blocks == 1:
            rows[...] = block[...]
        else:
            offset = pl.multiple_of((at_req ^ s) * width, LANES)
            rows[:, pl.ds(offset, width)] = block[...]
    squares = sum(
        jnp.sum(jnp.square(b[...].astype(jnp.float32)), axis=-1, keepdims=True) for b in blocks
    )
    scale = lax.rsqrt(squares / model + NORM_EPS)
    eye = lax.broadcasted_iota(jnp.int32, (tokens, tokens), 0) == lax.broadcasted_iota(
        jnp.int32, (tokens, tokens), 1
    )
    for e in range(n_exp):
        named = jnp.where(routes[...] == at_req * n_exp + e, weights[...], 0.0)
        coef = jnp.sum(named, axis=0, keepdims=True)
        coef = jnp.sum(jnp.where(eye, coef, 0.0), axis=1, keepdims=True)
        active = jax.nn.silu(totals[e] * scale) * (totals[n_exp + e] * scale) * coef
        hidden[:, e * units : (e + 1) * units] = active.astype(jnp.bfloat16)
    sliced = len(out.shape) == 4
    if sliced:
        n_chunks, per, chunk = out.shape[1:]
        columns = pl.ds(pl.multiple_of(at_ctx * chunk, LANES), chunk)
        own = one_hot((per, tokens), lambda row: row + at_req * per)
        kept[...] = jnp.dot(own, rows[:, columns], preferred_element_type=jnp.float32)
    else:
        n_chunks, chunk = 8, model // 8
        kept[...] = rows[...].astype(jnp.float32)
    split = [0]
    for weights in downs:
        split.append(split[-1] + weights.shape[0] * units)
    fetch.wait()
    for j in range(n_chunks):
        columns = slice(j * chunk, (j + 1) * chunk)
        total = sum(
            jnp.dot(
                hidden[:, start:end],
                part_down[:, :, columns].reshape(end - start, chunk),
                preferred_element_type=jnp.float32,
            )
            for start, end, part_down in zip(split, split[1:], downs)
        ).astype(out.dtype)
        if sliced:
            for q in range(out.shape[0]):
                out[q, j] = total[q * per : (q + 1) * per]
        else:
            out[:, columns] = total


def experts(blocks, gain, routes, route_weight, w_gate, w_up, w_down, n_req, n_ctx):
    n_exp, units, model = w_gate.shape
    tokens = blocks[0].shape[0]
    slice_width = model // n_ctx
    aligned = slice_width % LANES == 0
    w_gate, w_up = [pltpu.with_memory_space_constraint(w, pltpu.VMEM) for w in (w_gate, w_up)]
    w_down = pltpu.with_memory_space_constraint(w_down, pltpu.HBM)
    parts, held = [], []
    if len(blocks) > 2:
        for s, (first, number) in enumerate(((0, n_exp // 2), (n_exp // 2, n_exp // 4))):
            made = part(s, first, number, blocks[s], gain, w_gate, w_up, w_down)
            parts += made[:1]
            held += made[1:]
    rest = n_exp - sum(w.shape[0] for w in held)
    shape = (n_req, n_ctx, tokens // n_req, slice_width) if aligned else (tokens, model)
    kept = (tokens // n_req, slice_width) if aligned else (tokens, model)
    return pl.pallas_call(
        functools.partial(experts_kernel, len(blocks), len(parts), len(held)),
        out_shape=[
            jax.ShapeDtypeStruct(shape, jnp.bfloat16),
            jax.ShapeDtypeStruct(kept, jnp.float32),
        ],
        in_specs=[VMEM] * (len(blocks) + len(parts) + len(held) + 5) + [HBM],
        out_specs=[VMEM, VMEM],
        scratch_shapes=[
            pltpu.VMEM((tokens, model), jnp.bfloat16),
            pltpu.VMEM((tokens, n_exp * units), jnp.bfloat16),
            pltpu.VMEM((rest, units, model), jnp.bfloat16),
            pltpu.SemaphoreType.DMA(()),
        ],
        compiler_params=pltpu.CompilerParams(vmem_limit_bytes=8 * MIB),
        cost_estimate=pl.CostEstimate(
            flops=6 * tokens * w_gate.size,
            bytes_accessed=6 * w_gate.size,
            transcendentals=n_exp * units * tokens,
        ),
        name="experts",
    )(*blocks, *parts, *held, gain, routes, route_weight, w_gate, w_up, w_down)


def local(
    residual,
    query,
    latent_cache,
    lengths,
    w_uv,
    w_o,
    norm_gain,
    routes,
    route_weight,
    w_gate,
    w_up,
    w_down,
):
    n_ctx = lax.axis_size("ctx")
    n_req = lax.axis_size("req")
    chip_steps = range(CORES, n_ctx, CORES)
    req_steps = range(1, n_req)
    req_local = latent_cache.shape[0]
    heads_local, lat_width, _ = w_uv.shape
    tok_local = query.shape[0]
    q_tokens = tok_local // req_local

    cache = jnp.swapaxes(latent_cache, 1, 2)
    other_cache = swap(cache, "ctx", 1, n_ctx)
    query = query.reshape(req_local, q_tokens * heads_local, query.shape[2])
    received = [swap(query, "ctx", s, n_ctx) for s in chip_steps]
    cache, query, w_uv, w_o = stage([cache, query, w_uv, w_o])
    blocks = [query] + received
    outs = attend(blocks, (cache, other_cache), lengths, lat_width, q_tokens)
    outs = [outs[0]] + [swap(o, "ctx", s, n_ctx) for o, s in zip(outs[1:], chip_steps)]

    logs_in = [
        o[..., lat_width].astype(jnp.float32) + o[..., lat_width + 1].astype(jnp.float32)
        for o in outs
    ]
    top_log = functools.reduce(jnp.maximum, logs_in)
    factors = [jnp.exp(log - top_log) for log in logs_in]
    numer = sum(f[..., None] * o[..., :lat_width].astype(jnp.float32) for f, o in zip(factors, outs))
    latent = (numer / sum(factors)[..., None]).astype(jnp.bfloat16)
    latent = latent.reshape(tok_local, heads_local, lat_width)
    projected = jnp.einsum("nhd,hde->nhe", latent, w_uv, preferred_element_type=jnp.float32)
    head_values = projected.astype(jnp.bfloat16).reshape(tok_local, -1)
    blocks = [head_values] + [swap(head_values, "req", s, n_req) for s in req_steps]
    partial_mid = out_proj(blocks, w_o, residual)

    other = swap(partial_mid, "ctx", 1, n_ctx)
    chip_mid = (partial_mid.astype(jnp.float32) + other.astype(jnp.float32)).astype(jnp.bfloat16)
    pieces = [chip_mid] + [swap(chip_mid, "ctx", s, n_ctx) for s in chip_steps]
    mid = sum(p.astype(jnp.float32) for p in pieces).astype(jnp.bfloat16)
    if mid.shape[1] % LANES == 0:
        blocks = [mid] + [swap(mid, "req", s, n_req) for s in req_steps]
    else:
        blocks = [lax.all_gather(mid, "req", axis=1, tiled=True)]

    partial_sum, kept = experts(
        blocks,
        norm_gain.reshape(1, -1),
        routes.T,
        route_weight.T,
        w_gate,
        w_up,
        w_down,
        n_req,
        n_ctx,
    )
    tokens = mid.shape[0]
    model_width = w_gate.shape[2]
    rows_out = tokens // n_req
    slice_width = model_width // n_ctx
    if partial_sum.ndim == 2:
        partial_sum = partial_sum.reshape(n_req, rows_out, n_ctx, slice_width)
        partial_sum = jnp.swapaxes(partial_sum, 1, 2)
        kept = lax.dynamic_slice(
            kept,
            (lax.axis_index("req") * rows_out, lax.axis_index("ctx") * slice_width),
            (rows_out, slice_width),
        )
    partial_sum = partial_sum.reshape(n_req * n_ctx, rows_out, slice_width)
    landed = lax.all_to_all(partial_sum, ("req", "ctx"), split_axis=0, concat_axis=0, tiled=True)
    return (kept + jnp.sum(landed.astype(jnp.float32), axis=0)).astype(jnp.bfloat16)


def solution(mesh):
    in_specs = (
        P("ctx", "req"),
        P("req", "ctx", None),
        P("req", "ctx", None),
        P("req"),
        P("ctx", None, None),
        P("ctx", "req"),
        P(),
        P(),
        P(),
        P("req", "ctx", None),
        P("req", "ctx", None),
        P("req", "ctx", None),
    )
    out_specs = P("req", "ctx")
    return jax.shard_map(local, mesh=mesh, in_specs=in_specs, out_specs=out_specs, check_vma=False)
```

```python
import functools

import jax
import jax.numpy as jnp
from jax import lax
from jax.experimental import pallas as pl
from jax.experimental.pallas import tpu as pltpu
from jax.sharding import PartitionSpec as P

SOFTMAX_SCALE = 192.0 ** (-0.5)
NEG_FILL = -1e30
NORM_EPS = 1e-06
CORES = 2
OVERLAP = 60
LANES = 128
MIB = 1 << 20
NT = (((1,), (1,)), ((), ()))
VMEM = pl.BlockSpec(memory_space=pltpu.VMEM)
HBM = pl.BlockSpec(memory_space=pltpu.HBM)


def swap(x, axis, step, size):
    return lax.ppermute(x, axis, [(i, i ^ step) for i in range(size)])


def stack_rows(blocks):
    if len(blocks) == 1:
        return blocks[0]
    if all(b.shape[0] % 16 == 0 for b in blocks):
        return jnp.concatenate(blocks, axis=0)
    return jnp.concatenate([b.astype(jnp.float32) for b in blocks], axis=0).astype(blocks[0].dtype)


def attend_kernel(n_blocks, q_tokens, width, lengths, *refs):
    queries, caches, outs = refs[:n_blocks], refs[n_blocks : n_blocks + 2], refs[n_blocks + 2 :]
    req_local, rows, _ = queries[0].shape
    ctx_local = caches[0].shape[2]
    total_rows = n_blocks * rows
    heads_local = rows // q_tokens
    row = lax.broadcasted_iota(jnp.int32, (total_rows, ctx_local), 0)
    column = lax.broadcasted_iota(jnp.int32, (total_rows, ctx_local), 1)
    token = (row // heads_local) % q_tokens
    lane = lax.broadcasted_iota(jnp.int32, (total_rows, LANES), 1)
    for r in range(req_local):
        grouped = stack_rows([q[r] for q in queries])
        limit = lengths[:, r : r + 1] - q_tokens + token
        masked = []
        for half, cache in enumerate(caches):
            score = jnp.dot(grouped, cache[r], preferred_element_type=jnp.float32)
            visible = column + (lax.axis_index("ctx") ^ half) * ctx_local <= limit
            masked.append(jnp.where(visible, score * SOFTMAX_SCALE, -jnp.inf))
        peak = jnp.maximum(
            jnp.max(masked[0], axis=-1, keepdims=True), jnp.max(masked[1], axis=-1, keepdims=True)
        )
        peak = jnp.where(peak > -jnp.inf, peak, 0.0)
        total = jnp.zeros((total_rows, 1), jnp.float32)
        mixed = jnp.zeros((total_rows, width), jnp.float32)
        for scores, cache in zip(masked, caches):
            raised = jnp.exp(scores - peak)
            total += jnp.sum(raised, axis=-1, keepdims=True)
            mixed += lax.dot_general(
                raised.astype(jnp.bfloat16),
                cache[r, :width, :],
                NT,
                preferred_element_type=jnp.float32,
            )
        filled = total > 0.0
        safe = jnp.where(filled, total, 1.0)
        mean = jnp.where(filled, mixed / safe, 0.0).astype(jnp.bfloat16)
        log = jnp.where(filled, peak + jnp.log(safe), NEG_FILL)
        high = log.astype(jnp.bfloat16).astype(jnp.float32)
        tail = jnp.where(lane == 0, high, jnp.where(lane == 1, log - high, 0.0))
        tail = tail.astype(jnp.bfloat16)
        for s, out in enumerate(outs):
            out[r, :, :width] = mean[s * rows : (s + 1) * rows]
            out[r, :, width:] = tail[s * rows : (s + 1) * rows]


def attend(blocks, caches, lengths, width, q_tokens):
    req_local, rows, lat = blocks[0].shape
    n = len(blocks)
    ctx_local = caches[0].shape[2]
    shape = jax.ShapeDtypeStruct((req_local, rows, width + LANES), jnp.bfloat16)
    return pl.pallas_call(
        functools.partial(attend_kernel, n, q_tokens, width),
        out_shape=[shape] * n,
        in_specs=[VMEM] * (n + 3),
        out_specs=[VMEM] * n,
        compiler_params=pltpu.CompilerParams(vmem_limit_bytes=4 * MIB),
        cost_estimate=pl.CostEstimate(
            flops=OVERLAP * 4 * req_local * n * rows * ctx_local * (lat + width),
            bytes_accessed=4 * req_local * ctx_local * lat,
            transcendentals=2 * req_local * n * rows * ctx_local,
        ),
        name="attend",
    )(lengths.reshape(1, -1), *blocks, *caches)


def stage_kernel(*refs):
    n = len(refs) // 2
    sems = refs[-1]
    copies = [
        pltpu.make_async_copy(source, target, sems.at[i])
        for i, (source, target) in enumerate(zip(refs[:n], refs[n : 2 * n]))
    ]
    for copy in copies:
        copy.start()
    for copy in copies:
        copy.wait()


def stage(arrays):
    return pl.pallas_call(
        stage_kernel,
        out_shape=[pltpu.VMEM(x.shape, x.dtype) for x in arrays],
        in_specs=[HBM] * len(arrays),
        out_specs=[VMEM] * len(arrays),
        scratch_shapes=[pltpu.SemaphoreType.DMA((len(arrays),))],
        compiler_params=pltpu.CompilerParams(vmem_limit_bytes=4 * MIB),
        cost_estimate=pl.CostEstimate(
            flops=0, bytes_accessed=sum(x.size * 2 for x in arrays), transcendentals=0
        ),
        name="stage",
    )(*[pltpu.with_memory_space_constraint(x, pltpu.HBM) for x in arrays])


def combine_kernel(n_blocks, q_tokens, *refs):
    blocks, (w_uv, out) = refs[:n_blocks], refs[n_blocks:]
    heads, width, value_width = w_uv.shape
    req_local, rows, _ = blocks[0].shape
    total_rows = req_local * rows
    parts = [b[...].astype(jnp.float32).reshape(total_rows, -1) for b in blocks]
    logs = [p[:, width : width + 1] + p[:, width + 1 : width + 2] for p in parts]
    top = functools.reduce(jnp.maximum, logs)
    factors = [jnp.exp(log - top) for log in logs]
    numer = sum(f * p[:, :width] for f, p in zip(factors, parts))
    latent = (numer / sum(factors)).astype(jnp.bfloat16)
    head = lax.broadcasted_iota(jnp.int32, (total_rows, value_width), 0) % heads
    values = []
    for h in range(heads):
        value = jnp.dot(latent, w_uv[h], preferred_element_type=jnp.float32)
        values.append(jnp.where(head == h, value, 0.0).astype(jnp.bfloat16))
    values = jnp.concatenate(values, axis=1)
    tokens = req_local * q_tokens
    token = lax.broadcasted_iota(jnp.int32, (tokens, total_rows), 0)
    at = lax.broadcasted_iota(jnp.int32, (tokens, total_rows), 1)
    fold = jnp.where(at // heads == token, 1.0, 0.0).astype(jnp.bfloat16)
    out[...] = jnp.dot(fold, values, preferred_element_type=jnp.float32).astype(out.dtype)


def combine(blocks, w_uv, q_tokens):
    heads, width, value_width = w_uv.shape
    req_local, rows, _ = blocks[0].shape
    tokens = req_local * q_tokens
    return pl.pallas_call(
        functools.partial(combine_kernel, len(blocks), q_tokens),
        out_shape=jax.ShapeDtypeStruct((tokens, heads * value_width), jnp.bfloat16),
        in_specs=[VMEM] * (len(blocks) + 1),
        out_specs=VMEM,
        compiler_params=pltpu.CompilerParams(vmem_limit_bytes=4 * MIB),
        cost_estimate=pl.CostEstimate(
            flops=2 * req_local * rows * w_uv.size, bytes_accessed=2 * w_uv.size, transcendentals=0
        ),
        name="combine",
    )(*blocks, w_uv)


def one_hot(shape, target):
    at = lax.broadcasted_iota(jnp.int32, shape, 1)
    return jnp.where(at == target(lax.broadcasted_iota(jnp.int32, shape, 0)), 1.0, 0.0).astype(
        jnp.bfloat16
    )


def out_proj_kernel(n_blocks, *refs):
    blocks, (w_o, residual, out) = refs[:n_blocks], refs[n_blocks:]
    per = blocks[0].shape[0]
    tokens = n_blocks * per
    stacked = stack_rows([b[...] for b in blocks])
    at_ctx, at_req = lax.axis_index("ctx"), lax.axis_index("req")
    order = one_hot((tokens, tokens), lambda row: (row // per ^ at_req) * per + row % per)
    ordered = jnp.dot(order, stacked, preferred_element_type=jnp.float32).astype(jnp.bfloat16)
    total = jnp.dot(ordered, w_o[...], preferred_element_type=jnp.float32)
    own = residual.shape[0]
    row = lax.broadcasted_iota(jnp.int32, total.shape, 0) - at_ctx * own
    rows = residual[...].astype(jnp.float32)
    for i in range(own):
        total += jnp.where(row == i, rows[i : i + 1], 0.0)
    out[...] = total.astype(out.dtype)


def out_proj(blocks, w_o, residual):
    n = len(blocks)
    tokens = n * blocks[0].shape[0]
    return pl.pallas_call(
        functools.partial(out_proj_kernel, n),
        out_shape=jax.ShapeDtypeStruct((tokens, w_o.shape[1]), jnp.bfloat16),
        in_specs=[VMEM] * (n + 2),
        out_specs=VMEM,
        compiler_params=pltpu.CompilerParams(vmem_limit_bytes=4 * MIB),
        cost_estimate=pl.CostEstimate(
            flops=2 * tokens * w_o.size, bytes_accessed=2 * w_o.size, transcendentals=0
        ),
        name="out_proj",
    )(*blocks, w_o, residual)


def add_products(totals, steps, blocks, gain, gate, up):
    n_exp = gate.shape[0]
    width = blocks[0].shape[1]
    for step, block in zip(steps, blocks):
        columns = pl.ds(0, width)
        if width < gate.shape[2]:
            columns = pl.ds(pl.multiple_of((lax.axis_index("req") ^ step) * width, LANES), width)
        rows = block[...].astype(jnp.float32) * gain[:, columns].astype(jnp.float32)
        rows = rows.astype(jnp.bfloat16)
        for m, weights in enumerate((gate, up)):
            for e in range(n_exp):
                product = lax.dot_general(
                    weights[e, :, columns], rows, NT, preferred_element_type=jnp.float32
                )
                at = m * n_exp + e
                totals[at] = product if totals[at] is None else totals[at] + product
    return totals


def part_kernel(steps, block, gain, gate, up, out):
    totals = add_products([None] * out.shape[0], steps, [block], gain, gate, up)
    for at, total in enumerate(totals):
        out[at] = total


def part(step, block, gain, w_gate, w_up):
    n_exp, units, _ = w_gate.shape
    tokens, width = block.shape
    return pl.pallas_call(
        functools.partial(part_kernel, [step]),
        out_shape=pltpu.VMEM((2 * n_exp, units, tokens), jnp.float32),
        in_specs=[VMEM] * 4,
        out_specs=VMEM,
        compiler_params=pltpu.CompilerParams(vmem_limit_bytes=4 * MIB),
        cost_estimate=pl.CostEstimate(
            flops=4 * tokens * n_exp * units * width,
            bytes_accessed=4 * n_exp * units * width,
            transcendentals=0,
        ),
        name="part",
    )(block, gain, w_gate, w_up)


def experts_kernel(n_blocks, n_parts, *refs):
    blocks, refs = refs[:n_blocks], refs[n_blocks:]
    parts, refs = refs[:n_parts], refs[n_parts:]
    gain, routes, weights, gate, up, down, out, kept, rows, hidden = refs
    at_ctx, at_req = lax.axis_index("ctx"), lax.axis_index("req")
    n_exp, units, model = gate.shape
    tokens = rows.shape[0]
    width = blocks[0].shape[1]
    steps = range(n_parts, n_blocks)
    totals = [None] * (2 * n_exp)
    for done in parts:
        totals = [done[at] if t is None else t + done[at] for at, t in enumerate(totals)]
    totals = add_products(totals, steps, blocks[n_parts:], gain, gate, up)
    totals = [t.T for t in totals]
    for s, block in enumerate(blocks):
        if n_blocks == 1:
            rows[...] = block[...]
        else:
            offset = pl.multiple_of((at_req ^ s) * width, LANES)
            rows[:, pl.ds(offset, width)] = block[...]
    squares = sum(
        jnp.sum(jnp.square(b[...].astype(jnp.float32)), axis=-1, keepdims=True) for b in blocks
    )
    scale = lax.rsqrt(squares / model + NORM_EPS)
    eye = lax.broadcasted_iota(jnp.int32, (tokens, tokens), 0) == lax.broadcasted_iota(
        jnp.int32, (tokens, tokens), 1
    )
    for e in range(n_exp):
        named = jnp.where(routes[...] == at_req * n_exp + e, weights[...], 0.0)
        coef = jnp.sum(named, axis=0, keepdims=True)
        coef = jnp.sum(jnp.where(eye, coef, 0.0), axis=1, keepdims=True)
        active = jax.nn.silu(totals[e] * scale) * (totals[n_exp + e] * scale) * coef
        hidden[:, e * units : (e + 1) * units] = active.astype(jnp.bfloat16)
    sliced = len(out.shape) == 4
    if sliced:
        n_chunks, per, chunk = out.shape[1:]
        columns = pl.ds(pl.multiple_of(at_ctx * chunk, LANES), chunk)
        own = one_hot((per, tokens), lambda row: row + at_req * per)
        kept[...] = jnp.dot(own, rows[:, columns], preferred_element_type=jnp.float32)
    else:
        n_chunks, chunk = 8, model // 8
        kept[...] = rows[...].astype(jnp.float32)
    held = hidden[...]
    for j in range(n_chunks):
        columns = slice(j * chunk, (j + 1) * chunk)
        part_down = down[:, :, columns].reshape(n_exp * units, chunk)
        total = jnp.dot(held, part_down, preferred_element_type=jnp.float32).astype(out.dtype)
        if sliced:
            for q in range(out.shape[0]):
                out[q, j] = total[q * per : (q + 1) * per]
        else:
            out[:, columns] = total


def experts(blocks, gain, routes, route_weight, w_gate, w_up, w_down, n_req, n_ctx):
    n_exp, units, model = w_gate.shape
    tokens = blocks[0].shape[0]
    slice_width = model // n_ctx
    aligned = slice_width % LANES == 0
    w_gate, w_up, w_down = [
        pltpu.with_memory_space_constraint(w, pltpu.VMEM) for w in (w_gate, w_up, w_down)
    ]
    parts = []
    if len(blocks) > 2:
        parts = [part(s, blocks[s], gain, w_gate, w_up) for s in range(2)]
    shape = (n_req, n_ctx, tokens // n_req, slice_width) if aligned else (tokens, model)
    kept = (tokens // n_req, slice_width) if aligned else (tokens, model)
    return pl.pallas_call(
        functools.partial(experts_kernel, len(blocks), len(parts)),
        out_shape=[
            jax.ShapeDtypeStruct(shape, jnp.bfloat16),
            jax.ShapeDtypeStruct(kept, jnp.float32),
        ],
        in_specs=[VMEM] * (len(blocks) + len(parts) + 6),
        out_specs=[VMEM, VMEM],
        scratch_shapes=[
            pltpu.VMEM((tokens, model), jnp.bfloat16),
            pltpu.VMEM((tokens, n_exp * units), jnp.bfloat16),
        ],
        compiler_params=pltpu.CompilerParams(vmem_limit_bytes=4 * MIB),
        cost_estimate=pl.CostEstimate(
            flops=6 * tokens * w_gate.size,
            bytes_accessed=6 * w_gate.size,
            transcendentals=n_exp * units * tokens,
        ),
        name="experts",
    )(*blocks, *parts, gain, routes, route_weight, w_gate, w_up, w_down)


def local(
    residual,
    query,
    latent_cache,
    lengths,
    w_uv,
    w_o,
    norm_gain,
    routes,
    route_weight,
    w_gate,
    w_up,
    w_down,
):
    n_ctx = lax.axis_size("ctx")
    n_req = lax.axis_size("req")
    chip_steps = range(CORES, n_ctx, CORES)
    req_steps = range(1, n_req)
    req_local = latent_cache.shape[0]
    heads_local, lat_width, _ = w_uv.shape
    tok_local = query.shape[0]
    q_tokens = tok_local // req_local

    cache = jnp.swapaxes(latent_cache, 1, 2)
    other_cache = swap(cache, "ctx", 1, n_ctx)
    query = query.reshape(req_local, q_tokens * heads_local, query.shape[2])
    received = [swap(query, "ctx", s, n_ctx) for s in chip_steps]
    cache, query, w_uv, w_o = stage([cache, query, w_uv, w_o])
    blocks = [query] + received
    outs = attend(blocks, (cache, other_cache), lengths, lat_width, q_tokens)
    outs = [outs[0]] + [swap(o, "ctx", s, n_ctx) for o, s in zip(outs[1:], chip_steps)]

    head_values = combine(outs, w_uv, q_tokens)
    blocks = [head_values] + [swap(head_values, "req", s, n_req) for s in req_steps]
    partial_mid = out_proj(blocks, w_o, residual)

    other = swap(partial_mid, "ctx", 1, n_ctx)
    chip_mid = (partial_mid.astype(jnp.float32) + other.astype(jnp.float32)).astype(jnp.bfloat16)
    pieces = [chip_mid] + [swap(chip_mid, "ctx", s, n_ctx) for s in chip_steps]
    mid = sum(p.astype(jnp.float32) for p in pieces).astype(jnp.bfloat16)
    if mid.shape[1] % LANES == 0:
        blocks = [mid] + [swap(mid, "req", s, n_req) for s in req_steps]
    else:
        blocks = [lax.all_gather(mid, "req", axis=1, tiled=True)]

    partial_sum, kept = experts(
        blocks,
        norm_gain.reshape(1, -1),
        routes.T,
        route_weight.T,
        w_gate,
        w_up,
        w_down,
        n_req,
        n_ctx,
    )
    tokens = mid.shape[0]
    model_width = w_gate.shape[2]
    rows_out = tokens // n_req
    slice_width = model_width // n_ctx
    if partial_sum.ndim == 2:
        partial_sum = partial_sum.reshape(n_req, rows_out, n_ctx, slice_width)
        partial_sum = jnp.swapaxes(partial_sum, 1, 2)
        kept = lax.dynamic_slice(
            kept,
            (lax.axis_index("req") * rows_out, lax.axis_index("ctx") * slice_width),
            (rows_out, slice_width),
        )
    partial_sum = partial_sum.reshape(n_req * n_ctx, rows_out, slice_width)
    landed = lax.all_to_all(partial_sum, ("req", "ctx"), split_axis=0, concat_axis=0, tiled=True)
    return (kept + jnp.sum(landed.astype(jnp.float32), axis=0)).astype(jnp.bfloat16)


def solution(mesh):
    in_specs = (
        P("ctx", "req"),
        P("req", "ctx", None),
        P("req", "ctx", None),
        P("req"),
        P("ctx", None, None),
        P("ctx", "req"),
        P(),
        P(),
        P(),
        P("req", "ctx", None),
        P("req", "ctx", None),
        P("req", "ctx", None),
    )
    out_specs = P("req", "ctx")
    return jax.shard_map(local, mesh=mesh, in_specs=in_specs, out_specs=out_specs, check_vma=False)
```

```python
import functools

import jax
import jax.numpy as jnp
from jax import lax
from jax.experimental import pallas as pl
from jax.experimental.pallas import tpu as pltpu
from jax.sharding import PartitionSpec as P

SOFTMAX_SCALE = 192.0 ** (-0.5)
NEG_FILL = -1e30
NORM_EPS = 1e-06
CORES = 2
OVERLAP = 60
LANES = 128
MIB = 1 << 20
NT = (((1,), (1,)), ((), ()))
VMEM = pl.BlockSpec(memory_space=pltpu.VMEM)
HBM = pl.BlockSpec(memory_space=pltpu.HBM)


def swap(x, axis, step, size):
    return lax.ppermute(x, axis, [(i, i ^ step) for i in range(size)])


def stack_rows(blocks):
    if len(blocks) == 1:
        return blocks[0]
    if all(b.shape[0] % 16 == 0 for b in blocks):
        return jnp.concatenate(blocks, axis=0)
    return jnp.concatenate([b.astype(jnp.float32) for b in blocks], axis=0).astype(blocks[0].dtype)


def attend_kernel(n_blocks, q_tokens, width, lengths, *refs):
    queries, caches, outs = refs[:n_blocks], refs[n_blocks : n_blocks + 2], refs[n_blocks + 2 :]
    req_local, rows, _ = queries[0].shape
    ctx_local = caches[0].shape[2]
    total_rows = n_blocks * rows
    heads_local = rows // q_tokens
    row = lax.broadcasted_iota(jnp.int32, (total_rows, ctx_local), 0)
    column = lax.broadcasted_iota(jnp.int32, (total_rows, ctx_local), 1)
    token = (row // heads_local) % q_tokens
    lane = lax.broadcasted_iota(jnp.int32, (total_rows, LANES), 1)
    for r in range(req_local):
        grouped = stack_rows([q[r] for q in queries])
        limit = lengths[:, r : r + 1] - q_tokens + token
        masked = []
        for half, cache in enumerate(caches):
            score = jnp.dot(grouped, cache[r], preferred_element_type=jnp.float32)
            visible = column + (lax.axis_index("ctx") ^ half) * ctx_local <= limit
            masked.append(jnp.where(visible, score * SOFTMAX_SCALE, -jnp.inf))
        peak = jnp.maximum(
            jnp.max(masked[0], axis=-1, keepdims=True), jnp.max(masked[1], axis=-1, keepdims=True)
        )
        peak = jnp.where(peak > -jnp.inf, peak, 0.0)
        total = jnp.zeros((total_rows, 1), jnp.float32)
        mixed = jnp.zeros((total_rows, width), jnp.float32)
        for scores, cache in zip(masked, caches):
            raised = jnp.exp(scores - peak)
            total += jnp.sum(raised, axis=-1, keepdims=True)
            mixed += lax.dot_general(
                raised.astype(jnp.bfloat16),
                cache[r, :width, :],
                NT,
                preferred_element_type=jnp.float32,
            )
        filled = total > 0.0
        safe = jnp.where(filled, total, 1.0)
        mean = jnp.where(filled, mixed / safe, 0.0).astype(jnp.bfloat16)
        log = jnp.where(filled, peak + jnp.log(safe), NEG_FILL)
        high = log.astype(jnp.bfloat16).astype(jnp.float32)
        tail = jnp.where(lane == 0, high, jnp.where(lane == 1, log - high, 0.0))
        tail = tail.astype(jnp.bfloat16)
        for s, out in enumerate(outs):
            out[r, :, :width] = mean[s * rows : (s + 1) * rows]
            out[r, :, width:] = tail[s * rows : (s + 1) * rows]


def attend(blocks, caches, lengths, width, q_tokens):
    req_local, rows, lat = blocks[0].shape
    n = len(blocks)
    ctx_local = caches[0].shape[2]
    shape = jax.ShapeDtypeStruct((req_local, rows, width + LANES), jnp.bfloat16)
    return pl.pallas_call(
        functools.partial(attend_kernel, n, q_tokens, width),
        out_shape=[shape] * n,
        in_specs=[VMEM] * (n + 3),
        out_specs=[VMEM] * n,
        compiler_params=pltpu.CompilerParams(vmem_limit_bytes=4 * MIB),
        cost_estimate=pl.CostEstimate(
            flops=OVERLAP * 4 * req_local * n * rows * ctx_local * (lat + width),
            bytes_accessed=4 * req_local * ctx_local * lat,
            transcendentals=2 * req_local * n * rows * ctx_local,
        ),
        name="attend",
    )(lengths.reshape(1, -1), *blocks, *caches)


def stage_kernel(*refs):
    n = len(refs) // 2
    sems = refs[-1]
    copies = [
        pltpu.make_async_copy(source, target, sems.at[i])
        for i, (source, target) in enumerate(zip(refs[:n], refs[n : 2 * n]))
    ]
    for copy in copies:
        copy.start()
    for copy in copies:
        copy.wait()


def stage(arrays):
    return pl.pallas_call(
        stage_kernel,
        out_shape=[pltpu.VMEM(x.shape, x.dtype) for x in arrays],
        in_specs=[HBM] * len(arrays),
        out_specs=[VMEM] * len(arrays),
        scratch_shapes=[pltpu.SemaphoreType.DMA((len(arrays),))],
        compiler_params=pltpu.CompilerParams(vmem_limit_bytes=4 * MIB),
        cost_estimate=pl.CostEstimate(
            flops=0, bytes_accessed=sum(x.size * 2 for x in arrays), transcendentals=0
        ),
        name="stage",
    )(*[pltpu.with_memory_space_constraint(x, pltpu.HBM) for x in arrays])


def combine_kernel(n_blocks, q_tokens, *refs):
    blocks, (w_uv, out) = refs[:n_blocks], refs[n_blocks:]
    heads, width, value_width = w_uv.shape
    req_local, rows, _ = blocks[0].shape
    total_rows = req_local * rows
    parts = [b[...].astype(jnp.float32).reshape(total_rows, -1) for b in blocks]
    logs = [p[:, width : width + 1] + p[:, width + 1 : width + 2] for p in parts]
    top = functools.reduce(jnp.maximum, logs)
    factors = [jnp.exp(log - top) for log in logs]
    numer = sum(f * p[:, :width] for f, p in zip(factors, parts))
    latent = (numer / sum(factors)).astype(jnp.bfloat16)
    head = lax.broadcasted_iota(jnp.int32, (total_rows, value_width), 0) % heads
    values = []
    for h in range(heads):
        value = jnp.dot(latent, w_uv[h], preferred_element_type=jnp.float32)
        values.append(jnp.where(head == h, value, 0.0).astype(jnp.bfloat16))
    values = jnp.concatenate(values, axis=1)
    tokens = req_local * q_tokens
    token = lax.broadcasted_iota(jnp.int32, (tokens, total_rows), 0)
    at = lax.broadcasted_iota(jnp.int32, (tokens, total_rows), 1)
    fold = jnp.where(at // heads == token, 1.0, 0.0).astype(jnp.bfloat16)
    out[...] = jnp.dot(fold, values, preferred_element_type=jnp.float32).astype(out.dtype)


def combine(blocks, w_uv, q_tokens):
    heads, width, value_width = w_uv.shape
    req_local, rows, _ = blocks[0].shape
    tokens = req_local * q_tokens
    return pl.pallas_call(
        functools.partial(combine_kernel, len(blocks), q_tokens),
        out_shape=jax.ShapeDtypeStruct((tokens, heads * value_width), jnp.bfloat16),
        in_specs=[VMEM] * (len(blocks) + 1),
        out_specs=VMEM,
        compiler_params=pltpu.CompilerParams(vmem_limit_bytes=4 * MIB),
        cost_estimate=pl.CostEstimate(
            flops=2 * req_local * rows * w_uv.size, bytes_accessed=2 * w_uv.size, transcendentals=0
        ),
        name="combine",
    )(*blocks, w_uv)


def one_hot(shape, target):
    at = lax.broadcasted_iota(jnp.int32, shape, 1)
    return jnp.where(at == target(lax.broadcasted_iota(jnp.int32, shape, 0)), 1.0, 0.0).astype(
        jnp.bfloat16
    )


def out_proj_kernel(n_blocks, *refs):
    blocks, (w_o, residual, out) = refs[:n_blocks], refs[n_blocks:]
    per = blocks[0].shape[0]
    tokens = n_blocks * per
    stacked = stack_rows([b[...] for b in blocks])
    at_ctx, at_req = lax.axis_index("ctx"), lax.axis_index("req")
    order = one_hot((tokens, tokens), lambda row: (row // per ^ at_req) * per + row % per)
    ordered = jnp.dot(order, stacked, preferred_element_type=jnp.float32).astype(jnp.bfloat16)
    total = jnp.dot(ordered, w_o[...], preferred_element_type=jnp.float32)
    own = residual.shape[0]
    row = lax.broadcasted_iota(jnp.int32, total.shape, 0) - at_ctx * own
    rows = residual[...].astype(jnp.float32)
    for i in range(own):
        total += jnp.where(row == i, rows[i : i + 1], 0.0)
    out[...] = total.astype(out.dtype)


def out_proj(blocks, w_o, residual):
    n = len(blocks)
    tokens = n * blocks[0].shape[0]
    return pl.pallas_call(
        functools.partial(out_proj_kernel, n),
        out_shape=jax.ShapeDtypeStruct((tokens, w_o.shape[1]), jnp.bfloat16),
        in_specs=[VMEM] * (n + 2),
        out_specs=VMEM,
        compiler_params=pltpu.CompilerParams(vmem_limit_bytes=4 * MIB),
        cost_estimate=pl.CostEstimate(
            flops=2 * tokens * w_o.size, bytes_accessed=2 * w_o.size, transcendentals=0
        ),
        name="out_proj",
    )(*blocks, w_o, residual)


def add_products(totals, steps, blocks, gain, gate, up):
    n_exp = gate.shape[0]
    width = blocks[0].shape[1]
    for step, block in zip(steps, blocks):
        columns = pl.ds(0, width)
        if width < gate.shape[2]:
            columns = pl.ds(pl.multiple_of((lax.axis_index("req") ^ step) * width, LANES), width)
        rows = block[...].astype(jnp.float32) * gain[:, columns].astype(jnp.float32)
        rows = rows.astype(jnp.bfloat16)
        for m, weights in enumerate((gate, up)):
            for e in range(n_exp):
                product = lax.dot_general(
                    weights[e, :, columns], rows, NT, preferred_element_type=jnp.float32
                )
                at = m * n_exp + e
                totals[at] = product if totals[at] is None else totals[at] + product
    return totals


def part_kernel(steps, block, gain, gate, up, *refs):
    out = refs[-1]
    totals = add_products([None] * out.shape[0], steps, [block], gain, gate, up)
    for at, total in enumerate(totals):
        out[at] = total


def part(step, block, gain, w_gate, w_up, *held):
    n_exp, units, _ = w_gate.shape
    tokens, width = block.shape
    return pl.pallas_call(
        functools.partial(part_kernel, [step]),
        out_shape=pltpu.VMEM((2 * n_exp, units, tokens), jnp.float32),
        in_specs=[VMEM] * (4 + len(held)),
        out_specs=VMEM,
        compiler_params=pltpu.CompilerParams(vmem_limit_bytes=4 * MIB),
        cost_estimate=pl.CostEstimate(
            flops=4 * tokens * n_exp * units * width,
            bytes_accessed=4 * n_exp * units * width,
            transcendentals=0,
        ),
        name="part",
    )(block, gain, w_gate, w_up, *held)


def experts_kernel(n_blocks, n_parts, *refs):
    blocks, refs = refs[:n_blocks], refs[n_blocks:]
    parts, refs = refs[:n_parts], refs[n_parts:]
    gain, routes, weights, gate, up, down, out, kept, rows, hidden = refs
    at_ctx, at_req = lax.axis_index("ctx"), lax.axis_index("req")
    n_exp, units, model = gate.shape
    tokens = rows.shape[0]
    width = blocks[0].shape[1]
    steps = range(n_parts, n_blocks)
    totals = [None] * (2 * n_exp)
    for done in parts:
        totals = [done[at] if t is None else t + done[at] for at, t in enumerate(totals)]
    totals = add_products(totals, steps, blocks[n_parts:], gain, gate, up)
    totals = [t.T for t in totals]
    for s, block in enumerate(blocks):
        if n_blocks == 1:
            rows[...] = block[...]
        else:
            offset = pl.multiple_of((at_req ^ s) * width, LANES)
            rows[:, pl.ds(offset, width)] = block[...]
    squares = sum(
        jnp.sum(jnp.square(b[...].astype(jnp.float32)), axis=-1, keepdims=True) for b in blocks
    )
    scale = lax.rsqrt(squares / model + NORM_EPS)
    eye = lax.broadcasted_iota(jnp.int32, (tokens, tokens), 0) == lax.broadcasted_iota(
        jnp.int32, (tokens, tokens), 1
    )
    for e in range(n_exp):
        named = jnp.where(routes[...] == at_req * n_exp + e, weights[...], 0.0)
        coef = jnp.sum(named, axis=0, keepdims=True)
        coef = jnp.sum(jnp.where(eye, coef, 0.0), axis=1, keepdims=True)
        active = jax.nn.silu(totals[e] * scale) * (totals[n_exp + e] * scale) * coef
        hidden[:, e * units : (e + 1) * units] = active.astype(jnp.bfloat16)
    sliced = len(out.shape) == 4
    if sliced:
        n_chunks, per, chunk = out.shape[1:]
        columns = pl.ds(pl.multiple_of(at_ctx * chunk, LANES), chunk)
        own = one_hot((per, tokens), lambda row: row + at_req * per)
        kept[...] = jnp.dot(own, rows[:, columns], preferred_element_type=jnp.float32)
    else:
        n_chunks, chunk = 8, model // 8
        kept[...] = rows[...].astype(jnp.float32)
    held = hidden[...]
    for j in range(n_chunks):
        columns = slice(j * chunk, (j + 1) * chunk)
        part_down = down[:, :, columns].reshape(n_exp * units, chunk)
        total = jnp.dot(held, part_down, preferred_element_type=jnp.float32).astype(out.dtype)
        if sliced:
            for q in range(out.shape[0]):
                out[q, j] = total[q * per : (q + 1) * per]
        else:
            out[:, columns] = total


def experts(blocks, gain, routes, route_weight, w_gate, w_up, w_down, n_req, n_ctx):
    n_exp, units, model = w_gate.shape
    tokens = blocks[0].shape[0]
    slice_width = model // n_ctx
    aligned = slice_width % LANES == 0
    w_gate, w_up, w_down = [
        pltpu.with_memory_space_constraint(w, pltpu.VMEM) for w in (w_gate, w_up, w_down)
    ]
    parts = []
    if len(blocks) > 2:
        parts = [part(s, blocks[s], gain, w_gate, w_up, w_down) for s in range(2)]
    shape = (n_req, n_ctx, tokens // n_req, slice_width) if aligned else (tokens, model)
    kept = (tokens // n_req, slice_width) if aligned else (tokens, model)
    return pl.pallas_call(
        functools.partial(experts_kernel, len(blocks), len(parts)),
        out_shape=[
            jax.ShapeDtypeStruct(shape, jnp.bfloat16),
            jax.ShapeDtypeStruct(kept, jnp.float32),
        ],
        in_specs=[VMEM] * (len(blocks) + len(parts) + 6),
        out_specs=[VMEM, VMEM],
        scratch_shapes=[
            pltpu.VMEM((tokens, model), jnp.bfloat16),
            pltpu.VMEM((tokens, n_exp * units), jnp.bfloat16),
        ],
        compiler_params=pltpu.CompilerParams(vmem_limit_bytes=4 * MIB),
        cost_estimate=pl.CostEstimate(
            flops=6 * tokens * w_gate.size,
            bytes_accessed=6 * w_gate.size,
            transcendentals=n_exp * units * tokens,
        ),
        name="experts",
    )(*blocks, *parts, gain, routes, route_weight, w_gate, w_up, w_down)


def local(
    residual,
    query,
    latent_cache,
    lengths,
    w_uv,
    w_o,
    norm_gain,
    routes,
    route_weight,
    w_gate,
    w_up,
    w_down,
):
    n_ctx = lax.axis_size("ctx")
    n_req = lax.axis_size("req")
    chip_steps = range(CORES, n_ctx, CORES)
    req_steps = range(1, n_req)
    req_local = latent_cache.shape[0]
    heads_local, lat_width, _ = w_uv.shape
    tok_local = query.shape[0]
    q_tokens = tok_local // req_local

    cache = jnp.swapaxes(latent_cache, 1, 2)
    other_cache = swap(cache, "ctx", 1, n_ctx)
    query = query.reshape(req_local, q_tokens * heads_local, query.shape[2])
    received = [swap(query, "ctx", s, n_ctx) for s in chip_steps]
    cache, query, w_uv, w_o = stage([cache, query, w_uv, w_o])
    blocks = [query] + received
    outs = attend(blocks, (cache, other_cache), lengths, lat_width, q_tokens)
    outs = [outs[0]] + [swap(o, "ctx", s, n_ctx) for o, s in zip(outs[1:], chip_steps)]

    head_values = combine(outs, w_uv, q_tokens)
    blocks = [head_values] + [swap(head_values, "req", s, n_req) for s in req_steps]
    partial_mid = out_proj(blocks, w_o, residual)

    other = swap(partial_mid, "ctx", 1, n_ctx)
    chip_mid = (partial_mid.astype(jnp.float32) + other.astype(jnp.float32)).astype(jnp.bfloat16)
    pieces = [chip_mid] + [swap(chip_mid, "ctx", s, n_ctx) for s in chip_steps]
    mid = sum(p.astype(jnp.float32) for p in pieces).astype(jnp.bfloat16)
    if mid.shape[1] % LANES == 0:
        blocks = [mid] + [swap(mid, "req", s, n_req) for s in req_steps]
    else:
        blocks = [lax.all_gather(mid, "req", axis=1, tiled=True)]

    partial_sum, kept = experts(
        blocks,
        norm_gain.reshape(1, -1),
        routes.T,
        route_weight.T,
        w_gate,
        w_up,
        w_down,
        n_req,
        n_ctx,
    )
    tokens = mid.shape[0]
    model_width = w_gate.shape[2]
    rows_out = tokens // n_req
    slice_width = model_width // n_ctx
    if partial_sum.ndim == 2:
        partial_sum = partial_sum.reshape(n_req, rows_out, n_ctx, slice_width)
        partial_sum = jnp.swapaxes(partial_sum, 1, 2)
        kept = lax.dynamic_slice(
            kept,
            (lax.axis_index("req") * rows_out, lax.axis_index("ctx") * slice_width),
            (rows_out, slice_width),
        )
    partial_sum = partial_sum.reshape(n_req * n_ctx, rows_out, slice_width)
    landed = lax.all_to_all(partial_sum, ("req", "ctx"), split_axis=0, concat_axis=0, tiled=True)
    return (kept + jnp.sum(landed.astype(jnp.float32), axis=0)).astype(jnp.bfloat16)


def solution(mesh):
    in_specs = (
        P("ctx", "req"),
        P("req", "ctx", None),
        P("req", "ctx", None),
        P("req"),
        P("ctx", None, None),
        P("ctx", "req"),
        P(),
        P(),
        P(),
        P("req", "ctx", None),
        P("req", "ctx", None),
        P("req", "ctx", None),
    )
    out_specs = P("req", "ctx")
    return jax.shard_map(local, mesh=mesh, in_specs=in_specs, out_specs=out_specs, check_vma=False)
```

```python
import functools

import jax
import jax.numpy as jnp
from jax import lax
from jax.experimental import pallas as pl
from jax.experimental.pallas import tpu as pltpu
from jax.sharding import PartitionSpec as P

SOFTMAX_SCALE = 192.0 ** (-0.5)
NEG_FILL = -1e30
NORM_EPS = 1e-06
CORES = 2
OVERLAP = 60
LANES = 128
MIB = 1 << 20
NT = (((1,), (1,)), ((), ()))
VMEM = pl.BlockSpec(memory_space=pltpu.VMEM)
HBM = pl.BlockSpec(memory_space=pltpu.HBM)


def swap(x, axis, step, size):
    return lax.ppermute(x, axis, [(i, i ^ step) for i in range(size)])


def stack_rows(blocks):
    if len(blocks) == 1:
        return blocks[0]
    if all(b.shape[0] % 16 == 0 for b in blocks):
        return jnp.concatenate(blocks, axis=0)
    return jnp.concatenate([b.astype(jnp.float32) for b in blocks], axis=0).astype(blocks[0].dtype)


def attend_kernel(n_blocks, q_tokens, width, lengths, *refs):
    queries, caches, outs = refs[:n_blocks], refs[n_blocks : n_blocks + 2], refs[n_blocks + 2 :]
    req_local, rows, _ = queries[0].shape
    ctx_local = caches[0].shape[2]
    total_rows = n_blocks * rows
    heads_local = rows // q_tokens
    row = lax.broadcasted_iota(jnp.int32, (total_rows, ctx_local), 0)
    column = lax.broadcasted_iota(jnp.int32, (total_rows, ctx_local), 1)
    token = (row // heads_local) % q_tokens
    lane = lax.broadcasted_iota(jnp.int32, (total_rows, LANES), 1)
    for r in range(req_local):
        grouped = stack_rows([q[r] for q in queries])
        limit = lengths[:, r : r + 1] - q_tokens + token
        masked = []
        for half, cache in enumerate(caches):
            score = jnp.dot(grouped, cache[r], preferred_element_type=jnp.float32)
            visible = column + (lax.axis_index("ctx") ^ half) * ctx_local <= limit
            masked.append(jnp.where(visible, score * SOFTMAX_SCALE, -jnp.inf))
        peak = jnp.maximum(
            jnp.max(masked[0], axis=-1, keepdims=True), jnp.max(masked[1], axis=-1, keepdims=True)
        )
        peak = jnp.where(peak > -jnp.inf, peak, 0.0)
        total = jnp.zeros((total_rows, 1), jnp.float32)
        mixed = jnp.zeros((total_rows, width), jnp.float32)
        for scores, cache in zip(masked, caches):
            raised = jnp.exp(scores - peak)
            total += jnp.sum(raised, axis=-1, keepdims=True)
            mixed += lax.dot_general(
                raised.astype(jnp.bfloat16),
                cache[r, :width, :],
                NT,
                preferred_element_type=jnp.float32,
            )
        filled = total > 0.0
        safe = jnp.where(filled, total, 1.0)
        mean = jnp.where(filled, mixed / safe, 0.0).astype(jnp.bfloat16)
        log = jnp.where(filled, peak + jnp.log(safe), NEG_FILL)
        high = log.astype(jnp.bfloat16).astype(jnp.float32)
        tail = jnp.where(lane == 0, high, jnp.where(lane == 1, log - high, 0.0))
        tail = tail.astype(jnp.bfloat16)
        for s, out in enumerate(outs):
            out[r, :, :width] = mean[s * rows : (s + 1) * rows]
            out[r, :, width:] = tail[s * rows : (s + 1) * rows]


def attend(blocks, caches, lengths, width, q_tokens):
    req_local, rows, lat = blocks[0].shape
    n = len(blocks)
    ctx_local = caches[0].shape[2]
    shape = jax.ShapeDtypeStruct((req_local, rows, width + LANES), jnp.bfloat16)
    return pl.pallas_call(
        functools.partial(attend_kernel, n, q_tokens, width),
        out_shape=[shape] * n,
        in_specs=[VMEM] * (n + 3),
        out_specs=[VMEM] * n,
        compiler_params=pltpu.CompilerParams(vmem_limit_bytes=4 * MIB),
        cost_estimate=pl.CostEstimate(
            flops=OVERLAP * 4 * req_local * n * rows * ctx_local * (lat + width),
            bytes_accessed=4 * req_local * ctx_local * lat,
            transcendentals=2 * req_local * n * rows * ctx_local,
        ),
        name="attend",
    )(lengths.reshape(1, -1), *blocks, *caches)


def stage_kernel(*refs):
    n = len(refs) // 2
    sems = refs[-1]
    copies = [
        pltpu.make_async_copy(source, target, sems.at[i])
        for i, (source, target) in enumerate(zip(refs[:n], refs[n : 2 * n]))
    ]
    for copy in copies:
        copy.start()
    for copy in copies:
        copy.wait()


def stage(arrays):
    return pl.pallas_call(
        stage_kernel,
        out_shape=[pltpu.VMEM(x.shape, x.dtype) for x in arrays],
        in_specs=[HBM] * len(arrays),
        out_specs=[VMEM] * len(arrays),
        scratch_shapes=[pltpu.SemaphoreType.DMA((len(arrays),))],
        compiler_params=pltpu.CompilerParams(vmem_limit_bytes=4 * MIB),
        cost_estimate=pl.CostEstimate(
            flops=0, bytes_accessed=sum(x.size * 2 for x in arrays), transcendentals=0
        ),
        name="stage",
    )(*[pltpu.with_memory_space_constraint(x, pltpu.HBM) for x in arrays])


def combine_kernel(n_blocks, q_tokens, *refs):
    blocks, (w_uv, out) = refs[:n_blocks], refs[n_blocks:]
    heads, width, value_width = w_uv.shape
    req_local, rows, _ = blocks[0].shape
    total_rows = req_local * rows
    parts = [b[...].astype(jnp.float32).reshape(total_rows, -1) for b in blocks]
    logs = [p[:, width : width + 1] + p[:, width + 1 : width + 2] for p in parts]
    top = functools.reduce(jnp.maximum, logs)
    factors = [jnp.exp(log - top) for log in logs]
    numer = sum(f * p[:, :width] for f, p in zip(factors, parts))
    latent = (numer / sum(factors)).astype(jnp.bfloat16)
    head = lax.broadcasted_iota(jnp.int32, (total_rows, value_width), 0) % heads
    values = []
    for h in range(heads):
        value = jnp.dot(latent, w_uv[h], preferred_element_type=jnp.float32)
        values.append(jnp.where(head == h, value, 0.0).astype(jnp.bfloat16))
    values = jnp.concatenate(values, axis=1)
    tokens = req_local * q_tokens
    token = lax.broadcasted_iota(jnp.int32, (tokens, total_rows), 0)
    at = lax.broadcasted_iota(jnp.int32, (tokens, total_rows), 1)
    fold = jnp.where(at // heads == token, 1.0, 0.0).astype(jnp.bfloat16)
    out[...] = jnp.dot(fold, values, preferred_element_type=jnp.float32).astype(out.dtype)


def combine(blocks, w_uv, q_tokens):
    heads, width, value_width = w_uv.shape
    req_local, rows, _ = blocks[0].shape
    tokens = req_local * q_tokens
    return pl.pallas_call(
        functools.partial(combine_kernel, len(blocks), q_tokens),
        out_shape=jax.ShapeDtypeStruct((tokens, heads * value_width), jnp.bfloat16),
        in_specs=[VMEM] * (len(blocks) + 1),
        out_specs=VMEM,
        compiler_params=pltpu.CompilerParams(vmem_limit_bytes=4 * MIB),
        cost_estimate=pl.CostEstimate(
            flops=2 * req_local * rows * w_uv.size, bytes_accessed=2 * w_uv.size, transcendentals=0
        ),
        name="combine",
    )(*blocks, w_uv)


def one_hot(shape, target):
    at = lax.broadcasted_iota(jnp.int32, shape, 1)
    return jnp.where(at == target(lax.broadcasted_iota(jnp.int32, shape, 0)), 1.0, 0.0).astype(
        jnp.bfloat16
    )


def out_proj_kernel(n_blocks, *refs):
    blocks, (w_o, residual, out) = refs[:n_blocks], refs[n_blocks:]
    per = blocks[0].shape[0]
    tokens = n_blocks * per
    stacked = stack_rows([b[...] for b in blocks])
    at_ctx, at_req = lax.axis_index("ctx"), lax.axis_index("req")
    order = one_hot((tokens, tokens), lambda row: (row // per ^ at_req) * per + row % per)
    ordered = jnp.dot(order, stacked, preferred_element_type=jnp.float32).astype(jnp.bfloat16)
    total = jnp.dot(ordered, w_o[...], preferred_element_type=jnp.float32)
    own = residual.shape[0]
    row = lax.broadcasted_iota(jnp.int32, total.shape, 0) - at_ctx * own
    rows = residual[...].astype(jnp.float32)
    for i in range(own):
        total += jnp.where(row == i, rows[i : i + 1], 0.0)
    out[...] = total.astype(out.dtype)


def out_proj(blocks, w_o, residual):
    n = len(blocks)
    tokens = n * blocks[0].shape[0]
    return pl.pallas_call(
        functools.partial(out_proj_kernel, n),
        out_shape=jax.ShapeDtypeStruct((tokens, w_o.shape[1]), jnp.bfloat16),
        in_specs=[VMEM] * (n + 2),
        out_specs=VMEM,
        compiler_params=pltpu.CompilerParams(vmem_limit_bytes=4 * MIB),
        cost_estimate=pl.CostEstimate(
            flops=2 * tokens * w_o.size, bytes_accessed=2 * w_o.size, transcendentals=0
        ),
        name="out_proj",
    )(*blocks, w_o, residual)


def add_products(totals, steps, blocks, gain, gate, up):
    n_exp = gate.shape[0]
    width = blocks[0].shape[1]
    for step, block in zip(steps, blocks):
        columns = pl.ds(0, width)
        if width < gate.shape[2]:
            columns = pl.ds(pl.multiple_of((lax.axis_index("req") ^ step) * width, LANES), width)
        rows = block[...].astype(jnp.float32) * gain[:, columns].astype(jnp.float32)
        rows = rows.astype(jnp.bfloat16)
        for m, weights in enumerate((gate, up)):
            for e in range(n_exp):
                product = lax.dot_general(
                    weights[e, :, columns], rows, NT, preferred_element_type=jnp.float32
                )
                at = m * n_exp + e
                totals[at] = product if totals[at] is None else totals[at] + product
    return totals


def part_kernel(steps, block, gain, gate, up, *refs):
    out = refs[-1]
    totals = add_products([None] * out.shape[0], steps, [block], gain, gate, up)
    for at, total in enumerate(totals):
        out[at] = total


def part(step, block, gain, w_gate, w_up, *held):
    n_exp, units, _ = w_gate.shape
    tokens, width = block.shape
    return pl.pallas_call(
        functools.partial(part_kernel, [step]),
        out_shape=pltpu.VMEM((2 * n_exp, units, tokens), jnp.float32),
        in_specs=[VMEM] * (4 + len(held)),
        out_specs=VMEM,
        compiler_params=pltpu.CompilerParams(vmem_limit_bytes=4 * MIB),
        cost_estimate=pl.CostEstimate(
            flops=4 * tokens * n_exp * units * width,
            bytes_accessed=4 * n_exp * units * width,
            transcendentals=0,
        ),
        name="part",
    )(block, gain, w_gate, w_up, *held)


def experts_kernel(n_blocks, n_parts, *refs):
    blocks, refs = refs[:n_blocks], refs[n_blocks:]
    parts, refs = refs[:n_parts], refs[n_parts:]
    gain, routes, weights, gate, up, down, out, kept, hidden, rows = refs
    at_ctx, at_req = lax.axis_index("ctx"), lax.axis_index("req")
    n_exp, units, model = gate.shape
    tokens = rows.shape[0]
    width = blocks[0].shape[1]
    steps = range(n_parts, n_blocks)
    totals = [None] * (2 * n_exp)
    for done in parts:
        totals = [done[at] if t is None else t + done[at] for at, t in enumerate(totals)]
    totals = add_products(totals, steps, blocks[n_parts:], gain, gate, up)
    totals = [t.T for t in totals]
    for s, block in enumerate(blocks):
        if n_blocks == 1:
            rows[...] = block[...]
        else:
            offset = pl.multiple_of((at_req ^ s) * width, LANES)
            rows[:, pl.ds(offset, width)] = block[...]
    squares = sum(
        jnp.sum(jnp.square(b[...].astype(jnp.float32)), axis=-1, keepdims=True) for b in blocks
    )
    scale = lax.rsqrt(squares / model + NORM_EPS)
    eye = lax.broadcasted_iota(jnp.int32, (tokens, tokens), 0) == lax.broadcasted_iota(
        jnp.int32, (tokens, tokens), 1
    )
    for e in range(n_exp):
        named = jnp.where(routes[...] == at_req * n_exp + e, weights[...], 0.0)
        coef = jnp.sum(named, axis=0, keepdims=True)
        coef = jnp.sum(jnp.where(eye, coef, 0.0), axis=1, keepdims=True)
        active = jax.nn.silu(totals[e] * scale) * (totals[n_exp + e] * scale) * coef
        hidden[:, e * units : (e + 1) * units] = active.astype(jnp.bfloat16)
    sliced = len(out.shape) == 4
    if sliced:
        per, chunk = out.shape[2:]
        columns = pl.ds(pl.multiple_of(at_ctx * chunk, LANES), chunk)
        own = one_hot((per, tokens), lambda row: row + at_req * per)
        kept[...] = jnp.dot(own, rows[:, columns], preferred_element_type=jnp.float32)
        down_products(out, hidden, down, 1 - at_ctx % CORES)
    else:
        chunk = model // 8
        kept[...] = rows[...].astype(jnp.float32)
        for j in range(8):
            columns = slice(j * chunk, (j + 1) * chunk)
            part_down = down[:, :, columns].reshape(n_exp * units, chunk)
            total = jnp.dot(hidden[...], part_down, preferred_element_type=jnp.float32)
            out[:, columns] = total.astype(out.dtype)


def down_products(out, hidden, down, core):
    n_exp, units, _ = down.shape
    n_req, n_chips, per, chunk = out.shape
    for p in range(n_chips):
        columns = pl.ds(pl.multiple_of((p * CORES + core) * chunk, LANES), chunk)
        part_down = down[:, :, columns].reshape(n_exp * units, chunk)
        total = jnp.dot(hidden[...], part_down, preferred_element_type=jnp.float32)
        total = total.astype(out.dtype)
        for q in range(n_req):
            out[q, p] = total[q * per : (q + 1) * per]


def own_down_kernel(hidden, down, *refs):
    out = refs[-1]
    down_products(out, hidden, down, lax.axis_index("ctx") % CORES)


def own_down(hidden, w_down, shape, *held):
    weights = [pltpu.with_memory_space_constraint(w, pltpu.VMEM) for w in (w_down, *held)]
    return pl.pallas_call(
        own_down_kernel,
        out_shape=jax.ShapeDtypeStruct(shape, jnp.float32),
        in_specs=[VMEM] * (1 + len(weights)),
        out_specs=VMEM,
        compiler_params=pltpu.CompilerParams(vmem_limit_bytes=4 * MIB),
        cost_estimate=pl.CostEstimate(
            flops=hidden.shape[0] * w_down.size, bytes_accessed=w_down.size, transcendentals=0
        ),
        name="own_down",
    )(hidden, *weights)


def experts(blocks, gain, routes, route_weight, w_gate, w_up, w_down, n_req, n_ctx):
    n_exp, units, model = w_gate.shape
    tokens = blocks[0].shape[0]
    slice_width = model // n_ctx
    aligned = slice_width % LANES == 0
    w_gate, w_up, w_down = [
        pltpu.with_memory_space_constraint(w, pltpu.VMEM) for w in (w_gate, w_up, w_down)
    ]
    parts = []
    if len(blocks) > 2:
        parts = [part(s, blocks[s], gain, w_gate, w_up, w_down) for s in range(2)]
    shape = (n_req, n_ctx // CORES, tokens // n_req, slice_width) if aligned else (tokens, model)
    kept = (tokens // n_req, slice_width) if aligned else (tokens, model)
    return pl.pallas_call(
        functools.partial(experts_kernel, len(blocks), len(parts)),
        out_shape=[
            jax.ShapeDtypeStruct(shape, jnp.bfloat16),
            jax.ShapeDtypeStruct(kept, jnp.float32),
            jax.ShapeDtypeStruct((tokens, n_exp * units), jnp.bfloat16),
        ],
        in_specs=[VMEM] * (len(blocks) + len(parts) + 6),
        out_specs=[VMEM] * 3,
        scratch_shapes=[
            pltpu.VMEM((tokens, model), jnp.bfloat16),
        ],
        compiler_params=pltpu.CompilerParams(vmem_limit_bytes=4 * MIB),
        cost_estimate=pl.CostEstimate(
            flops=6 * tokens * w_gate.size,
            bytes_accessed=6 * w_gate.size,
            transcendentals=n_exp * units * tokens,
        ),
        name="experts",
    )(*blocks, *parts, gain, routes, route_weight, w_gate, w_up, w_down)


def local(
    residual,
    query,
    latent_cache,
    lengths,
    w_uv,
    w_o,
    norm_gain,
    routes,
    route_weight,
    w_gate,
    w_up,
    w_down,
):
    n_ctx = lax.axis_size("ctx")
    n_req = lax.axis_size("req")
    chip_steps = range(CORES, n_ctx, CORES)
    req_steps = range(1, n_req)
    req_local = latent_cache.shape[0]
    heads_local, lat_width, _ = w_uv.shape
    tok_local = query.shape[0]
    q_tokens = tok_local // req_local

    cache = jnp.swapaxes(latent_cache, 1, 2)
    other_cache = swap(cache, "ctx", 1, n_ctx)
    query = query.reshape(req_local, q_tokens * heads_local, query.shape[2])
    received = [swap(query, "ctx", s, n_ctx) for s in chip_steps]
    cache, query, w_uv, w_o = stage([cache, query, w_uv, w_o])
    blocks = [query] + received
    outs = attend(blocks, (cache, other_cache), lengths, lat_width, q_tokens)
    outs = [outs[0]] + [swap(o, "ctx", s, n_ctx) for o, s in zip(outs[1:], chip_steps)]

    head_values = combine(outs, w_uv, q_tokens)
    blocks = [head_values] + [swap(head_values, "req", s, n_req) for s in req_steps]
    partial_mid = out_proj(blocks, w_o, residual)

    other = swap(partial_mid, "ctx", 1, n_ctx)
    chip_mid = (partial_mid.astype(jnp.float32) + other.astype(jnp.float32)).astype(jnp.bfloat16)
    pieces = [chip_mid] + [swap(chip_mid, "ctx", s, n_ctx) for s in chip_steps]
    mid = sum(p.astype(jnp.float32) for p in pieces).astype(jnp.bfloat16)
    if mid.shape[1] % LANES == 0:
        blocks = [mid] + [swap(mid, "req", s, n_req) for s in req_steps]
    else:
        blocks = [lax.all_gather(mid, "req", axis=1, tiled=True)]

    partial_sum, kept, hidden = experts(
        blocks,
        norm_gain.reshape(1, -1),
        routes.T,
        route_weight.T,
        w_gate,
        w_up,
        w_down,
        n_req,
        n_ctx,
    )
    tokens = mid.shape[0]
    model_width = w_gate.shape[2]
    rows_out = tokens // n_req
    slice_width = model_width // n_ctx
    groups = None
    if partial_sum.ndim == 2:
        partial_sum = partial_sum.reshape(n_req, rows_out, n_ctx, slice_width)
        partial_sum = jnp.swapaxes(partial_sum, 1, 2)
        kept = lax.dynamic_slice(
            kept,
            (lax.axis_index("req") * rows_out, lax.axis_index("ctx") * slice_width),
            (rows_out, slice_width),
        )
    else:
        other = swap(partial_sum, "ctx", 1, n_ctx)
        own = own_down(hidden, w_down, partial_sum.shape, w_gate, w_up)
        partial_sum = (own + other.astype(jnp.float32)).astype(jnp.bfloat16)
        groups = [list(range(core, n_req * n_ctx, CORES)) for core in range(CORES)]
    partial_sum = partial_sum.reshape(-1, rows_out, slice_width)
    landed = lax.all_to_all(
        partial_sum,
        ("req", "ctx"),
        split_axis=0,
        concat_axis=0,
        axis_index_groups=groups,
        tiled=True,
    )
    return (kept + jnp.sum(landed.astype(jnp.float32), axis=0)).astype(jnp.bfloat16)


def solution(mesh):
    in_specs = (
        P("ctx", "req"),
        P("req", "ctx", None),
        P("req", "ctx", None),
        P("req"),
        P("ctx", None, None),
        P("ctx", "req"),
        P(),
        P(),
        P(),
        P("req", "ctx", None),
        P("req", "ctx", None),
        P("req", "ctx", None),
    )
    out_specs = P("req", "ctx")
    return jax.shard_map(local, mesh=mesh, in_specs=in_specs, out_specs=out_specs, check_vma=False)
```

```python
import functools

import jax
import jax.numpy as jnp
from jax import lax
from jax.experimental import pallas as pl
from jax.experimental.pallas import tpu as pltpu
from jax.sharding import PartitionSpec as P

SOFTMAX_SCALE = 192.0 ** (-0.5)
NEG_FILL = -1e30
NORM_EPS = 1e-06
CORES = 2
OVERLAP = 60
LANES = 128
LOG_ROWS = 16
MIB = 1 << 20
NT = (((1,), (1,)), ((), ()))
VMEM = pl.BlockSpec(memory_space=pltpu.VMEM)
HBM = pl.BlockSpec(memory_space=pltpu.HBM)


def swap(x, axis, step, size):
    return lax.ppermute(x, axis, [(i, i ^ step) for i in range(size)])


def stack_rows(blocks):
    if len(blocks) == 1:
        return blocks[0]
    if all(b.shape[0] % 16 == 0 for b in blocks):
        return jnp.concatenate(blocks, axis=0)
    return jnp.concatenate([b.astype(jnp.float32) for b in blocks], axis=0).astype(blocks[0].dtype)


def attend_kernel(n_blocks, q_tokens, width, lengths, *refs):
    queries, caches, outs = refs[:n_blocks], refs[n_blocks : n_blocks + 2], refs[n_blocks + 2 :]
    req_local, rows, _ = queries[0].shape
    ctx_local = caches[0].shape[2]
    total_rows = n_blocks * rows
    heads_local = rows // q_tokens
    row = lax.broadcasted_iota(jnp.int32, (total_rows, ctx_local), 0)
    column = lax.broadcasted_iota(jnp.int32, (total_rows, ctx_local), 1)
    token = (row // heads_local) % q_tokens
    means, log_rows = [], [jnp.zeros((1, LANES), jnp.float32)] * n_blocks
    for r in range(req_local):
        grouped = stack_rows([q[r] for q in queries])
        limit = lengths[:, r : r + 1] - q_tokens + token
        masked = []
        for half, cache in enumerate(caches):
            score = jnp.dot(grouped, cache[r], preferred_element_type=jnp.float32)
            visible = column + (lax.axis_index("ctx") ^ half) * ctx_local <= limit
            masked.append(jnp.where(visible, score * SOFTMAX_SCALE, -jnp.inf))
        peak = jnp.maximum(
            jnp.max(masked[0], axis=-1, keepdims=True), jnp.max(masked[1], axis=-1, keepdims=True)
        )
        peak = jnp.where(peak > -jnp.inf, peak, 0.0)
        total = jnp.zeros((total_rows, 1), jnp.float32)
        mixed = jnp.zeros((total_rows, width), jnp.float32)
        for scores, cache in zip(masked, caches):
            raised = jnp.exp(scores - peak)
            total += jnp.sum(raised, axis=-1, keepdims=True)
            mixed += lax.dot_general(
                raised.astype(jnp.bfloat16),
                cache[r, :width, :],
                NT,
                preferred_element_type=jnp.float32,
            )
        filled = total > 0.0
        safe = jnp.where(filled, total, 1.0)
        mean = jnp.where(filled, mixed / safe, 0.0).astype(jnp.bfloat16)
        log = jnp.where(filled, peak + jnp.log(safe), NEG_FILL)
        high = log.astype(jnp.bfloat16).astype(jnp.float32)
        means.append(mean)
        for s in range(n_blocks):
            block = slice(s * rows, (s + 1) * rows)
            logs = log_lanes(
                lambda where_high, where_low: jnp.where(
                    where_high, high[block], jnp.where(where_low, (log - high)[block], 0.0)
                ),
                rows,
                r * rows,
            )
            log_rows[s] += jnp.sum(logs, axis=0, keepdims=True)
    packed = req_local * rows
    for s, (row, out) in enumerate(zip(log_rows, outs)):
        for i in range(width // LANES):
            columns = slice(i * LANES, (i + 1) * LANES)
            out[i * packed : (i + 1) * packed] = stack_rows(
                [mean[s * rows : (s + 1) * rows, columns] for mean in means]
            )
        spread = jnp.broadcast_to(row, (LOG_ROWS, LANES))
        out[out.shape[0] - LOG_ROWS :] = spread.astype(jnp.bfloat16)


def log_lanes(pick, rows, start):
    row = start + lax.broadcasted_iota(jnp.int32, (rows, LANES), 0)
    lane = lax.broadcasted_iota(jnp.int32, (rows, LANES), 1)
    return pick(lane == row, lane == row + LANES // 2)


def attend(blocks, caches, lengths, width, q_tokens):
    req_local, rows, lat = blocks[0].shape
    n = len(blocks)
    ctx_local = caches[0].shape[2]
    packed = req_local * rows * width // LANES + LOG_ROWS
    shape = jax.ShapeDtypeStruct((packed, LANES), jnp.bfloat16)
    return pl.pallas_call(
        functools.partial(attend_kernel, n, q_tokens, width),
        out_shape=[shape] * n,
        in_specs=[VMEM] * (n + 3),
        out_specs=[VMEM] * n,
        compiler_params=pltpu.CompilerParams(vmem_limit_bytes=4 * MIB),
        cost_estimate=pl.CostEstimate(
            flops=OVERLAP * 4 * req_local * n * rows * ctx_local * (lat + width),
            bytes_accessed=4 * req_local * ctx_local * lat,
            transcendentals=2 * req_local * n * rows * ctx_local,
        ),
        name="attend",
    )(lengths.reshape(1, -1), *blocks, *caches)


def stage_kernel(*refs):
    n = len(refs) // 2
    sems = refs[-1]
    copies = [
        pltpu.make_async_copy(source, target, sems.at[i])
        for i, (source, target) in enumerate(zip(refs[:n], refs[n : 2 * n]))
    ]
    for copy in copies:
        copy.start()
    for copy in copies:
        copy.wait()


def stage(arrays):
    return pl.pallas_call(
        stage_kernel,
        out_shape=[pltpu.VMEM(x.shape, x.dtype) for x in arrays],
        in_specs=[HBM] * len(arrays),
        out_specs=[VMEM] * len(arrays),
        scratch_shapes=[pltpu.SemaphoreType.DMA((len(arrays),))],
        compiler_params=pltpu.CompilerParams(vmem_limit_bytes=4 * MIB),
        cost_estimate=pl.CostEstimate(
            flops=0, bytes_accessed=sum(x.size * 2 for x in arrays), transcendentals=0
        ),
        name="stage",
    )(*[pltpu.with_memory_space_constraint(x, pltpu.HBM) for x in arrays])


def combine_kernel(n_blocks, *refs):
    blocks, (w_uv, out) = refs[:n_blocks], refs[n_blocks:]
    heads, width, value_width = w_uv.shape
    total_rows = (blocks[0].shape[0] - LOG_ROWS) * LANES // width
    parts, logs = [], []
    for block in blocks:
        columns = [
            block[i * total_rows : (i + 1) * total_rows].astype(jnp.float32)
            for i in range(width // LANES)
        ]
        parts.append(jnp.concatenate(columns, axis=1))
        row = block[block.shape[0] - LOG_ROWS :].astype(jnp.float32)[:1]
        lanes = log_lanes(lambda high, low: jnp.where(high | low, row, 0.0), total_rows, 0)
        logs.append(jnp.sum(lanes, axis=1, keepdims=True))
    top = functools.reduce(jnp.maximum, logs)
    factors = [jnp.exp(log - top) for log in logs]
    numer = sum(f * p for f, p in zip(factors, parts))
    latent = (numer / sum(factors)).astype(jnp.bfloat16)
    head = lax.broadcasted_iota(jnp.int32, (total_rows, value_width), 0) % heads
    values = []
    for h in range(heads):
        value = jnp.dot(latent, w_uv[h], preferred_element_type=jnp.float32)
        values.append(jnp.where(head == h, value, 0.0).astype(jnp.bfloat16))
    values = jnp.concatenate(values, axis=1)
    tokens = total_rows // heads
    token = lax.broadcasted_iota(jnp.int32, (tokens, total_rows), 0)
    at = lax.broadcasted_iota(jnp.int32, (tokens, total_rows), 1)
    fold = jnp.where(at // heads == token, 1.0, 0.0).astype(jnp.bfloat16)
    out[...] = jnp.dot(fold, values, preferred_element_type=jnp.float32).astype(out.dtype)


def combine(blocks, w_uv):
    heads, width, value_width = w_uv.shape
    rows = (blocks[0].shape[0] - LOG_ROWS) * LANES // width
    tokens = rows // heads
    return pl.pallas_call(
        functools.partial(combine_kernel, len(blocks)),
        out_shape=jax.ShapeDtypeStruct((tokens, heads * value_width), jnp.bfloat16),
        in_specs=[VMEM] * (len(blocks) + 1),
        out_specs=VMEM,
        compiler_params=pltpu.CompilerParams(vmem_limit_bytes=4 * MIB),
        cost_estimate=pl.CostEstimate(
            flops=2 * rows * w_uv.size, bytes_accessed=2 * w_uv.size, transcendentals=0
        ),
        name="combine",
    )(*blocks, w_uv)


def one_hot(shape, target):
    at = lax.broadcasted_iota(jnp.int32, shape, 1)
    return jnp.where(at == target(lax.broadcasted_iota(jnp.int32, shape, 0)), 1.0, 0.0).astype(
        jnp.bfloat16
    )


def out_proj_kernel(n_blocks, *refs):
    blocks, (w_o, residual, out) = refs[:n_blocks], refs[n_blocks:]
    per = blocks[0].shape[0]
    tokens = n_blocks * per
    stacked = stack_rows([b[...] for b in blocks])
    at_ctx, at_req = lax.axis_index("ctx"), lax.axis_index("req")
    order = one_hot((tokens, tokens), lambda row: (row // per ^ at_req) * per + row % per)
    ordered = jnp.dot(order, stacked, preferred_element_type=jnp.float32).astype(jnp.bfloat16)
    total = jnp.dot(ordered, w_o[...], preferred_element_type=jnp.float32)
    own = residual.shape[0]
    row = lax.broadcasted_iota(jnp.int32, total.shape, 0) - at_ctx * own
    rows = residual[...].astype(jnp.float32)
    for i in range(own):
        total += jnp.where(row == i, rows[i : i + 1], 0.0)
    out[...] = total.astype(out.dtype)


def out_proj(blocks, w_o, residual):
    n = len(blocks)
    tokens = n * blocks[0].shape[0]
    return pl.pallas_call(
        functools.partial(out_proj_kernel, n),
        out_shape=jax.ShapeDtypeStruct((tokens, w_o.shape[1]), jnp.bfloat16),
        in_specs=[VMEM] * (n + 2),
        out_specs=VMEM,
        compiler_params=pltpu.CompilerParams(vmem_limit_bytes=4 * MIB),
        cost_estimate=pl.CostEstimate(
            flops=2 * tokens * w_o.size, bytes_accessed=2 * w_o.size, transcendentals=0
        ),
        name="out_proj",
    )(*blocks, w_o, residual)


def add_products(totals, steps, blocks, gain, gate, up):
    n_exp = gate.shape[0]
    width = blocks[0].shape[1]
    for step, block in zip(steps, blocks):
        columns = pl.ds(0, width)
        if width < gate.shape[2]:
            columns = pl.ds(pl.multiple_of((lax.axis_index("req") ^ step) * width, LANES), width)
        rows = block[...].astype(jnp.float32) * gain[:, columns].astype(jnp.float32)
        rows = rows.astype(jnp.bfloat16)
        for m, weights in enumerate((gate, up)):
            for e in range(n_exp):
                product = lax.dot_general(
                    weights[e, :, columns], rows, NT, preferred_element_type=jnp.float32
                )
                at = m * n_exp + e
                totals[at] = product if totals[at] is None else totals[at] + product
    return totals


def part_kernel(steps, block, gain, gate, up, *refs):
    out = refs[-1]
    totals = add_products([None] * out.shape[0], steps, [block], gain, gate, up)
    for at, total in enumerate(totals):
        out[at] = total


def part(step, block, gain, w_gate, w_up, *held):
    n_exp, units, _ = w_gate.shape
    tokens, width = block.shape
    return pl.pallas_call(
        functools.partial(part_kernel, [step]),
        out_shape=pltpu.VMEM((2 * n_exp, units, tokens), jnp.float32),
        in_specs=[VMEM] * (4 + len(held)),
        out_specs=VMEM,
        compiler_params=pltpu.CompilerParams(vmem_limit_bytes=4 * MIB),
        cost_estimate=pl.CostEstimate(
            flops=4 * tokens * n_exp * units * width,
            bytes_accessed=4 * n_exp * units * width,
            transcendentals=0,
        ),
        name="part",
    )(block, gain, w_gate, w_up, *held)


def experts_kernel(n_blocks, n_parts, *refs):
    blocks, refs = refs[:n_blocks], refs[n_blocks:]
    parts, refs = refs[:n_parts], refs[n_parts:]
    gain, routes, weights, gate, up, down, out, kept, hidden, rows = refs
    at_ctx, at_req = lax.axis_index("ctx"), lax.axis_index("req")
    n_exp, units, model = gate.shape
    tokens = rows.shape[0]
    width = blocks[0].shape[1]
    steps = range(n_parts, n_blocks)
    totals = [None] * (2 * n_exp)
    for done in parts:
        totals = [done[at] if t is None else t + done[at] for at, t in enumerate(totals)]
    totals = add_products(totals, steps, blocks[n_parts:], gain, gate, up)
    totals = [t.T for t in totals]
    for s, block in enumerate(blocks):
        if n_blocks == 1:
            rows[...] = block[...]
        else:
            offset = pl.multiple_of((at_req ^ s) * width, LANES)
            rows[:, pl.ds(offset, width)] = block[...]
    squares = sum(
        jnp.sum(jnp.square(b[...].astype(jnp.float32)), axis=-1, keepdims=True) for b in blocks
    )
    scale = lax.rsqrt(squares / model + NORM_EPS)
    eye = lax.broadcasted_iota(jnp.int32, (tokens, tokens), 0) == lax.broadcasted_iota(
        jnp.int32, (tokens, tokens), 1
    )
    for e in range(n_exp):
        named = jnp.where(routes[...] == at_req * n_exp + e, weights[...], 0.0)
        coef = jnp.sum(named, axis=0, keepdims=True)
        coef = jnp.sum(jnp.where(eye, coef, 0.0), axis=1, keepdims=True)
        active = jax.nn.silu(totals[e] * scale) * (totals[n_exp + e] * scale) * coef
        hidden[:, e * units : (e + 1) * units] = active.astype(jnp.bfloat16)
    sliced = len(out.shape) == 4
    if sliced:
        per, chunk = out.shape[2:]
        columns = pl.ds(pl.multiple_of(at_ctx * chunk, LANES), chunk)
        own = one_hot((per, tokens), lambda row: row + at_req * per)
        kept[...] = jnp.dot(own, rows[:, columns], preferred_element_type=jnp.float32)
        down_products(out, hidden, down, 1 - at_ctx % CORES)
    else:
        chunk = model // 8
        kept[...] = rows[...].astype(jnp.float32)
        for j in range(8):
            columns = slice(j * chunk, (j + 1) * chunk)
            part_down = down[:, :, columns].reshape(n_exp * units, chunk)
            total = jnp.dot(hidden[...], part_down, preferred_element_type=jnp.float32)
            out[:, columns] = total.astype(out.dtype)


def down_products(out, hidden, down, core):
    n_exp, units, _ = down.shape
    n_chips, n_req, per, chunk = out.shape
    at_chip, at_req = lax.axis_index("ctx") // CORES, lax.axis_index("req")
    for s in range(n_chips):
        columns = pl.ds(pl.multiple_of(((at_chip ^ s) * CORES + core) * chunk, LANES), chunk)
        part_down = down[:, :, columns].reshape(n_exp * units, chunk)
        total = jnp.dot(hidden[...], part_down, preferred_element_type=jnp.float32)
        total = total.astype(out.dtype)
        for q in range(n_req):
            out[s, at_req ^ q] = total[q * per : (q + 1) * per]


def own_down_kernel(hidden, down, *refs):
    out = refs[-1]
    down_products(out, hidden, down, lax.axis_index("ctx") % CORES)


def own_down(hidden, w_down, shape, *held):
    weights = [pltpu.with_memory_space_constraint(w, pltpu.VMEM) for w in (w_down, *held)]
    return pl.pallas_call(
        own_down_kernel,
        out_shape=jax.ShapeDtypeStruct(shape, jnp.float32),
        in_specs=[VMEM] * (1 + len(weights)),
        out_specs=VMEM,
        compiler_params=pltpu.CompilerParams(vmem_limit_bytes=4 * MIB),
        cost_estimate=pl.CostEstimate(
            flops=hidden.shape[0] * w_down.size, bytes_accessed=w_down.size, transcendentals=0
        ),
        name="own_down",
    )(hidden, *weights)


def experts(blocks, gain, routes, route_weight, w_gate, w_up, w_down, n_req, n_ctx):
    n_exp, units, model = w_gate.shape
    tokens = blocks[0].shape[0]
    slice_width = model // n_ctx
    aligned = slice_width % LANES == 0
    w_gate, w_up, w_down = [
        pltpu.with_memory_space_constraint(w, pltpu.VMEM) for w in (w_gate, w_up, w_down)
    ]
    parts = []
    if len(blocks) > 2:
        parts = [part(s, blocks[s], gain, w_gate, w_up, w_down) for s in range(2)]
    shape = (n_ctx // CORES, n_req, tokens // n_req, slice_width) if aligned else (tokens, model)
    kept = (tokens // n_req, slice_width) if aligned else (tokens, model)
    return pl.pallas_call(
        functools.partial(experts_kernel, len(blocks), len(parts)),
        out_shape=[
            jax.ShapeDtypeStruct(shape, jnp.bfloat16),
            jax.ShapeDtypeStruct(kept, jnp.float32),
            jax.ShapeDtypeStruct((tokens, n_exp * units), jnp.bfloat16),
        ],
        in_specs=[VMEM] * (len(blocks) + len(parts) + 6),
        out_specs=[VMEM] * 3,
        scratch_shapes=[
            pltpu.VMEM((tokens, model), jnp.bfloat16),
        ],
        compiler_params=pltpu.CompilerParams(vmem_limit_bytes=4 * MIB),
        cost_estimate=pl.CostEstimate(
            flops=6 * tokens * w_gate.size,
            bytes_accessed=6 * w_gate.size,
            transcendentals=n_exp * units * tokens,
        ),
        name="experts",
    )(*blocks, *parts, gain, routes, route_weight, w_gate, w_up, w_down)


def local(
    residual,
    query,
    latent_cache,
    lengths,
    w_uv,
    w_o,
    norm_gain,
    routes,
    route_weight,
    w_gate,
    w_up,
    w_down,
):
    n_ctx = lax.axis_size("ctx")
    n_req = lax.axis_size("req")
    chip_steps = range(CORES, n_ctx, CORES)
    req_steps = range(1, n_req)
    req_local = latent_cache.shape[0]
    heads_local, lat_width, _ = w_uv.shape
    tok_local = query.shape[0]
    q_tokens = tok_local // req_local

    cache = jnp.swapaxes(latent_cache, 1, 2)
    other_cache = swap(cache, "ctx", 1, n_ctx)
    query = query.reshape(req_local, q_tokens * heads_local, query.shape[2])
    received = [swap(query, "ctx", s, n_ctx) for s in chip_steps]
    cache, query, w_uv, w_o = stage([cache, query, w_uv, w_o])
    blocks = [query] + received
    outs = attend(blocks, (cache, other_cache), lengths, lat_width, q_tokens)
    outs = [outs[0]] + [swap(o, "ctx", s, n_ctx) for o, s in zip(outs[1:], chip_steps)]

    head_values = combine(outs, w_uv)
    blocks = [head_values] + [swap(head_values, "req", s, n_req) for s in req_steps]
    partial_mid = out_proj(blocks, w_o, residual)

    other = swap(partial_mid, "ctx", 1, n_ctx)
    chip_mid = (partial_mid.astype(jnp.float32) + other.astype(jnp.float32)).astype(jnp.bfloat16)
    pieces = [chip_mid] + [swap(chip_mid, "ctx", s, n_ctx) for s in chip_steps]
    mid = sum(p.astype(jnp.float32) for p in pieces).astype(jnp.bfloat16)
    if mid.shape[1] % LANES == 0:
        blocks = [mid] + [swap(mid, "req", s, n_req) for s in req_steps]
    else:
        blocks = [lax.all_gather(mid, "req", axis=1, tiled=True)]

    partial_sum, kept, hidden = experts(
        blocks,
        norm_gain.reshape(1, -1),
        routes.T,
        route_weight.T,
        w_gate,
        w_up,
        w_down,
        n_req,
        n_ctx,
    )
    tokens = mid.shape[0]
    model_width = w_gate.shape[2]
    rows_out = tokens // n_req
    slice_width = model_width // n_ctx
    if partial_sum.ndim == 2:
        partial_sum = partial_sum.reshape(n_req, rows_out, n_ctx, slice_width)
        partial_sum = jnp.swapaxes(partial_sum, 1, 2).reshape(-1, rows_out, slice_width)
        landed = lax.all_to_all(
            partial_sum, ("req", "ctx"), split_axis=0, concat_axis=0, tiled=True
        )
        kept = lax.dynamic_slice(
            kept,
            (lax.axis_index("req") * rows_out, lax.axis_index("ctx") * slice_width),
            (rows_out, slice_width),
        )
        return (kept + jnp.sum(landed.astype(jnp.float32), axis=0)).astype(jnp.bfloat16)
    other = swap(partial_sum, "ctx", 1, n_ctx)
    own = own_down(hidden, w_down, partial_sum.shape, w_gate, w_up)
    chip_sum = [(own[i] + other[i].astype(jnp.float32)) for i in range(n_ctx // CORES)]
    landed = [
        swap(x.astype(jnp.bfloat16), "ctx", s, n_ctx) for x, s in zip(chip_sum[1:], chip_steps)
    ]
    req_sum = sum([x.astype(jnp.float32) for x in landed], chip_sum[0])
    landed = [swap(req_sum[s].astype(jnp.bfloat16), "req", s, n_req) for s in req_steps]
    total = sum([x.astype(jnp.float32) for x in landed], kept + req_sum[0])
    return total.astype(jnp.bfloat16)


def solution(mesh):
    in_specs = (
        P("ctx", "req"),
        P("req", "ctx", None),
        P("req", "ctx", None),
        P("req"),
        P("ctx", None, None),
        P("ctx", "req"),
        P(),
        P(),
        P(),
        P("req", "ctx", None),
        P("req", "ctx", None),
        P("req", "ctx", None),
    )
    out_specs = P("req", "ctx")
    return jax.shard_map(local, mesh=mesh, in_specs=in_specs, out_specs=out_specs, check_vma=False)
```

```python
import functools

import jax
import jax.numpy as jnp
from jax import lax
from jax.experimental import pallas as pl
from jax.experimental.pallas import tpu as pltpu
from jax.sharding import PartitionSpec as P

SOFTMAX_SCALE = 192.0 ** (-0.5)
NEG_FILL = -1e30
NORM_EPS = 1e-06
CORES = 2
OVERLAP = 60
LANES = 128
LOG_ROWS = 16
MIB = 1 << 20
NT = (((1,), (1,)), ((), ()))
VMEM = pl.BlockSpec(memory_space=pltpu.VMEM)
HBM = pl.BlockSpec(memory_space=pltpu.HBM)


def swap(x, axis, step, size):
    return lax.ppermute(x, axis, [(i, i ^ step) for i in range(size)])


def stack_rows(blocks):
    if len(blocks) == 1:
        return blocks[0]
    if all(b.shape[0] % 16 == 0 for b in blocks):
        return jnp.concatenate(blocks, axis=0)
    return jnp.concatenate([b.astype(jnp.float32) for b in blocks], axis=0).astype(blocks[0].dtype)


def attend_kernel(n_blocks, q_tokens, width, lengths, *refs):
    queries, caches, outs = refs[:n_blocks], refs[n_blocks : n_blocks + 2], refs[n_blocks + 2 :]
    req_local, rows, _ = queries[0].shape
    ctx_local = caches[0].shape[2]
    total_rows = n_blocks * rows
    heads_local = rows // q_tokens
    row = lax.broadcasted_iota(jnp.int32, (total_rows, ctx_local), 0)
    column = lax.broadcasted_iota(jnp.int32, (total_rows, ctx_local), 1)
    token = (row // heads_local) % q_tokens
    means, log_rows = [], [jnp.zeros((1, LANES), jnp.float32)] * n_blocks
    for r in range(req_local):
        grouped = stack_rows([q[r] for q in queries])
        limit = lengths[:, r : r + 1] - q_tokens + token
        masked = []
        for half, cache in enumerate(caches):
            score = jnp.dot(grouped, cache[r], preferred_element_type=jnp.float32)
            visible = column + (lax.axis_index("ctx") ^ half) * ctx_local <= limit
            masked.append(jnp.where(visible, score * SOFTMAX_SCALE, -jnp.inf))
        peak = jnp.maximum(
            jnp.max(masked[0], axis=-1, keepdims=True), jnp.max(masked[1], axis=-1, keepdims=True)
        )
        peak = jnp.where(peak > -jnp.inf, peak, 0.0)
        total = jnp.zeros((total_rows, 1), jnp.float32)
        mixed = jnp.zeros((total_rows, width), jnp.float32)
        for scores, cache in zip(masked, caches):
            raised = jnp.exp(scores - peak)
            total += jnp.sum(raised, axis=-1, keepdims=True)
            mixed += lax.dot_general(
                raised.astype(jnp.bfloat16),
                cache[r, :width, :],
                NT,
                preferred_element_type=jnp.float32,
            )
        filled = total > 0.0
        safe = jnp.where(filled, total, 1.0)
        mean = jnp.where(filled, mixed / safe, 0.0).astype(jnp.bfloat16)
        log = jnp.where(filled, peak + jnp.log(safe), NEG_FILL)
        high = log.astype(jnp.bfloat16).astype(jnp.float32)
        means.append(mean)
        for s in range(n_blocks):
            block = slice(s * rows, (s + 1) * rows)
            logs = log_lanes(
                lambda where_high, where_low: jnp.where(
                    where_high, high[block], jnp.where(where_low, (log - high)[block], 0.0)
                ),
                rows,
                r * rows,
            )
            log_rows[s] += jnp.sum(logs, axis=0, keepdims=True)
    packed = req_local * rows
    for s, (row, out) in enumerate(zip(log_rows, outs)):
        for i in range(width // LANES):
            columns = slice(i * LANES, (i + 1) * LANES)
            out[i * packed : (i + 1) * packed] = stack_rows(
                [mean[s * rows : (s + 1) * rows, columns] for mean in means]
            )
        spread = jnp.broadcast_to(row, (LOG_ROWS, LANES))
        out[out.shape[0] - LOG_ROWS :] = spread.astype(jnp.bfloat16)


def log_lanes(pick, rows, start):
    row = start + lax.broadcasted_iota(jnp.int32, (rows, LANES), 0)
    lane = lax.broadcasted_iota(jnp.int32, (rows, LANES), 1)
    return pick(lane == row, lane == row + LANES // 2)


def attend(blocks, caches, lengths, width, q_tokens):
    req_local, rows, lat = blocks[0].shape
    n = len(blocks)
    ctx_local = caches[0].shape[2]
    packed = req_local * rows * width // LANES + LOG_ROWS
    shape = jax.ShapeDtypeStruct((packed, LANES), jnp.bfloat16)
    return pl.pallas_call(
        functools.partial(attend_kernel, n, q_tokens, width),
        out_shape=[shape] * n,
        in_specs=[VMEM] * (n + 3),
        out_specs=[VMEM] * n,
        compiler_params=pltpu.CompilerParams(vmem_limit_bytes=4 * MIB),
        cost_estimate=pl.CostEstimate(
            flops=OVERLAP * 4 * req_local * n * rows * ctx_local * (lat + width),
            bytes_accessed=4 * req_local * ctx_local * lat,
            transcendentals=2 * req_local * n * rows * ctx_local,
        ),
        name="attend",
    )(lengths.reshape(1, -1), *blocks, *caches)


def stage_kernel(*refs):
    n = len(refs) // 2
    sems = refs[-1]
    copies = [
        pltpu.make_async_copy(source, target, sems.at[i])
        for i, (source, target) in enumerate(zip(refs[:n], refs[n : 2 * n]))
    ]
    for copy in copies:
        copy.start()
    for copy in copies:
        copy.wait()


def stage(arrays):
    return pl.pallas_call(
        stage_kernel,
        out_shape=[pltpu.VMEM(x.shape, x.dtype) for x in arrays],
        in_specs=[HBM] * len(arrays),
        out_specs=[VMEM] * len(arrays),
        scratch_shapes=[pltpu.SemaphoreType.DMA((len(arrays),))],
        compiler_params=pltpu.CompilerParams(vmem_limit_bytes=4 * MIB),
        cost_estimate=pl.CostEstimate(
            flops=0, bytes_accessed=sum(x.size * 2 for x in arrays), transcendentals=0
        ),
        name="stage",
    )(*[pltpu.with_memory_space_constraint(x, pltpu.HBM) for x in arrays])


def combine_kernel(n_blocks, *refs):
    blocks, (w_uv, out) = refs[:n_blocks], refs[n_blocks:]
    heads, width, value_width = w_uv.shape
    total_rows = (blocks[0].shape[0] - LOG_ROWS) * LANES // width
    parts, logs = [], []
    for block in blocks:
        columns = [
            block[i * total_rows : (i + 1) * total_rows].astype(jnp.float32)
            for i in range(width // LANES)
        ]
        parts.append(jnp.concatenate(columns, axis=1))
        row = block[block.shape[0] - LOG_ROWS :].astype(jnp.float32)[:1]
        lanes = log_lanes(lambda high, low: jnp.where(high | low, row, 0.0), total_rows, 0)
        logs.append(jnp.sum(lanes, axis=1, keepdims=True))
    top = functools.reduce(jnp.maximum, logs)
    factors = [jnp.exp(log - top) for log in logs]
    numer = sum(f * p for f, p in zip(factors, parts))
    latent = (numer / sum(factors)).astype(jnp.bfloat16)
    head = lax.broadcasted_iota(jnp.int32, (total_rows, value_width), 0) % heads
    values = []
    for h in range(heads):
        value = jnp.dot(latent, w_uv[h], preferred_element_type=jnp.float32)
        values.append(jnp.where(head == h, value, 0.0).astype(jnp.bfloat16))
    values = jnp.concatenate(values, axis=1)
    tokens = total_rows // heads
    token = lax.broadcasted_iota(jnp.int32, (tokens, total_rows), 0)
    at = lax.broadcasted_iota(jnp.int32, (tokens, total_rows), 1)
    fold = jnp.where(at // heads == token, 1.0, 0.0).astype(jnp.bfloat16)
    out[...] = jnp.dot(fold, values, preferred_element_type=jnp.float32).astype(out.dtype)


def combine(blocks, w_uv):
    heads, width, value_width = w_uv.shape
    rows = (blocks[0].shape[0] - LOG_ROWS) * LANES // width
    tokens = rows // heads
    return pl.pallas_call(
        functools.partial(combine_kernel, len(blocks)),
        out_shape=jax.ShapeDtypeStruct((tokens, heads * value_width), jnp.bfloat16),
        in_specs=[VMEM] * (len(blocks) + 1),
        out_specs=VMEM,
        compiler_params=pltpu.CompilerParams(vmem_limit_bytes=4 * MIB),
        cost_estimate=pl.CostEstimate(
            flops=2 * rows * w_uv.size, bytes_accessed=2 * w_uv.size, transcendentals=0
        ),
        name="combine",
    )(*blocks, w_uv)


def one_hot(shape, target):
    at = lax.broadcasted_iota(jnp.int32, shape, 1)
    return jnp.where(at == target(lax.broadcasted_iota(jnp.int32, shape, 0)), 1.0, 0.0).astype(
        jnp.bfloat16
    )


def out_proj_kernel(n_blocks, *refs):
    blocks, (w_o, residual, out) = refs[:n_blocks], refs[n_blocks:]
    blocks = blocks[:1] + blocks[:0:-1]
    per = blocks[0].shape[0]
    tokens = n_blocks * per
    stacked = stack_rows([b[...] for b in blocks])
    at_ctx, at_req = lax.axis_index("ctx"), lax.axis_index("req")
    order = one_hot((tokens, tokens), lambda row: (row // per ^ at_req) * per + row % per)
    ordered = jnp.dot(order, stacked, preferred_element_type=jnp.float32).astype(jnp.bfloat16)
    total = jnp.dot(ordered, w_o[...], preferred_element_type=jnp.float32)
    own = residual.shape[0]
    row = lax.broadcasted_iota(jnp.int32, total.shape, 0) - at_ctx * own
    rows = residual[...].astype(jnp.float32)
    for i in range(own):
        total += jnp.where(row == i, rows[i : i + 1], 0.0)
    out[...] = total.astype(out.dtype)


def out_proj(blocks, w_o, residual):
    n = len(blocks)
    tokens = n * blocks[0].shape[0]
    return pl.pallas_call(
        functools.partial(out_proj_kernel, n),
        out_shape=jax.ShapeDtypeStruct((tokens, w_o.shape[1]), jnp.bfloat16),
        in_specs=[VMEM] * (n + 2),
        out_specs=VMEM,
        compiler_params=pltpu.CompilerParams(vmem_limit_bytes=4 * MIB),
        cost_estimate=pl.CostEstimate(
            flops=2 * tokens * w_o.size, bytes_accessed=2 * w_o.size, transcendentals=0
        ),
        name="out_proj",
    )(*blocks, w_o, residual)


def add_products(totals, steps, blocks, gain, gate, up):
    n_exp = gate.shape[0]
    width = blocks[0].shape[1]
    for step, block in zip(steps, blocks):
        columns = pl.ds(0, width)
        if width < gate.shape[2]:
            columns = pl.ds(pl.multiple_of((lax.axis_index("req") ^ step) * width, LANES), width)
        rows = block[...].astype(jnp.float32) * gain[:, columns].astype(jnp.float32)
        rows = rows.astype(jnp.bfloat16)
        for m, weights in enumerate((gate, up)):
            for e in range(n_exp):
                product = lax.dot_general(
                    weights[e, :, columns], rows, NT, preferred_element_type=jnp.float32
                )
                at = m * n_exp + e
                totals[at] = product if totals[at] is None else totals[at] + product
    return totals


def part_kernel(steps, block, gain, gate, up, *refs):
    out = refs[-1]
    totals = add_products([None] * out.shape[0], steps, [block], gain, gate, up)
    for at, total in enumerate(totals):
        out[at] = total


def part(step, block, gain, w_gate, w_up, *held):
    n_exp, units, _ = w_gate.shape
    tokens, width = block.shape
    return pl.pallas_call(
        functools.partial(part_kernel, [step]),
        out_shape=pltpu.VMEM((2 * n_exp, units, tokens), jnp.float32),
        in_specs=[VMEM] * (4 + len(held)),
        out_specs=VMEM,
        compiler_params=pltpu.CompilerParams(vmem_limit_bytes=4 * MIB),
        cost_estimate=pl.CostEstimate(
            flops=4 * tokens * n_exp * units * width,
            bytes_accessed=4 * n_exp * units * width,
            transcendentals=0,
        ),
        name="part",
    )(block, gain, w_gate, w_up, *held)


def experts_kernel(order, n_parts, *refs):
    n_blocks = len(order)
    blocks, refs = refs[:n_blocks], refs[n_blocks:]
    parts, refs = refs[:n_parts], refs[n_parts:]
    gain, routes, weights, gate, up, down, out, kept, hidden, rows = refs
    at_ctx, at_req = lax.axis_index("ctx"), lax.axis_index("req")
    n_exp, units, model = gate.shape
    tokens = rows.shape[0]
    width = blocks[0].shape[1]
    totals = [None] * (2 * n_exp)
    for done in parts:
        totals = [done[at] if t is None else t + done[at] for at, t in enumerate(totals)]
    totals = add_products(totals, order[n_parts:], blocks[n_parts:], gain, gate, up)
    totals = [t.T for t in totals]
    for s, block in zip(order, blocks):
        if n_blocks == 1:
            rows[...] = block[...]
        else:
            offset = pl.multiple_of((at_req ^ s) * width, LANES)
            rows[:, pl.ds(offset, width)] = block[...]
    squares = sum(
        jnp.sum(jnp.square(b[...].astype(jnp.float32)), axis=-1, keepdims=True) for b in blocks
    )
    scale = lax.rsqrt(squares / model + NORM_EPS)
    eye = lax.broadcasted_iota(jnp.int32, (tokens, tokens), 0) == lax.broadcasted_iota(
        jnp.int32, (tokens, tokens), 1
    )
    for e in range(n_exp):
        named = jnp.where(routes[...] == at_req * n_exp + e, weights[...], 0.0)
        coef = jnp.sum(named, axis=0, keepdims=True)
        coef = jnp.sum(jnp.where(eye, coef, 0.0), axis=1, keepdims=True)
        active = jax.nn.silu(totals[e] * scale) * (totals[n_exp + e] * scale) * coef
        hidden[:, e * units : (e + 1) * units] = active.astype(jnp.bfloat16)
    sliced = len(out.shape) == 4
    if sliced:
        per, chunk = out.shape[2:]
        columns = pl.ds(pl.multiple_of(at_ctx * chunk, LANES), chunk)
        own = one_hot((per, tokens), lambda row: row + at_req * per)
        kept[...] = jnp.dot(own, rows[:, columns], preferred_element_type=jnp.float32)
        down_products(out, hidden, down, 1 - at_ctx % CORES)
    else:
        chunk = model // 8
        kept[...] = rows[...].astype(jnp.float32)
        for j in range(8):
            columns = slice(j * chunk, (j + 1) * chunk)
            part_down = down[:, :, columns].reshape(n_exp * units, chunk)
            total = jnp.dot(hidden[...], part_down, preferred_element_type=jnp.float32)
            out[:, columns] = total.astype(out.dtype)


def down_products(out, hidden, down, core):
    n_exp, units, _ = down.shape
    n_req, n_chips, per, chunk = out.shape
    for p in range(n_chips):
        columns = pl.ds(pl.multiple_of((p * CORES + core) * chunk, LANES), chunk)
        part_down = down[:, :, columns].reshape(n_exp * units, chunk)
        total = jnp.dot(hidden[...], part_down, preferred_element_type=jnp.float32)
        total = total.astype(out.dtype)
        for q in range(n_req):
            out[q, p] = total[q * per : (q + 1) * per]


def own_down_kernel(hidden, down, *refs):
    out = refs[-1]
    down_products(out, hidden, down, lax.axis_index("ctx") % CORES)


def own_down(hidden, w_down, shape, *held):
    weights = [pltpu.with_memory_space_constraint(w, pltpu.VMEM) for w in (w_down, *held)]
    return pl.pallas_call(
        own_down_kernel,
        out_shape=jax.ShapeDtypeStruct(shape, jnp.float32),
        in_specs=[VMEM] * (1 + len(weights)),
        out_specs=VMEM,
        compiler_params=pltpu.CompilerParams(vmem_limit_bytes=4 * MIB),
        cost_estimate=pl.CostEstimate(
            flops=hidden.shape[0] * w_down.size, bytes_accessed=w_down.size, transcendentals=0
        ),
        name="own_down",
    )(hidden, *weights)


def experts(order, blocks, gain, routes, route_weight, w_gate, w_up, w_down, n_req, n_ctx):
    n_exp, units, model = w_gate.shape
    tokens = blocks[0].shape[0]
    slice_width = model // n_ctx
    aligned = slice_width % LANES == 0
    w_gate, w_up, w_down = [
        pltpu.with_memory_space_constraint(w, pltpu.VMEM) for w in (w_gate, w_up, w_down)
    ]
    parts = []
    if len(blocks) > 2:
        parts = [part(order[i], blocks[i], gain, w_gate, w_up, w_down) for i in range(2)]
    shape = (n_req, n_ctx // CORES, tokens // n_req, slice_width) if aligned else (tokens, model)
    kept = (tokens // n_req, slice_width) if aligned else (tokens, model)
    return pl.pallas_call(
        functools.partial(experts_kernel, order, len(parts)),
        out_shape=[
            jax.ShapeDtypeStruct(shape, jnp.bfloat16),
            jax.ShapeDtypeStruct(kept, jnp.float32),
            jax.ShapeDtypeStruct((tokens, n_exp * units), jnp.bfloat16),
        ],
        in_specs=[VMEM] * (len(blocks) + len(parts) + 6),
        out_specs=[VMEM] * 3,
        scratch_shapes=[
            pltpu.VMEM((tokens, model), jnp.bfloat16),
        ],
        compiler_params=pltpu.CompilerParams(vmem_limit_bytes=4 * MIB),
        cost_estimate=pl.CostEstimate(
            flops=6 * tokens * w_gate.size,
            bytes_accessed=6 * w_gate.size,
            transcendentals=n_exp * units * tokens,
        ),
        name="experts",
    )(*blocks, *parts, gain, routes, route_weight, w_gate, w_up, w_down)


def local(
    residual,
    query,
    latent_cache,
    lengths,
    w_uv,
    w_o,
    norm_gain,
    routes,
    route_weight,
    w_gate,
    w_up,
    w_down,
):
    n_ctx = lax.axis_size("ctx")
    n_req = lax.axis_size("req")
    chip_steps = range(CORES, n_ctx, CORES)
    req_steps = range(1, n_req)
    req_local = latent_cache.shape[0]
    heads_local, lat_width, _ = w_uv.shape
    tok_local = query.shape[0]
    q_tokens = tok_local // req_local

    cache = jnp.swapaxes(latent_cache, 1, 2)
    other_cache = swap(cache, "ctx", 1, n_ctx)
    query = query.reshape(req_local, q_tokens * heads_local, query.shape[2])
    received = [swap(query, "ctx", s, n_ctx) for s in chip_steps]
    cache, query, w_uv, w_o = stage([cache, query, w_uv, w_o])
    blocks = [query] + received
    outs = attend(blocks, (cache, other_cache), lengths, lat_width, q_tokens)
    outs = [outs[0]] + [swap(o, "ctx", s, n_ctx) for o, s in zip(outs[1:], chip_steps)]

    head_values = combine(outs, w_uv)
    blocks = [head_values] + [swap(head_values, "req", s, n_req) for s in reversed(req_steps)]
    partial_mid = out_proj(blocks, w_o, residual)

    other = swap(partial_mid, "ctx", 1, n_ctx)
    chip_mid = (partial_mid.astype(jnp.float32) + other.astype(jnp.float32)).astype(jnp.bfloat16)
    pieces = [chip_mid] + [swap(chip_mid, "ctx", s, n_ctx) for s in chip_steps]
    mid = sum(p.astype(jnp.float32) for p in pieces).astype(jnp.bfloat16)
    if mid.shape[1] % LANES == 0:
        order = [0, 1, *range(n_req - 1, 1, -1)]
        blocks = [mid] + [swap(mid, "req", s, n_req) for s in order[1:]]
    else:
        order = [0]
        blocks = [lax.all_gather(mid, "req", axis=1, tiled=True)]

    partial_sum, kept, hidden = experts(
        order,
        blocks,
        norm_gain.reshape(1, -1),
        routes.T,
        route_weight.T,
        w_gate,
        w_up,
        w_down,
        n_req,
        n_ctx,
    )
    tokens = mid.shape[0]
    model_width = w_gate.shape[2]
    rows_out = tokens // n_req
    slice_width = model_width // n_ctx
    groups = None
    if partial_sum.ndim == 2:
        partial_sum = partial_sum.reshape(n_req, rows_out, n_ctx, slice_width)
        partial_sum = jnp.swapaxes(partial_sum, 1, 2)
        kept = lax.dynamic_slice(
            kept,
            (lax.axis_index("req") * rows_out, lax.axis_index("ctx") * slice_width),
            (rows_out, slice_width),
        )
    else:
        other = swap(partial_sum, "ctx", 1, n_ctx)
        own = own_down(hidden, w_down, partial_sum.shape, w_gate, w_up)
        partial_sum = (own + other.astype(jnp.float32)).astype(jnp.bfloat16)
        groups = [list(range(core, n_req * n_ctx, CORES)) for core in range(CORES)]
    partial_sum = partial_sum.reshape(-1, rows_out, slice_width)
    landed = lax.all_to_all(
        partial_sum,
        ("req", "ctx"),
        split_axis=0,
        concat_axis=0,
        axis_index_groups=groups,
        tiled=True,
    )
    return (kept + jnp.sum(landed.astype(jnp.float32), axis=0)).astype(jnp.bfloat16)


def solution(mesh):
    in_specs = (
        P("ctx", "req"),
        P("req", "ctx", None),
        P("req", "ctx", None),
        P("req"),
        P("ctx", None, None),
        P("ctx", "req"),
        P(),
        P(),
        P(),
        P("req", "ctx", None),
        P("req", "ctx", None),
        P("req", "ctx", None),
    )
    out_specs = P("req", "ctx")
    return jax.shard_map(local, mesh=mesh, in_specs=in_specs, out_specs=out_specs, check_vma=False)
```

```python
import functools

import jax
import jax.numpy as jnp
from jax import lax
from jax.experimental import pallas as pl
from jax.experimental.pallas import tpu as pltpu
from jax.sharding import PartitionSpec as P

SOFTMAX_SCALE = 192.0 ** (-0.5)
NEG_FILL = -1e30
NORM_EPS = 1e-06
CORES = 2
OVERLAP = 60
LANES = 128
LOG_ROWS = 16
MIB = 1 << 20
NT = (((1,), (1,)), ((), ()))
VMEM = pl.BlockSpec(memory_space=pltpu.VMEM)
HBM = pl.BlockSpec(memory_space=pltpu.HBM)


def swap(x, axis, step, size):
    return lax.ppermute(x, axis, [(i, i ^ step) for i in range(size)])


def stack_rows(blocks):
    if len(blocks) == 1:
        return blocks[0]
    if all(b.shape[0] % 16 == 0 for b in blocks):
        return jnp.concatenate(blocks, axis=0)
    return jnp.concatenate([b.astype(jnp.float32) for b in blocks], axis=0).astype(blocks[0].dtype)


def attend_kernel(n_blocks, q_tokens, width, lengths, *refs):
    queries, caches, outs = refs[:n_blocks], refs[n_blocks : n_blocks + 2], refs[n_blocks + 2 :]
    req_local, rows, _ = queries[0].shape
    ctx_local = caches[0].shape[2]
    total_rows = n_blocks * rows
    heads_local = rows // q_tokens
    row = lax.broadcasted_iota(jnp.int32, (total_rows, ctx_local), 0)
    column = lax.broadcasted_iota(jnp.int32, (total_rows, ctx_local), 1)
    token = (row // heads_local) % q_tokens
    means, log_rows = [], [jnp.zeros((1, LANES), jnp.float32)] * n_blocks
    for r in range(req_local):
        grouped = stack_rows([q[r] for q in queries])
        limit = lengths[:, r : r + 1] - q_tokens + token
        masked = []
        for half, cache in enumerate(caches):
            score = jnp.dot(grouped, cache[r], preferred_element_type=jnp.float32)
            visible = column + (lax.axis_index("ctx") ^ half) * ctx_local <= limit
            masked.append(jnp.where(visible, score * SOFTMAX_SCALE, -jnp.inf))
        peak = jnp.maximum(
            jnp.max(masked[0], axis=-1, keepdims=True), jnp.max(masked[1], axis=-1, keepdims=True)
        )
        peak = jnp.where(peak > -jnp.inf, peak, 0.0)
        total = jnp.zeros((total_rows, 1), jnp.float32)
        mixed = jnp.zeros((total_rows, width), jnp.float32)
        for scores, cache in zip(masked, caches):
            raised = jnp.exp(scores - peak)
            total += jnp.sum(raised, axis=-1, keepdims=True)
            mixed += lax.dot_general(
                raised.astype(jnp.bfloat16),
                cache[r, :width, :],
                NT,
                preferred_element_type=jnp.float32,
            )
        filled = total > 0.0
        safe = jnp.where(filled, total, 1.0)
        mean = jnp.where(filled, mixed / safe, 0.0).astype(jnp.bfloat16)
        log = jnp.where(filled, peak + jnp.log(safe), NEG_FILL)
        high = log.astype(jnp.bfloat16).astype(jnp.float32)
        means.append(mean)
        for s in range(n_blocks):
            block = slice(s * rows, (s + 1) * rows)
            logs = log_lanes(
                lambda where_high, where_low: jnp.where(
                    where_high, high[block], jnp.where(where_low, (log - high)[block], 0.0)
                ),
                rows,
                r * rows,
            )
            log_rows[s] += jnp.sum(logs, axis=0, keepdims=True)
    packed = req_local * rows
    for s, (row, out) in enumerate(zip(log_rows, outs)):
        for i in range(width // LANES):
            columns = slice(i * LANES, (i + 1) * LANES)
            out[i * packed : (i + 1) * packed] = stack_rows(
                [mean[s * rows : (s + 1) * rows, columns] for mean in means]
            )
        spread = jnp.broadcast_to(row, (LOG_ROWS, LANES))
        out[out.shape[0] - LOG_ROWS :] = spread.astype(jnp.bfloat16)


def log_lanes(pick, rows, start):
    row = start + lax.broadcasted_iota(jnp.int32, (rows, LANES), 0)
    lane = lax.broadcasted_iota(jnp.int32, (rows, LANES), 1)
    return pick(lane == row, lane == row + LANES // 2)


def attend(blocks, caches, lengths, width, q_tokens):
    req_local, rows, lat = blocks[0].shape
    n = len(blocks)
    ctx_local = caches[0].shape[2]
    packed = req_local * rows * width // LANES + LOG_ROWS
    shape = jax.ShapeDtypeStruct((packed, LANES), jnp.bfloat16)
    return pl.pallas_call(
        functools.partial(attend_kernel, n, q_tokens, width),
        out_shape=[shape] * n,
        in_specs=[VMEM] * (n + 3),
        out_specs=[VMEM] * n,
        compiler_params=pltpu.CompilerParams(vmem_limit_bytes=4 * MIB),
        cost_estimate=pl.CostEstimate(
            flops=OVERLAP * 4 * req_local * n * rows * ctx_local * (lat + width),
            bytes_accessed=4 * req_local * ctx_local * lat,
            transcendentals=2 * req_local * n * rows * ctx_local,
        ),
        name="attend",
    )(lengths.reshape(1, -1), *blocks, *caches)


def stage_kernel(*refs):
    n = len(refs) // 2
    sems = refs[-1]
    copies = [
        pltpu.make_async_copy(source, target, sems.at[i])
        for i, (source, target) in enumerate(zip(refs[:n], refs[n : 2 * n]))
    ]
    for copy in copies:
        copy.start()
    for copy in copies:
        copy.wait()


def stage(arrays):
    return pl.pallas_call(
        stage_kernel,
        out_shape=[pltpu.VMEM(x.shape, x.dtype) for x in arrays],
        in_specs=[HBM] * len(arrays),
        out_specs=[VMEM] * len(arrays),
        scratch_shapes=[pltpu.SemaphoreType.DMA((len(arrays),))],
        compiler_params=pltpu.CompilerParams(vmem_limit_bytes=4 * MIB),
        cost_estimate=pl.CostEstimate(
            flops=0, bytes_accessed=sum(x.size * 2 for x in arrays), transcendentals=0
        ),
        name="stage",
    )(*[pltpu.with_memory_space_constraint(x, pltpu.HBM) for x in arrays])


def combine_kernel(n_blocks, *refs):
    blocks, (w_uv, out) = refs[:n_blocks], refs[n_blocks:]
    heads, width, value_width = w_uv.shape
    total_rows = (blocks[0].shape[0] - LOG_ROWS) * LANES // width
    parts, logs = [], []
    for block in blocks:
        columns = [
            block[i * total_rows : (i + 1) * total_rows].astype(jnp.float32)
            for i in range(width // LANES)
        ]
        parts.append(jnp.concatenate(columns, axis=1))
        row = block[block.shape[0] - LOG_ROWS :].astype(jnp.float32)[:1]
        lanes = log_lanes(lambda high, low: jnp.where(high | low, row, 0.0), total_rows, 0)
        logs.append(jnp.sum(lanes, axis=1, keepdims=True))
    top = functools.reduce(jnp.maximum, logs)
    factors = [jnp.exp(log - top) for log in logs]
    numer = sum(f * p for f, p in zip(factors, parts))
    latent = (numer / sum(factors)).astype(jnp.bfloat16)
    head = lax.broadcasted_iota(jnp.int32, (total_rows, value_width), 0) % heads
    values = []
    for h in range(heads):
        value = jnp.dot(latent, w_uv[h], preferred_element_type=jnp.float32)
        values.append(jnp.where(head == h, value, 0.0).astype(jnp.bfloat16))
    values = jnp.concatenate(values, axis=1)
    tokens = total_rows // heads
    token = lax.broadcasted_iota(jnp.int32, (tokens, total_rows), 0)
    at = lax.broadcasted_iota(jnp.int32, (tokens, total_rows), 1)
    fold = jnp.where(at // heads == token, 1.0, 0.0).astype(jnp.bfloat16)
    out[...] = jnp.dot(fold, values, preferred_element_type=jnp.float32).astype(out.dtype)


def combine(blocks, w_uv):
    heads, width, value_width = w_uv.shape
    rows = (blocks[0].shape[0] - LOG_ROWS) * LANES // width
    tokens = rows // heads
    return pl.pallas_call(
        functools.partial(combine_kernel, len(blocks)),
        out_shape=jax.ShapeDtypeStruct((tokens, heads * value_width), jnp.bfloat16),
        in_specs=[VMEM] * (len(blocks) + 1),
        out_specs=VMEM,
        compiler_params=pltpu.CompilerParams(vmem_limit_bytes=4 * MIB),
        cost_estimate=pl.CostEstimate(
            flops=2 * rows * w_uv.size, bytes_accessed=2 * w_uv.size, transcendentals=0
        ),
        name="combine",
    )(*blocks, w_uv)


def one_hot(shape, target):
    at = lax.broadcasted_iota(jnp.int32, shape, 1)
    return jnp.where(at == target(lax.broadcasted_iota(jnp.int32, shape, 0)), 1.0, 0.0).astype(
        jnp.bfloat16
    )


def out_proj_kernel(n_blocks, *refs):
    blocks, (w_o, residual, out) = refs[:n_blocks], refs[n_blocks:]
    blocks = blocks[:1] + blocks[:0:-1]
    per = blocks[0].shape[0]
    tokens = n_blocks * per
    stacked = stack_rows([b[...] for b in blocks])
    at_ctx, at_req = lax.axis_index("ctx"), lax.axis_index("req")
    order = one_hot((tokens, tokens), lambda row: (row // per ^ at_req) * per + row % per)
    ordered = jnp.dot(order, stacked, preferred_element_type=jnp.float32).astype(jnp.bfloat16)
    total = jnp.dot(ordered, w_o[...], preferred_element_type=jnp.float32)
    own = residual.shape[0]
    row = lax.broadcasted_iota(jnp.int32, total.shape, 0) - at_ctx * own
    rows = residual[...].astype(jnp.float32)
    for i in range(own):
        total += jnp.where(row == i, rows[i : i + 1], 0.0)
    out[...] = total.astype(out.dtype)


def out_proj(blocks, w_o, residual):
    n = len(blocks)
    tokens = n * blocks[0].shape[0]
    return pl.pallas_call(
        functools.partial(out_proj_kernel, n),
        out_shape=jax.ShapeDtypeStruct((tokens, w_o.shape[1]), jnp.bfloat16),
        in_specs=[VMEM] * (n + 2),
        out_specs=VMEM,
        compiler_params=pltpu.CompilerParams(vmem_limit_bytes=4 * MIB),
        cost_estimate=pl.CostEstimate(
            flops=2 * tokens * w_o.size, bytes_accessed=2 * w_o.size, transcendentals=0
        ),
        name="out_proj",
    )(*blocks, w_o, residual)


def add_products(totals, steps, blocks, gain, gate, up):
    n_exp = gate.shape[0]
    width = blocks[0].shape[1]
    for step, block in zip(steps, blocks):
        columns = pl.ds(0, width)
        if width < gate.shape[2]:
            columns = pl.ds(pl.multiple_of((lax.axis_index("req") ^ step) * width, LANES), width)
        rows = block[...].astype(jnp.float32) * gain[:, columns].astype(jnp.float32)
        rows = rows.astype(jnp.bfloat16)
        for m, weights in enumerate((gate, up)):
            for e in range(n_exp):
                product = lax.dot_general(
                    weights[e, :, columns], rows, NT, preferred_element_type=jnp.float32
                )
                at = m * n_exp + e
                totals[at] = product if totals[at] is None else totals[at] + product
    return totals


def part_kernel(steps, block, gain, gate, up, *refs):
    out = refs[-1]
    totals = add_products([None] * out.shape[0], steps, [block], gain, gate, up)
    for at, total in enumerate(totals):
        out[at] = total


def part(step, block, gain, w_gate, w_up, *held):
    n_exp, units, _ = w_gate.shape
    tokens, width = block.shape
    return pl.pallas_call(
        functools.partial(part_kernel, [step]),
        out_shape=pltpu.VMEM((2 * n_exp, units, tokens), jnp.float32),
        in_specs=[VMEM] * (4 + len(held)),
        out_specs=VMEM,
        compiler_params=pltpu.CompilerParams(vmem_limit_bytes=4 * MIB),
        cost_estimate=pl.CostEstimate(
            flops=4 * tokens * n_exp * units * width,
            bytes_accessed=4 * n_exp * units * width,
            transcendentals=0,
        ),
        name="part",
    )(block, gain, w_gate, w_up, *held)


def experts_kernel(order, n_parts, *refs):
    n_blocks = len(order)
    blocks, refs = refs[:n_blocks], refs[n_blocks:]
    parts, refs = refs[:n_parts], refs[n_parts:]
    gain, routes, weights, gate, up, down, out, kept, hidden, rows = refs
    at_ctx, at_req = lax.axis_index("ctx"), lax.axis_index("req")
    n_exp, units, model = gate.shape
    tokens = rows.shape[0]
    width = blocks[0].shape[1]
    totals = [None] * (2 * n_exp)
    for done in parts:
        totals = [done[at] if t is None else t + done[at] for at, t in enumerate(totals)]
    totals = add_products(totals, order[n_parts:], blocks[n_parts:], gain, gate, up)
    totals = [t.T for t in totals]
    for s, block in zip(order, blocks):
        if n_blocks == 1:
            rows[...] = block[...]
        else:
            offset = pl.multiple_of((at_req ^ s) * width, LANES)
            rows[:, pl.ds(offset, width)] = block[...]
    squares = sum(
        jnp.sum(jnp.square(b[...].astype(jnp.float32)), axis=-1, keepdims=True) for b in blocks
    )
    scale = lax.rsqrt(squares / model + NORM_EPS)
    eye = lax.broadcasted_iota(jnp.int32, (tokens, tokens), 0) == lax.broadcasted_iota(
        jnp.int32, (tokens, tokens), 1
    )
    for e in range(n_exp):
        named = jnp.where(routes[...] == at_req * n_exp + e, weights[...], 0.0)
        coef = jnp.sum(named, axis=0, keepdims=True)
        coef = jnp.sum(jnp.where(eye, coef, 0.0), axis=1, keepdims=True)
        active = jax.nn.silu(totals[e] * scale) * (totals[n_exp + e] * scale) * coef
        hidden[:, e * units : (e + 1) * units] = active.astype(jnp.bfloat16)
    sliced = len(out.shape) == 4
    if sliced:
        per, chunk = out.shape[2:]
        columns = pl.ds(pl.multiple_of(at_ctx * chunk, LANES), chunk)
        own = one_hot((per, tokens), lambda row: row + at_req * per)
        kept[...] = jnp.dot(own, rows[:, columns], preferred_element_type=jnp.float32)
        down_products(out, hidden, down, 1 - at_ctx % CORES)
    else:
        chunk = model // 8
        kept[...] = rows[...].astype(jnp.float32)
        for j in range(8):
            columns = slice(j * chunk, (j + 1) * chunk)
            part_down = down[:, :, columns].reshape(n_exp * units, chunk)
            total = jnp.dot(hidden[...], part_down, preferred_element_type=jnp.float32)
            out[:, columns] = total.astype(out.dtype)


def down_products(out, hidden, down, core):
    n_exp, units, _ = down.shape
    n_req, n_chips, per, chunk = out.shape
    for p in range(n_chips):
        columns = pl.ds(pl.multiple_of((p * CORES + core) * chunk, LANES), chunk)
        part_down = down[:, :, columns].reshape(n_exp * units, chunk)
        total = jnp.dot(hidden[...], part_down, preferred_element_type=jnp.float32)
        total = total.astype(out.dtype)
        for q in range(n_req):
            out[q, p] = total[q * per : (q + 1) * per]


def own_down_kernel(hidden, down, *refs):
    out = refs[-1]
    down_products(out, hidden, down, lax.axis_index("ctx") % CORES)


def own_down(hidden, w_down, shape, *held):
    weights = [pltpu.with_memory_space_constraint(w, pltpu.VMEM) for w in (w_down, *held)]
    return pl.pallas_call(
        own_down_kernel,
        out_shape=jax.ShapeDtypeStruct(shape, jnp.float32),
        in_specs=[VMEM] * (1 + len(weights)),
        out_specs=VMEM,
        compiler_params=pltpu.CompilerParams(vmem_limit_bytes=4 * MIB),
        cost_estimate=pl.CostEstimate(
            flops=hidden.shape[0] * w_down.size, bytes_accessed=w_down.size, transcendentals=0
        ),
        name="own_down",
    )(hidden, *weights)


def experts(order, blocks, gain, routes, route_weight, w_gate, w_up, w_down, n_req, n_ctx):
    n_exp, units, model = w_gate.shape
    tokens = blocks[0].shape[0]
    slice_width = model // n_ctx
    aligned = slice_width % LANES == 0
    w_gate, w_up, w_down = [
        pltpu.with_memory_space_constraint(w, pltpu.VMEM) for w in (w_gate, w_up, w_down)
    ]
    parts = []
    if len(blocks) > 2:
        parts = [part(order[i], blocks[i], gain, w_gate, w_up, w_down) for i in range(2)]
    shape = (n_req, n_ctx // CORES, tokens // n_req, slice_width) if aligned else (tokens, model)
    kept = (tokens // n_req, slice_width) if aligned else (tokens, model)
    return pl.pallas_call(
        functools.partial(experts_kernel, order, len(parts)),
        out_shape=[
            jax.ShapeDtypeStruct(shape, jnp.bfloat16),
            jax.ShapeDtypeStruct(kept, jnp.float32),
            jax.ShapeDtypeStruct((tokens, n_exp * units), jnp.bfloat16),
        ],
        in_specs=[VMEM] * (len(blocks) + len(parts) + 6),
        out_specs=[VMEM] * 3,
        scratch_shapes=[
            pltpu.VMEM((tokens, model), jnp.bfloat16),
        ],
        compiler_params=pltpu.CompilerParams(vmem_limit_bytes=4 * MIB),
        cost_estimate=pl.CostEstimate(
            flops=6 * tokens * w_gate.size,
            bytes_accessed=6 * w_gate.size,
            transcendentals=n_exp * units * tokens,
        ),
        name="experts",
    )(*blocks, *parts, gain, routes, route_weight, w_gate, w_up, w_down)


def local(
    residual,
    query,
    latent_cache,
    lengths,
    w_uv,
    w_o,
    norm_gain,
    routes,
    route_weight,
    w_gate,
    w_up,
    w_down,
):
    n_ctx = lax.axis_size("ctx")
    n_req = lax.axis_size("req")
    chip_steps = list(range(CORES, n_ctx, CORES))[::-1]
    req_steps = range(1, n_req)
    req_local = latent_cache.shape[0]
    heads_local, lat_width, _ = w_uv.shape
    tok_local = query.shape[0]
    q_tokens = tok_local // req_local

    cache = jnp.swapaxes(latent_cache, 1, 2)
    other_cache = swap(cache, "ctx", 1, n_ctx)
    query = query.reshape(req_local, q_tokens * heads_local, query.shape[2])
    received = [swap(query, "ctx", s, n_ctx) for s in chip_steps]
    cache, query, w_uv, w_o = stage([cache, query, w_uv, w_o])
    blocks = [query] + received
    outs = attend(blocks, (cache, other_cache), lengths, lat_width, q_tokens)
    outs = [outs[0]] + [swap(o, "ctx", s, n_ctx) for o, s in zip(outs[1:], chip_steps)]

    head_values = combine(outs, w_uv)
    blocks = [head_values] + [swap(head_values, "req", s, n_req) for s in reversed(req_steps)]
    partial_mid = out_proj(blocks, w_o, residual)

    other = swap(partial_mid, "ctx", 1, n_ctx)
    chip_mid = (partial_mid.astype(jnp.float32) + other.astype(jnp.float32)).astype(jnp.bfloat16)
    pieces = [chip_mid] + [swap(chip_mid, "ctx", s, n_ctx) for s in chip_steps]
    mid = sum(p.astype(jnp.float32) for p in pieces).astype(jnp.bfloat16)
    if mid.shape[1] % LANES == 0:
        order = [0, 1, *range(n_req - 1, 1, -1)]
        blocks = [mid] + [swap(mid, "req", s, n_req) for s in order[1:]]
    else:
        order = [0]
        blocks = [lax.all_gather(mid, "req", axis=1, tiled=True)]

    partial_sum, kept, hidden = experts(
        order,
        blocks,
        norm_gain.reshape(1, -1),
        routes.T,
        route_weight.T,
        w_gate,
        w_up,
        w_down,
        n_req,
        n_ctx,
    )
    tokens = mid.shape[0]
    model_width = w_gate.shape[2]
    rows_out = tokens // n_req
    slice_width = model_width // n_ctx
    groups = None
    if partial_sum.ndim == 2:
        partial_sum = partial_sum.reshape(n_req, rows_out, n_ctx, slice_width)
        partial_sum = jnp.swapaxes(partial_sum, 1, 2)
        kept = lax.dynamic_slice(
            kept,
            (lax.axis_index("req") * rows_out, lax.axis_index("ctx") * slice_width),
            (rows_out, slice_width),
        )
    else:
        other = swap(partial_sum, "ctx", 1, n_ctx)
        own = own_down(hidden, w_down, partial_sum.shape, w_gate, w_up)
        partial_sum = (own + other.astype(jnp.float32)).astype(jnp.bfloat16)
        groups = [list(range(core, n_req * n_ctx, CORES)) for core in range(CORES)]
    partial_sum = partial_sum.reshape(-1, rows_out, slice_width)
    landed = lax.all_to_all(
        partial_sum,
        ("req", "ctx"),
        split_axis=0,
        concat_axis=0,
        axis_index_groups=groups,
        tiled=True,
    )
    return (kept + jnp.sum(landed.astype(jnp.float32), axis=0)).astype(jnp.bfloat16)


def solution(mesh):
    in_specs = (
        P("ctx", "req"),
        P("req", "ctx", None),
        P("req", "ctx", None),
        P("req"),
        P("ctx", None, None),
        P("ctx", "req"),
        P(),
        P(),
        P(),
        P("req", "ctx", None),
        P("req", "ctx", None),
        P("req", "ctx", None),
    )
    out_specs = P("req", "ctx")
    return jax.shard_map(local, mesh=mesh, in_specs=in_specs, out_specs=out_specs, check_vma=False)
```

```python
import functools

import jax
import jax.numpy as jnp
from jax import lax
from jax.experimental import pallas as pl
from jax.experimental.pallas import tpu as pltpu
from jax.sharding import PartitionSpec as P

SOFTMAX_SCALE = 192.0 ** (-0.5)
NEG_FILL = -1e30
NORM_EPS = 1e-06
CORES = 2
OVERLAP = 60
LANES = 128
LOG_ROWS = 16
MIB = 1 << 20
NT = (((1,), (1,)), ((), ()))
VMEM = pl.BlockSpec(memory_space=pltpu.VMEM)
HBM = pl.BlockSpec(memory_space=pltpu.HBM)


def swap(x, axis, step, size):
    return lax.ppermute(x, axis, [(i, i ^ step) for i in range(size)])


def stack_rows(blocks):
    if len(blocks) == 1:
        return blocks[0]
    if all(b.shape[0] % 16 == 0 for b in blocks):
        return jnp.concatenate(blocks, axis=0)
    return jnp.concatenate([b.astype(jnp.float32) for b in blocks], axis=0).astype(blocks[0].dtype)


def attend_kernel(n_blocks, q_tokens, width, lengths, *refs):
    queries, caches, outs = refs[:n_blocks], refs[n_blocks : n_blocks + 2], refs[n_blocks + 2 :]
    req_local, rows, _ = queries[0].shape
    ctx_local = caches[0].shape[2]
    total_rows = n_blocks * rows
    heads_local = rows // q_tokens
    row = lax.broadcasted_iota(jnp.int32, (total_rows, ctx_local), 0)
    column = lax.broadcasted_iota(jnp.int32, (total_rows, ctx_local), 1)
    token = (row // heads_local) % q_tokens
    means, log_rows = [], [jnp.zeros((1, LANES), jnp.float32)] * n_blocks
    for r in range(req_local):
        grouped = stack_rows([q[r] for q in queries])
        limit = lengths[:, r : r + 1] - q_tokens + token
        masked = []
        for half, cache in enumerate(caches):
            score = jnp.dot(grouped, cache[r], preferred_element_type=jnp.float32)
            visible = column + (lax.axis_index("ctx") ^ half) * ctx_local <= limit
            masked.append(jnp.where(visible, score * SOFTMAX_SCALE, -jnp.inf))
        peak = jnp.maximum(
            jnp.max(masked[0], axis=-1, keepdims=True), jnp.max(masked[1], axis=-1, keepdims=True)
        )
        peak = jnp.where(peak > -jnp.inf, peak, 0.0)
        total = jnp.zeros((total_rows, 1), jnp.float32)
        mixed = jnp.zeros((total_rows, width), jnp.float32)
        for scores, cache in zip(masked, caches):
            raised = jnp.exp(scores - peak)
            total += jnp.sum(raised, axis=-1, keepdims=True)
            mixed += lax.dot_general(
                raised.astype(jnp.bfloat16),
                cache[r, :width, :],
                NT,
                preferred_element_type=jnp.float32,
            )
        filled = total > 0.0
        safe = jnp.where(filled, total, 1.0)
        mean = jnp.where(filled, mixed / safe, 0.0).astype(jnp.bfloat16)
        log = jnp.where(filled, peak + jnp.log(safe), NEG_FILL)
        high = log.astype(jnp.bfloat16).astype(jnp.float32)
        means.append(mean)
        for s in range(n_blocks):
            block = slice(s * rows, (s + 1) * rows)
            logs = log_lanes(
                lambda where_high, where_low: jnp.where(
                    where_high, high[block], jnp.where(where_low, (log - high)[block], 0.0)
                ),
                rows,
                r * rows,
            )
            log_rows[s] += jnp.sum(logs, axis=0, keepdims=True)
    packed = req_local * rows
    for s, (row, out) in enumerate(zip(log_rows, outs)):
        for i in range(width // LANES):
            columns = slice(i * LANES, (i + 1) * LANES)
            out[i * packed : (i + 1) * packed] = stack_rows(
                [mean[s * rows : (s + 1) * rows, columns] for mean in means]
            )
        spread = jnp.broadcast_to(row, (LOG_ROWS, LANES))
        out[out.shape[0] - LOG_ROWS :] = spread.astype(jnp.bfloat16)


def log_lanes(pick, rows, start):
    row = start + lax.broadcasted_iota(jnp.int32, (rows, LANES), 0)
    lane = lax.broadcasted_iota(jnp.int32, (rows, LANES), 1)
    return pick(lane == row, lane == row + LANES // 2)


def attend(blocks, caches, lengths, width, q_tokens):
    req_local, rows, lat = blocks[0].shape
    n = len(blocks)
    ctx_local = caches[0].shape[2]
    packed = req_local * rows * width // LANES + LOG_ROWS
    shape = jax.ShapeDtypeStruct((packed, LANES), jnp.bfloat16)
    return pl.pallas_call(
        functools.partial(attend_kernel, n, q_tokens, width),
        out_shape=[shape] * n,
        in_specs=[VMEM] * (n + 3),
        out_specs=[VMEM] * n,
        compiler_params=pltpu.CompilerParams(vmem_limit_bytes=4 * MIB),
        cost_estimate=pl.CostEstimate(
            flops=OVERLAP * 4 * req_local * n * rows * ctx_local * (lat + width),
            bytes_accessed=4 * req_local * ctx_local * lat,
            transcendentals=2 * req_local * n * rows * ctx_local,
        ),
        name="attend",
    )(lengths.reshape(1, -1), *blocks, *caches)


def stage_kernel(*refs):
    n = len(refs) // 2
    sems = refs[-1]
    copies = [
        pltpu.make_async_copy(source, target, sems.at[i])
        for i, (source, target) in enumerate(zip(refs[:n], refs[n : 2 * n]))
    ]
    for copy in copies:
        copy.start()
    for copy in copies:
        copy.wait()


def stage(arrays):
    return pl.pallas_call(
        stage_kernel,
        out_shape=[pltpu.VMEM(x.shape, x.dtype) for x in arrays],
        in_specs=[HBM] * len(arrays),
        out_specs=[VMEM] * len(arrays),
        scratch_shapes=[pltpu.SemaphoreType.DMA((len(arrays),))],
        compiler_params=pltpu.CompilerParams(vmem_limit_bytes=4 * MIB),
        cost_estimate=pl.CostEstimate(
            flops=0, bytes_accessed=sum(x.size * 2 for x in arrays), transcendentals=0
        ),
        name="stage",
    )(*[pltpu.with_memory_space_constraint(x, pltpu.HBM) for x in arrays])


def combine_kernel(n_blocks, *refs):
    blocks, (w_uv, out) = refs[:n_blocks], refs[n_blocks:]
    heads, width, value_width = w_uv.shape
    total_rows = (blocks[0].shape[0] - LOG_ROWS) * LANES // width
    parts, logs = [], []
    for block in blocks:
        columns = [
            block[i * total_rows : (i + 1) * total_rows].astype(jnp.float32)
            for i in range(width // LANES)
        ]
        parts.append(jnp.concatenate(columns, axis=1))
        row = block[block.shape[0] - LOG_ROWS :].astype(jnp.float32)[:1]
        lanes = log_lanes(lambda high, low: jnp.where(high | low, row, 0.0), total_rows, 0)
        logs.append(jnp.sum(lanes, axis=1, keepdims=True))
    top = functools.reduce(jnp.maximum, logs)
    factors = [jnp.exp(log - top) for log in logs]
    numer = sum(f * p for f, p in zip(factors, parts))
    latent = (numer / sum(factors)).astype(jnp.bfloat16)
    head = lax.broadcasted_iota(jnp.int32, (total_rows, value_width), 0) % heads
    values = []
    for h in range(heads):
        value = jnp.dot(latent, w_uv[h], preferred_element_type=jnp.float32)
        values.append(jnp.where(head == h, value, 0.0).astype(jnp.bfloat16))
    values = jnp.concatenate(values, axis=1)
    tokens = total_rows // heads
    token = lax.broadcasted_iota(jnp.int32, (tokens, total_rows), 0)
    at = lax.broadcasted_iota(jnp.int32, (tokens, total_rows), 1)
    fold = jnp.where(at // heads == token, 1.0, 0.0).astype(jnp.bfloat16)
    out[...] = jnp.dot(fold, values, preferred_element_type=jnp.float32).astype(out.dtype)


def combine(blocks, w_uv):
    heads, width, value_width = w_uv.shape
    rows = (blocks[0].shape[0] - LOG_ROWS) * LANES // width
    tokens = rows // heads
    return pl.pallas_call(
        functools.partial(combine_kernel, len(blocks)),
        out_shape=jax.ShapeDtypeStruct((tokens, heads * value_width), jnp.bfloat16),
        in_specs=[VMEM] * (len(blocks) + 1),
        out_specs=VMEM,
        compiler_params=pltpu.CompilerParams(vmem_limit_bytes=4 * MIB),
        cost_estimate=pl.CostEstimate(
            flops=2 * rows * w_uv.size, bytes_accessed=2 * w_uv.size, transcendentals=0
        ),
        name="combine",
    )(*blocks, w_uv)


def one_hot(shape, target):
    at = lax.broadcasted_iota(jnp.int32, shape, 1)
    return jnp.where(at == target(lax.broadcasted_iota(jnp.int32, shape, 0)), 1.0, 0.0).astype(
        jnp.bfloat16
    )


def out_proj_kernel(n_blocks, *refs):
    blocks, (w_o, residual, out) = refs[:n_blocks], refs[n_blocks:]
    blocks = blocks[:1] + blocks[:0:-1]
    per = blocks[0].shape[0]
    tokens = n_blocks * per
    stacked = stack_rows([b[...] for b in blocks])
    at_ctx, at_req = lax.axis_index("ctx"), lax.axis_index("req")
    order = one_hot((tokens, tokens), lambda row: (row // per ^ at_req) * per + row % per)
    ordered = jnp.dot(order, stacked, preferred_element_type=jnp.float32).astype(jnp.bfloat16)
    total = jnp.dot(ordered, w_o[...], preferred_element_type=jnp.float32)
    own = residual.shape[0]
    row = lax.broadcasted_iota(jnp.int32, total.shape, 0) - at_ctx * own
    rows = residual[...].astype(jnp.float32)
    for i in range(own):
        total += jnp.where(row == i, rows[i : i + 1], 0.0)
    out[...] = total.astype(out.dtype)


def out_proj(blocks, w_o, residual):
    n = len(blocks)
    tokens = n * blocks[0].shape[0]
    return pl.pallas_call(
        functools.partial(out_proj_kernel, n),
        out_shape=jax.ShapeDtypeStruct((tokens, w_o.shape[1]), jnp.bfloat16),
        in_specs=[VMEM] * (n + 2),
        out_specs=VMEM,
        compiler_params=pltpu.CompilerParams(vmem_limit_bytes=4 * MIB),
        cost_estimate=pl.CostEstimate(
            flops=2 * tokens * w_o.size, bytes_accessed=2 * w_o.size, transcendentals=0
        ),
        name="out_proj",
    )(*blocks, w_o, residual)


def add_products(totals, steps, blocks, gain, matrices):
    n_exp = matrices[0].shape[0]
    width = blocks[0].shape[1]
    for step, block in zip(steps, blocks):
        columns = pl.ds(0, width)
        if width < matrices[0].shape[2]:
            columns = pl.ds(pl.multiple_of((lax.axis_index("req") ^ step) * width, LANES), width)
        rows = block[...].astype(jnp.float32) * gain[:, columns].astype(jnp.float32)
        rows = rows.astype(jnp.bfloat16)
        for m, weights in enumerate(matrices):
            for e in range(n_exp):
                product = lax.dot_general(
                    weights[e, :, columns], rows, NT, preferred_element_type=jnp.float32
                )
                at = m * n_exp + e
                totals[at] = product if totals[at] is None else totals[at] + product
    return totals


def part_kernel(step, picks, n_weights, block, gain, *refs):
    weights, out, handed = refs[:n_weights], refs[n_weights], refs[n_weights + 1 :]
    matrices = [weights[i] for i in picks]
    totals = add_products([None] * out.shape[0], [step], [block], gain, matrices)
    for at, total in enumerate(totals):
        out[at] = total
    for copy in handed:
        copy[...] = block[...]


def part(step, picks, block, gain, weights, hand=False):
    n_exp, units, _ = weights[0].shape
    tokens, width = block.shape
    n = len(picks) * n_exp
    return pl.pallas_call(
        functools.partial(part_kernel, step, picks, len(weights)),
        out_shape=[pltpu.VMEM((n, units, tokens), jnp.float32)]
        + [pltpu.VMEM(block.shape, block.dtype)] * hand,
        in_specs=[VMEM] * (2 + len(weights)),
        out_specs=[VMEM] * (1 + hand),
        compiler_params=pltpu.CompilerParams(vmem_limit_bytes=4 * MIB),
        cost_estimate=pl.CostEstimate(
            flops=2 * tokens * n * units * width,
            bytes_accessed=2 * n * units * width,
            transcendentals=0,
        ),
        name="part",
    )(block, gain, *weights)


def experts_kernel(order, n_parts, *refs):
    n_blocks = len(order)
    blocks, refs = refs[:n_blocks], refs[n_blocks:]
    parts, refs = refs[:n_parts], refs[n_parts:]
    gain, routes, weights, gate, up, down, out, kept, hidden, rows = refs
    at_ctx, at_req = lax.axis_index("ctx"), lax.axis_index("req")
    n_exp, units, model = gate.shape
    tokens = rows.shape[0]
    width = blocks[0].shape[1]
    totals = [None] * (2 * n_exp)
    if parts:
        own_gate, own_up, first = parts
        totals = [own[e] for own in (own_gate, own_up) for e in range(n_exp)]
        totals = [total + first[at] for at, total in enumerate(totals)]
    rest = 2 if parts else 0
    totals = add_products(totals, order[rest:], blocks[rest:], gain, (gate, up))
    totals = [t.T for t in totals]
    for s, block in zip(order, blocks):
        if n_blocks == 1:
            rows[...] = block[...]
        else:
            offset = pl.multiple_of((at_req ^ s) * width, LANES)
            rows[:, pl.ds(offset, width)] = block[...]
    squares = sum(
        jnp.sum(jnp.square(b[...].astype(jnp.float32)), axis=-1, keepdims=True) for b in blocks
    )
    scale = lax.rsqrt(squares / model + NORM_EPS)
    eye = lax.broadcasted_iota(jnp.int32, (tokens, tokens), 0) == lax.broadcasted_iota(
        jnp.int32, (tokens, tokens), 1
    )
    for e in range(n_exp):
        named = jnp.where(routes[...] == at_req * n_exp + e, weights[...], 0.0)
        coef = jnp.sum(named, axis=0, keepdims=True)
        coef = jnp.sum(jnp.where(eye, coef, 0.0), axis=1, keepdims=True)
        active = jax.nn.silu(totals[e] * scale) * (totals[n_exp + e] * scale) * coef
        hidden[:, e * units : (e + 1) * units] = active.astype(jnp.bfloat16)
    sliced = len(out.shape) == 4
    if sliced:
        per, chunk = out.shape[2:]
        columns = pl.ds(pl.multiple_of(at_ctx * chunk, LANES), chunk)
        own = one_hot((per, tokens), lambda row: row + at_req * per)
        kept[...] = jnp.dot(own, rows[:, columns], preferred_element_type=jnp.float32)
        down_products(out, hidden, down, 1 - at_ctx % CORES)
    else:
        chunk = model // 8
        kept[...] = rows[...].astype(jnp.float32)
        for j in range(8):
            columns = slice(j * chunk, (j + 1) * chunk)
            part_down = down[:, :, columns].reshape(n_exp * units, chunk)
            total = jnp.dot(hidden[...], part_down, preferred_element_type=jnp.float32)
            out[:, columns] = total.astype(out.dtype)


def down_products(out, hidden, down, core):
    n_exp, units, _ = down.shape
    n_req, n_chips, per, chunk = out.shape
    for p in range(n_chips):
        columns = pl.ds(pl.multiple_of((p * CORES + core) * chunk, LANES), chunk)
        part_down = down[:, :, columns].reshape(n_exp * units, chunk)
        total = jnp.dot(hidden[...], part_down, preferred_element_type=jnp.float32)
        total = total.astype(out.dtype)
        for q in range(n_req):
            out[q, p] = total[q * per : (q + 1) * per]


def own_down_kernel(hidden, down, *refs):
    out = refs[-1]
    down_products(out, hidden, down, lax.axis_index("ctx") % CORES)


def own_down(hidden, w_down, shape, *held):
    weights = [pltpu.with_memory_space_constraint(w, pltpu.VMEM) for w in (w_down, *held)]
    return pl.pallas_call(
        own_down_kernel,
        out_shape=jax.ShapeDtypeStruct(shape, jnp.float32),
        in_specs=[VMEM] * (1 + len(weights)),
        out_specs=VMEM,
        compiler_params=pltpu.CompilerParams(vmem_limit_bytes=4 * MIB),
        cost_estimate=pl.CostEstimate(
            flops=hidden.shape[0] * w_down.size, bytes_accessed=w_down.size, transcendentals=0
        ),
        name="own_down",
    )(hidden, *weights)


def experts(mid, gain, routes, route_weight, w_gate, w_up, w_down, n_req, n_ctx):
    n_exp, units, model = w_gate.shape
    tokens = mid.shape[0]
    slice_width = model // n_ctx
    aligned = slice_width % LANES == 0
    weights = [pltpu.with_memory_space_constraint(w, pltpu.VMEM) for w in (w_gate, w_up, w_down)]
    parts = []
    if mid.shape[1] % LANES:
        order, blocks = [0], [lax.all_gather(mid, "req", axis=1, tiled=True)]
    elif n_req < 4:
        order = list(range(n_req))
        blocks = [mid] + [swap(mid, "req", s, n_req) for s in order[1:]]
    else:
        first = swap(mid, "req", 1, n_req)
        own_gate, handed = part(0, [0], mid, gain, weights, hand=True)
        far = [swap(handed, "req", s, n_req) for s in range(n_req - 1, 1, -1)]
        (own_up,) = part(0, [1], mid, gain, weights)
        (first_products,) = part(1, [0, 1], first, gain, weights)
        parts = [own_gate, own_up, first_products]
        order, blocks = [0, 1, *range(n_req - 1, 1, -1)], [mid, first, *far]
    shape = (n_req, n_ctx // CORES, tokens // n_req, slice_width) if aligned else (tokens, model)
    kept = (tokens // n_req, slice_width) if aligned else (tokens, model)
    return pl.pallas_call(
        functools.partial(experts_kernel, order, len(parts)),
        out_shape=[
            jax.ShapeDtypeStruct(shape, jnp.bfloat16),
            jax.ShapeDtypeStruct(kept, jnp.float32),
            jax.ShapeDtypeStruct((tokens, n_exp * units), jnp.bfloat16),
        ],
        in_specs=[VMEM] * (len(blocks) + len(parts) + 6),
        out_specs=[VMEM] * 3,
        scratch_shapes=[
            pltpu.VMEM((tokens, model), jnp.bfloat16),
        ],
        compiler_params=pltpu.CompilerParams(vmem_limit_bytes=4 * MIB),
        cost_estimate=pl.CostEstimate(
            flops=6 * tokens * w_gate.size,
            bytes_accessed=6 * w_gate.size,
            transcendentals=n_exp * units * tokens,
        ),
        name="experts",
    )(*blocks, *parts, gain, routes, route_weight, *weights)


def local(
    residual,
    query,
    latent_cache,
    lengths,
    w_uv,
    w_o,
    norm_gain,
    routes,
    route_weight,
    w_gate,
    w_up,
    w_down,
):
    n_ctx = lax.axis_size("ctx")
    n_req = lax.axis_size("req")
    chip_steps = list(range(CORES, n_ctx, CORES))[::-1]
    req_steps = range(1, n_req)
    req_local = latent_cache.shape[0]
    heads_local, lat_width, _ = w_uv.shape
    tok_local = query.shape[0]
    q_tokens = tok_local // req_local

    cache = jnp.swapaxes(latent_cache, 1, 2)
    other_cache = swap(cache, "ctx", 1, n_ctx)
    query = query.reshape(req_local, q_tokens * heads_local, query.shape[2])
    received = [swap(query, "ctx", s, n_ctx) for s in chip_steps]
    cache, query, w_uv, w_o = stage([cache, query, w_uv, w_o])
    blocks = [query] + received
    outs = attend(blocks, (cache, other_cache), lengths, lat_width, q_tokens)
    outs = [outs[0]] + [swap(o, "ctx", s, n_ctx) for o, s in zip(outs[1:], chip_steps)]

    head_values = combine(outs, w_uv)
    blocks = [head_values] + [swap(head_values, "req", s, n_req) for s in reversed(req_steps)]
    partial_mid = out_proj(blocks, w_o, residual)

    other = swap(partial_mid, "ctx", 1, n_ctx)
    chip_mid = (partial_mid.astype(jnp.float32) + other.astype(jnp.float32)).astype(jnp.bfloat16)
    pieces = [chip_mid] + [swap(chip_mid, "ctx", s, n_ctx) for s in chip_steps]
    mid = sum(p.astype(jnp.float32) for p in pieces).astype(jnp.bfloat16)
    partial_sum, kept, hidden = experts(
        mid,
        norm_gain.reshape(1, -1),
        routes.T,
        route_weight.T,
        w_gate,
        w_up,
        w_down,
        n_req,
        n_ctx,
    )
    tokens = mid.shape[0]
    model_width = w_gate.shape[2]
    rows_out = tokens // n_req
    slice_width = model_width // n_ctx
    groups = None
    if partial_sum.ndim == 2:
        partial_sum = partial_sum.reshape(n_req, rows_out, n_ctx, slice_width)
        partial_sum = jnp.swapaxes(partial_sum, 1, 2)
        kept = lax.dynamic_slice(
            kept,
            (lax.axis_index("req") * rows_out, lax.axis_index("ctx") * slice_width),
            (rows_out, slice_width),
        )
    else:
        other = swap(partial_sum, "ctx", 1, n_ctx)
        own = own_down(hidden, w_down, partial_sum.shape, w_gate, w_up)
        partial_sum = (own + other.astype(jnp.float32)).astype(jnp.bfloat16)
        groups = [list(range(core, n_req * n_ctx, CORES)) for core in range(CORES)]
    partial_sum = partial_sum.reshape(-1, rows_out, slice_width)
    landed = lax.all_to_all(
        partial_sum,
        ("req", "ctx"),
        split_axis=0,
        concat_axis=0,
        axis_index_groups=groups,
        tiled=True,
    )
    return (kept + jnp.sum(landed.astype(jnp.float32), axis=0)).astype(jnp.bfloat16)


def solution(mesh):
    in_specs = (
        P("ctx", "req"),
        P("req", "ctx", None),
        P("req", "ctx", None),
        P("req"),
        P("ctx", None, None),
        P("ctx", "req"),
        P(),
        P(),
        P(),
        P("req", "ctx", None),
        P("req", "ctx", None),
        P("req", "ctx", None),
    )
    out_specs = P("req", "ctx")
    return jax.shard_map(local, mesh=mesh, in_specs=in_specs, out_specs=out_specs, check_vma=False)
```

```python
import functools

import jax
import jax.numpy as jnp
from jax import lax
from jax.experimental import pallas as pl
from jax.experimental.pallas import tpu as pltpu
from jax.sharding import PartitionSpec as P

SOFTMAX_SCALE = 192.0 ** (-0.5)
NEG_FILL = -1e30
NORM_EPS = 1e-06
CORES = 2
OVERLAP = 60
LANES = 128
LOG_ROWS = 16
MIB = 1 << 20
NT = (((1,), (1,)), ((), ()))
VMEM = pl.BlockSpec(memory_space=pltpu.VMEM)
HBM = pl.BlockSpec(memory_space=pltpu.HBM)


def swap(x, axis, step, size):
    return lax.ppermute(x, axis, [(i, i ^ step) for i in range(size)])


def stack_rows(blocks):
    if len(blocks) == 1:
        return blocks[0]
    if all(b.shape[0] % 16 == 0 for b in blocks):
        return jnp.concatenate(blocks, axis=0)
    return jnp.concatenate([b.astype(jnp.float32) for b in blocks], axis=0).astype(blocks[0].dtype)


def attend_kernel(n_blocks, q_tokens, width, lengths, *refs):
    queries, caches, outs = refs[:n_blocks], refs[n_blocks : n_blocks + 2], refs[n_blocks + 2 :]
    req_local, rows, _ = queries[0].shape
    ctx_local = caches[0].shape[2]
    total_rows = n_blocks * rows
    heads_local = rows // q_tokens
    row = lax.broadcasted_iota(jnp.int32, (total_rows, ctx_local), 0)
    column = lax.broadcasted_iota(jnp.int32, (total_rows, ctx_local), 1)
    token = (row // heads_local) % q_tokens
    means, log_rows = [], [jnp.zeros((1, LANES), jnp.float32)] * n_blocks
    for r in range(req_local):
        grouped = stack_rows([q[r] for q in queries])
        limit = lengths[:, r : r + 1] - q_tokens + token
        masked = []
        for half, cache in enumerate(caches):
            score = jnp.dot(grouped, cache[r], preferred_element_type=jnp.float32)
            visible = column + (lax.axis_index("ctx") ^ half) * ctx_local <= limit
            masked.append(jnp.where(visible, score * SOFTMAX_SCALE, -jnp.inf))
        peak = jnp.maximum(
            jnp.max(masked[0], axis=-1, keepdims=True), jnp.max(masked[1], axis=-1, keepdims=True)
        )
        peak = jnp.where(peak > -jnp.inf, peak, 0.0)
        total = jnp.zeros((total_rows, 1), jnp.float32)
        mixed = jnp.zeros((total_rows, width), jnp.float32)
        for scores, cache in zip(masked, caches):
            raised = jnp.exp(scores - peak)
            total += jnp.sum(raised, axis=-1, keepdims=True)
            mixed += lax.dot_general(
                raised.astype(jnp.bfloat16),
                cache[r, :width, :],
                NT,
                preferred_element_type=jnp.float32,
            )
        filled = total > 0.0
        safe = jnp.where(filled, total, 1.0)
        mean = jnp.where(filled, mixed / safe, 0.0).astype(jnp.bfloat16)
        log = jnp.where(filled, peak + jnp.log(safe), NEG_FILL)
        high = log.astype(jnp.bfloat16).astype(jnp.float32)
        means.append(mean)
        for s in range(n_blocks):
            block = slice(s * rows, (s + 1) * rows)
            logs = log_lanes(
                lambda where_high, where_low: jnp.where(
                    where_high, high[block], jnp.where(where_low, (log - high)[block], 0.0)
                ),
                rows,
                r * rows,
            )
            log_rows[s] += jnp.sum(logs, axis=0, keepdims=True)
    packed = req_local * rows
    for s, (row, out) in enumerate(zip(log_rows, outs)):
        for i in range(width // LANES):
            columns = slice(i * LANES, (i + 1) * LANES)
            out[i * packed : (i + 1) * packed] = stack_rows(
                [mean[s * rows : (s + 1) * rows, columns] for mean in means]
            )
        spread = jnp.broadcast_to(row, (LOG_ROWS, LANES))
        out[out.shape[0] - LOG_ROWS :] = spread.astype(jnp.bfloat16)


def log_lanes(pick, rows, start):
    row = start + lax.broadcasted_iota(jnp.int32, (rows, LANES), 0)
    lane = lax.broadcasted_iota(jnp.int32, (rows, LANES), 1)
    return pick(lane == row, lane == row + LANES // 2)


def attend(blocks, caches, lengths, width, q_tokens):
    req_local, rows, lat = blocks[0].shape
    n = len(blocks)
    ctx_local = caches[0].shape[2]
    packed = req_local * rows * width // LANES + LOG_ROWS
    shape = jax.ShapeDtypeStruct((packed, LANES), jnp.bfloat16)
    return pl.pallas_call(
        functools.partial(attend_kernel, n, q_tokens, width),
        out_shape=[shape] * n,
        in_specs=[VMEM] * (n + 3),
        out_specs=[VMEM] * n,
        compiler_params=pltpu.CompilerParams(vmem_limit_bytes=4 * MIB),
        cost_estimate=pl.CostEstimate(
            flops=OVERLAP * 4 * req_local * n * rows * ctx_local * (lat + width),
            bytes_accessed=4 * req_local * ctx_local * lat,
            transcendentals=2 * req_local * n * rows * ctx_local,
        ),
        name="attend",
    )(lengths.reshape(1, -1), *blocks, *caches)


def stage_kernel(*refs):
    n = len(refs) // 2
    sems = refs[-1]
    copies = [
        pltpu.make_async_copy(source, target, sems.at[i])
        for i, (source, target) in enumerate(zip(refs[:n], refs[n : 2 * n]))
    ]
    for copy in copies:
        copy.start()
    for copy in copies:
        copy.wait()


def stage(arrays):
    return pl.pallas_call(
        stage_kernel,
        out_shape=[pltpu.VMEM(x.shape, x.dtype) for x in arrays],
        in_specs=[HBM] * len(arrays),
        out_specs=[VMEM] * len(arrays),
        scratch_shapes=[pltpu.SemaphoreType.DMA((len(arrays),))],
        compiler_params=pltpu.CompilerParams(vmem_limit_bytes=4 * MIB),
        cost_estimate=pl.CostEstimate(
            flops=0, bytes_accessed=sum(x.size * 2 for x in arrays), transcendentals=0
        ),
        name="stage",
    )(*[pltpu.with_memory_space_constraint(x, pltpu.HBM) for x in arrays])


def combine_kernel(n_blocks, *refs):
    blocks, (w_uv, out) = refs[:n_blocks], refs[n_blocks:]
    heads, width, value_width = w_uv.shape
    total_rows = (blocks[0].shape[0] - LOG_ROWS) * LANES // width
    parts, logs = [], []
    for block in blocks:
        columns = [
            block[i * total_rows : (i + 1) * total_rows].astype(jnp.float32)
            for i in range(width // LANES)
        ]
        parts.append(jnp.concatenate(columns, axis=1))
        row = block[block.shape[0] - LOG_ROWS :].astype(jnp.float32)[:1]
        lanes = log_lanes(lambda high, low: jnp.where(high | low, row, 0.0), total_rows, 0)
        logs.append(jnp.sum(lanes, axis=1, keepdims=True))
    top = functools.reduce(jnp.maximum, logs)
    factors = [jnp.exp(log - top) for log in logs]
    numer = sum(f * p for f, p in zip(factors, parts))
    latent = (numer / sum(factors)).astype(jnp.bfloat16)
    head = lax.broadcasted_iota(jnp.int32, (total_rows, value_width), 0) % heads
    values = []
    for h in range(heads):
        value = jnp.dot(latent, w_uv[h], preferred_element_type=jnp.float32)
        values.append(jnp.where(head == h, value, 0.0).astype(jnp.bfloat16))
    values = jnp.concatenate(values, axis=1)
    tokens = total_rows // heads
    token = lax.broadcasted_iota(jnp.int32, (tokens, total_rows), 0)
    at = lax.broadcasted_iota(jnp.int32, (tokens, total_rows), 1)
    fold = jnp.where(at // heads == token, 1.0, 0.0).astype(jnp.bfloat16)
    out[...] = jnp.dot(fold, values, preferred_element_type=jnp.float32).astype(out.dtype)


def combine(blocks, w_uv):
    heads, width, value_width = w_uv.shape
    rows = (blocks[0].shape[0] - LOG_ROWS) * LANES // width
    tokens = rows // heads
    return pl.pallas_call(
        functools.partial(combine_kernel, len(blocks)),
        out_shape=jax.ShapeDtypeStruct((tokens, heads * value_width), jnp.bfloat16),
        in_specs=[VMEM] * (len(blocks) + 1),
        out_specs=VMEM,
        compiler_params=pltpu.CompilerParams(vmem_limit_bytes=4 * MIB),
        cost_estimate=pl.CostEstimate(
            flops=2 * rows * w_uv.size, bytes_accessed=2 * w_uv.size, transcendentals=0
        ),
        name="combine",
    )(*blocks, w_uv)


def one_hot(shape, target):
    at = lax.broadcasted_iota(jnp.int32, shape, 1)
    return jnp.where(at == target(lax.broadcasted_iota(jnp.int32, shape, 0)), 1.0, 0.0).astype(
        jnp.bfloat16
    )


def out_proj_kernel(order, *refs):
    n_blocks = len(order)
    blocks, (w_o, residual, out) = refs[:n_blocks], refs[n_blocks:]
    blocks = [blocks[order.index(s)] for s in range(n_blocks)]
    per = blocks[0].shape[0]
    tokens = n_blocks * per
    stacked = stack_rows([b[...] for b in blocks])
    at_ctx, at_req = lax.axis_index("ctx"), lax.axis_index("req")
    order = one_hot((tokens, tokens), lambda row: (row // per ^ at_req) * per + row % per)
    ordered = jnp.dot(order, stacked, preferred_element_type=jnp.float32).astype(jnp.bfloat16)
    total = jnp.dot(ordered, w_o[...], preferred_element_type=jnp.float32)
    own = residual.shape[0]
    row = lax.broadcasted_iota(jnp.int32, total.shape, 0) - at_ctx * own
    rows = residual[...].astype(jnp.float32)
    for i in range(own):
        total += jnp.where(row == i, rows[i : i + 1], 0.0)
    out[...] = total.astype(out.dtype)


def out_proj(order, blocks, w_o, residual):
    n = len(blocks)
    tokens = n * blocks[0].shape[0]
    return pl.pallas_call(
        functools.partial(out_proj_kernel, order),
        out_shape=jax.ShapeDtypeStruct((tokens, w_o.shape[1]), jnp.bfloat16),
        in_specs=[VMEM] * (n + 2),
        out_specs=VMEM,
        compiler_params=pltpu.CompilerParams(vmem_limit_bytes=4 * MIB),
        cost_estimate=pl.CostEstimate(
            flops=2 * tokens * w_o.size, bytes_accessed=2 * w_o.size, transcendentals=0
        ),
        name="out_proj",
    )(*blocks, w_o, residual)


def add_products(totals, steps, blocks, gain, gate, up):
    n_exp = gate.shape[0]
    width = blocks[0].shape[1]
    for step, block in zip(steps, blocks):
        columns = pl.ds(0, width)
        if width < gate.shape[2]:
            columns = pl.ds(pl.multiple_of((lax.axis_index("req") ^ step) * width, LANES), width)
        rows = block[...].astype(jnp.float32) * gain[:, columns].astype(jnp.float32)
        rows = rows.astype(jnp.bfloat16)
        for m, weights in enumerate((gate, up)):
            for e in range(n_exp):
                product = lax.dot_general(
                    weights[e, :, columns], rows, NT, preferred_element_type=jnp.float32
                )
                at = m * n_exp + e
                totals[at] = product if totals[at] is None else totals[at] + product
    return totals


def part_kernel(steps, block, gain, gate, up, *refs):
    out = refs[-1]
    totals = add_products([None] * out.shape[0], steps, [block], gain, gate, up)
    for at, total in enumerate(totals):
        out[at] = total


def part(step, block, gain, w_gate, w_up, *held):
    n_exp, units, _ = w_gate.shape
    tokens, width = block.shape
    return pl.pallas_call(
        functools.partial(part_kernel, [step]),
        out_shape=pltpu.VMEM((2 * n_exp, units, tokens), jnp.float32),
        in_specs=[VMEM] * (4 + len(held)),
        out_specs=VMEM,
        compiler_params=pltpu.CompilerParams(vmem_limit_bytes=4 * MIB),
        cost_estimate=pl.CostEstimate(
            flops=4 * tokens * n_exp * units * width,
            bytes_accessed=4 * n_exp * units * width,
            transcendentals=0,
        ),
        name="part",
    )(block, gain, w_gate, w_up, *held)


def experts_kernel(order, n_parts, *refs):
    n_blocks = len(order)
    blocks, refs = refs[:n_blocks], refs[n_blocks:]
    parts, refs = refs[:n_parts], refs[n_parts:]
    gain, routes, weights, gate, up, down, out, kept, hidden, rows = refs
    at_ctx, at_req = lax.axis_index("ctx"), lax.axis_index("req")
    n_exp, units, model = gate.shape
    tokens = rows.shape[0]
    width = blocks[0].shape[1]
    totals = [None] * (2 * n_exp)
    for done in parts:
        totals = [done[at] if t is None else t + done[at] for at, t in enumerate(totals)]
    totals = add_products(totals, order[n_parts:], blocks[n_parts:], gain, gate, up)
    totals = [t.T for t in totals]
    for s, block in zip(order, blocks):
        if n_blocks == 1:
            rows[...] = block[...]
        else:
            offset = pl.multiple_of((at_req ^ s) * width, LANES)
            rows[:, pl.ds(offset, width)] = block[...]
    squares = sum(
        jnp.sum(jnp.square(b[...].astype(jnp.float32)), axis=-1, keepdims=True) for b in blocks
    )
    scale = lax.rsqrt(squares / model + NORM_EPS)
    eye = lax.broadcasted_iota(jnp.int32, (tokens, tokens), 0) == lax.broadcasted_iota(
        jnp.int32, (tokens, tokens), 1
    )
    for e in range(n_exp):
        named = jnp.where(routes[...] == at_req * n_exp + e, weights[...], 0.0)
        coef = jnp.sum(named, axis=0, keepdims=True)
        coef = jnp.sum(jnp.where(eye, coef, 0.0), axis=1, keepdims=True)
        active = jax.nn.silu(totals[e] * scale) * (totals[n_exp + e] * scale) * coef
        hidden[:, e * units : (e + 1) * units] = active.astype(jnp.bfloat16)
    sliced = len(out.shape) == 4
    if sliced:
        per, chunk = out.shape[2:]
        columns = pl.ds(pl.multiple_of(at_ctx * chunk, LANES), chunk)
        own = one_hot((per, tokens), lambda row: row + at_req * per)
        kept[...] = jnp.dot(own, rows[:, columns], preferred_element_type=jnp.float32)
        down_products(out, hidden, down, 1 - at_ctx % CORES)
    else:
        chunk = model // 8
        kept[...] = rows[...].astype(jnp.float32)
        for j in range(8):
            columns = slice(j * chunk, (j + 1) * chunk)
            part_down = down[:, :, columns].reshape(n_exp * units, chunk)
            total = jnp.dot(hidden[...], part_down, preferred_element_type=jnp.float32)
            out[:, columns] = total.astype(out.dtype)


def down_products(out, hidden, down, core):
    n_exp, units, _ = down.shape
    n_req, n_chips, per, chunk = out.shape
    for p in range(n_chips):
        columns = pl.ds(pl.multiple_of((p * CORES + core) * chunk, LANES), chunk)
        part_down = down[:, :, columns].reshape(n_exp * units, chunk)
        total = jnp.dot(hidden[...], part_down, preferred_element_type=jnp.float32)
        total = total.astype(out.dtype)
        for q in range(n_req):
            out[q, p] = total[q * per : (q + 1) * per]


def own_down_kernel(hidden, down, *refs):
    out = refs[-1]
    down_products(out, hidden, down, lax.axis_index("ctx") % CORES)


def own_down(hidden, w_down, shape, *held):
    weights = [pltpu.with_memory_space_constraint(w, pltpu.VMEM) for w in (w_down, *held)]
    return pl.pallas_call(
        own_down_kernel,
        out_shape=jax.ShapeDtypeStruct(shape, jnp.float32),
        in_specs=[VMEM] * (1 + len(weights)),
        out_specs=VMEM,
        compiler_params=pltpu.CompilerParams(vmem_limit_bytes=4 * MIB),
        cost_estimate=pl.CostEstimate(
            flops=hidden.shape[0] * w_down.size, bytes_accessed=w_down.size, transcendentals=0
        ),
        name="own_down",
    )(hidden, *weights)


def experts(order, blocks, gain, routes, route_weight, w_gate, w_up, w_down, n_req, n_ctx):
    n_exp, units, model = w_gate.shape
    tokens = blocks[0].shape[0]
    slice_width = model // n_ctx
    aligned = slice_width % LANES == 0
    w_gate, w_up, w_down = [
        pltpu.with_memory_space_constraint(w, pltpu.VMEM) for w in (w_gate, w_up, w_down)
    ]
    parts = []
    if len(blocks) > 2:
        parts = [part(order[i], blocks[i], gain, w_gate, w_up, w_down) for i in range(2)]
    shape = (n_req, n_ctx // CORES, tokens // n_req, slice_width) if aligned else (tokens, model)
    kept = (tokens // n_req, slice_width) if aligned else (tokens, model)
    return pl.pallas_call(
        functools.partial(experts_kernel, order, len(parts)),
        out_shape=[
            jax.ShapeDtypeStruct(shape, jnp.bfloat16),
            jax.ShapeDtypeStruct(kept, jnp.float32),
            jax.ShapeDtypeStruct((tokens, n_exp * units), jnp.bfloat16),
        ],
        in_specs=[VMEM] * (len(blocks) + len(parts) + 6),
        out_specs=[VMEM] * 3,
        scratch_shapes=[
            pltpu.VMEM((tokens, model), jnp.bfloat16),
        ],
        compiler_params=pltpu.CompilerParams(vmem_limit_bytes=4 * MIB),
        cost_estimate=pl.CostEstimate(
            flops=6 * tokens * w_gate.size,
            bytes_accessed=6 * w_gate.size,
            transcendentals=n_exp * units * tokens,
        ),
        name="experts",
    )(*blocks, *parts, gain, routes, route_weight, w_gate, w_up, w_down)


def local(
    residual,
    query,
    latent_cache,
    lengths,
    w_uv,
    w_o,
    norm_gain,
    routes,
    route_weight,
    w_gate,
    w_up,
    w_down,
):
    n_ctx = lax.axis_size("ctx")
    n_req = lax.axis_size("req")
    chip_steps = list(range(CORES, n_ctx, CORES))[::-1]
    order = [0] + sorted(range(1, n_req), key=lambda s: (s != n_req // 2, -s))
    req_local = latent_cache.shape[0]
    heads_local, lat_width, _ = w_uv.shape
    tok_local = query.shape[0]
    q_tokens = tok_local // req_local

    cache = jnp.swapaxes(latent_cache, 1, 2)
    other_cache = swap(cache, "ctx", 1, n_ctx)
    query = query.reshape(req_local, q_tokens * heads_local, query.shape[2])
    received = [swap(query, "ctx", s, n_ctx) for s in chip_steps]
    cache, query, w_uv, w_o = stage([cache, query, w_uv, w_o])
    blocks = [query] + received
    outs = attend(blocks, (cache, other_cache), lengths, lat_width, q_tokens)
    outs = [outs[0]] + [swap(o, "ctx", s, n_ctx) for o, s in zip(outs[1:], chip_steps)]

    head_values = combine(outs, w_uv)
    blocks = [head_values] + [swap(head_values, "req", s, n_req) for s in order[1:]]
    partial_mid = out_proj(order, blocks, w_o, residual)

    other = swap(partial_mid, "ctx", 1, n_ctx)
    chip_mid = (partial_mid.astype(jnp.float32) + other.astype(jnp.float32)).astype(jnp.bfloat16)
    pieces = [chip_mid] + [swap(chip_mid, "ctx", s, n_ctx) for s in chip_steps]
    mid = sum(p.astype(jnp.float32) for p in pieces).astype(jnp.bfloat16)
    if mid.shape[1] % LANES == 0:
        blocks = [mid] + [swap(mid, "req", s, n_req) for s in order[1:]]
    else:
        order = [0]
        blocks = [lax.all_gather(mid, "req", axis=1, tiled=True)]

    partial_sum, kept, hidden = experts(
        order,
        blocks,
        norm_gain.reshape(1, -1),
        routes.T,
        route_weight.T,
        w_gate,
        w_up,
        w_down,
        n_req,
        n_ctx,
    )
    tokens = mid.shape[0]
    model_width = w_gate.shape[2]
    rows_out = tokens // n_req
    slice_width = model_width // n_ctx
    groups = None
    if partial_sum.ndim == 2:
        partial_sum = partial_sum.reshape(n_req, rows_out, n_ctx, slice_width)
        partial_sum = jnp.swapaxes(partial_sum, 1, 2)
        kept = lax.dynamic_slice(
            kept,
            (lax.axis_index("req") * rows_out, lax.axis_index("ctx") * slice_width),
            (rows_out, slice_width),
        )
    else:
        other = swap(partial_sum, "ctx", 1, n_ctx)
        own = own_down(hidden, w_down, partial_sum.shape, w_gate, w_up)
        partial_sum = (own + other.astype(jnp.float32)).astype(jnp.bfloat16)
        groups = [list(range(core, n_req * n_ctx, CORES)) for core in range(CORES)]
    partial_sum = partial_sum.reshape(-1, rows_out, slice_width)
    landed = lax.all_to_all(
        partial_sum,
        ("req", "ctx"),
        split_axis=0,
        concat_axis=0,
        axis_index_groups=groups,
        tiled=True,
    )
    return (kept + jnp.sum(landed.astype(jnp.float32), axis=0)).astype(jnp.bfloat16)


def solution(mesh):
    in_specs = (
        P("ctx", "req"),
        P("req", "ctx", None),
        P("req", "ctx", None),
        P("req"),
        P("ctx", None, None),
        P("ctx", "req"),
        P(),
        P(),
        P(),
        P("req", "ctx", None),
        P("req", "ctx", None),
        P("req", "ctx", None),
    )
    out_specs = P("req", "ctx")
    return jax.shard_map(local, mesh=mesh, in_specs=in_specs, out_specs=out_specs, check_vma=False)
```

```python
import functools

import jax
import jax.numpy as jnp
from jax import lax
from jax.experimental import pallas as pl
from jax.experimental.pallas import tpu as pltpu
from jax.sharding import PartitionSpec as P

SOFTMAX_SCALE = 192.0 ** (-0.5)
NEG_FILL = -1e30
NORM_EPS = 1e-06
CORES = 2
OVERLAP = 60
LANES = 128
LOG_ROWS = 16
MIB = 1 << 20
NT = (((1,), (1,)), ((), ()))
VMEM = pl.BlockSpec(memory_space=pltpu.VMEM)
HBM = pl.BlockSpec(memory_space=pltpu.HBM)


def swap(x, axis, step, size):
    return lax.ppermute(x, axis, [(i, i ^ step) for i in range(size)])


def stack_rows(blocks):
    if len(blocks) == 1:
        return blocks[0]
    if all(b.shape[0] % 16 == 0 for b in blocks):
        return jnp.concatenate(blocks, axis=0)
    return jnp.concatenate([b.astype(jnp.float32) for b in blocks], axis=0).astype(blocks[0].dtype)


def attend_kernel(n_blocks, q_tokens, width, lengths, *refs):
    queries, caches, outs = refs[:n_blocks], refs[n_blocks : n_blocks + 2], refs[n_blocks + 2 :]
    req_local, rows, _ = queries[0].shape
    ctx_local = caches[0].shape[2]
    total_rows = n_blocks * rows
    heads_local = rows // q_tokens
    row = lax.broadcasted_iota(jnp.int32, (total_rows, ctx_local), 0)
    column = lax.broadcasted_iota(jnp.int32, (total_rows, ctx_local), 1)
    token = (row // heads_local) % q_tokens
    means, log_rows = [], [jnp.zeros((1, LANES), jnp.float32)] * n_blocks
    for r in range(req_local):
        grouped = stack_rows([q[r] for q in queries])
        limit = lengths[:, r : r + 1] - q_tokens + token
        masked = []
        for half, cache in enumerate(caches):
            score = jnp.dot(grouped, cache[r], preferred_element_type=jnp.float32)
            visible = column + (lax.axis_index("ctx") ^ half) * ctx_local <= limit
            masked.append(jnp.where(visible, score * SOFTMAX_SCALE, -jnp.inf))
        peak = jnp.maximum(
            jnp.max(masked[0], axis=-1, keepdims=True), jnp.max(masked[1], axis=-1, keepdims=True)
        )
        peak = jnp.where(peak > -jnp.inf, peak, 0.0)
        total = jnp.zeros((total_rows, 1), jnp.float32)
        mixed = jnp.zeros((total_rows, width), jnp.float32)
        for scores, cache in zip(masked, caches):
            raised = jnp.exp(scores - peak)
            total += jnp.sum(raised, axis=-1, keepdims=True)
            mixed += lax.dot_general(
                raised.astype(jnp.bfloat16),
                cache[r, :width, :],
                NT,
                preferred_element_type=jnp.float32,
            )
        filled = total > 0.0
        safe = jnp.where(filled, total, 1.0)
        mean = jnp.where(filled, mixed / safe, 0.0).astype(jnp.bfloat16)
        log = jnp.where(filled, peak + jnp.log(safe), NEG_FILL)
        high = log.astype(jnp.bfloat16).astype(jnp.float32)
        means.append(mean)
        for s in range(n_blocks):
            block = slice(s * rows, (s + 1) * rows)
            logs = log_lanes(
                lambda where_high, where_low: jnp.where(
                    where_high, high[block], jnp.where(where_low, (log - high)[block], 0.0)
                ),
                rows,
                r * rows,
            )
            log_rows[s] += jnp.sum(logs, axis=0, keepdims=True)
    packed = req_local * rows
    for s, (row, out) in enumerate(zip(log_rows, outs)):
        for i in range(width // LANES):
            columns = slice(i * LANES, (i + 1) * LANES)
            out[i * packed : (i + 1) * packed] = stack_rows(
                [mean[s * rows : (s + 1) * rows, columns] for mean in means]
            )
        spread = jnp.broadcast_to(row, (LOG_ROWS, LANES))
        out[out.shape[0] - LOG_ROWS :] = spread.astype(jnp.bfloat16)


def log_lanes(pick, rows, start):
    row = start + lax.broadcasted_iota(jnp.int32, (rows, LANES), 0)
    lane = lax.broadcasted_iota(jnp.int32, (rows, LANES), 1)
    return pick(lane == row, lane == row + LANES // 2)


def attend(blocks, caches, lengths, width, q_tokens):
    req_local, rows, lat = blocks[0].shape
    n = len(blocks)
    ctx_local = caches[0].shape[2]
    packed = req_local * rows * width // LANES + LOG_ROWS
    shape = jax.ShapeDtypeStruct((packed, LANES), jnp.bfloat16)
    return pl.pallas_call(
        functools.partial(attend_kernel, n, q_tokens, width),
        out_shape=[shape] * n,
        in_specs=[VMEM] * (n + 3),
        out_specs=[VMEM] * n,
        compiler_params=pltpu.CompilerParams(vmem_limit_bytes=4 * MIB),
        cost_estimate=pl.CostEstimate(
            flops=OVERLAP * 4 * req_local * n * rows * ctx_local * (lat + width),
            bytes_accessed=4 * req_local * ctx_local * lat,
            transcendentals=2 * req_local * n * rows * ctx_local,
        ),
        name="attend",
    )(lengths.reshape(1, -1), *blocks, *caches)


def stage_kernel(*refs):
    n = len(refs) // 2
    sems = refs[-1]
    copies = [
        pltpu.make_async_copy(source, target, sems.at[i])
        for i, (source, target) in enumerate(zip(refs[:n], refs[n : 2 * n]))
    ]
    for copy in copies:
        copy.start()
    for copy in copies:
        copy.wait()


def stage(arrays):
    return pl.pallas_call(
        stage_kernel,
        out_shape=[pltpu.VMEM(x.shape, x.dtype) for x in arrays],
        in_specs=[HBM] * len(arrays),
        out_specs=[VMEM] * len(arrays),
        scratch_shapes=[pltpu.SemaphoreType.DMA((len(arrays),))],
        compiler_params=pltpu.CompilerParams(vmem_limit_bytes=4 * MIB),
        cost_estimate=pl.CostEstimate(
            flops=0, bytes_accessed=sum(x.size * 2 for x in arrays), transcendentals=0
        ),
        name="stage",
    )(*[pltpu.with_memory_space_constraint(x, pltpu.HBM) for x in arrays])


def combine_kernel(n_blocks, *refs):
    blocks, (w_uv, out) = refs[:n_blocks], refs[n_blocks:]
    heads, width, value_width = w_uv.shape
    total_rows = (blocks[0].shape[0] - LOG_ROWS) * LANES // width
    parts, logs = [], []
    for block in blocks:
        columns = [
            block[i * total_rows : (i + 1) * total_rows].astype(jnp.float32)
            for i in range(width // LANES)
        ]
        parts.append(jnp.concatenate(columns, axis=1))
        row = block[block.shape[0] - LOG_ROWS :].astype(jnp.float32)[:1]
        lanes = log_lanes(lambda high, low: jnp.where(high | low, row, 0.0), total_rows, 0)
        logs.append(jnp.sum(lanes, axis=1, keepdims=True))
    top = functools.reduce(jnp.maximum, logs)
    factors = [jnp.exp(log - top) for log in logs]
    numer = sum(f * p for f, p in zip(factors, parts))
    latent = (numer / sum(factors)).astype(jnp.bfloat16)
    head = lax.broadcasted_iota(jnp.int32, (total_rows, value_width), 0) % heads
    values = []
    for h in range(heads):
        value = jnp.dot(latent, w_uv[h], preferred_element_type=jnp.float32)
        values.append(jnp.where(head == h, value, 0.0).astype(jnp.bfloat16))
    values = jnp.concatenate(values, axis=1)
    tokens = total_rows // heads
    token = lax.broadcasted_iota(jnp.int32, (tokens, total_rows), 0)
    at = lax.broadcasted_iota(jnp.int32, (tokens, total_rows), 1)
    fold = jnp.where(at // heads == token, 1.0, 0.0).astype(jnp.bfloat16)
    out[...] = jnp.dot(fold, values, preferred_element_type=jnp.float32).astype(out.dtype)


def combine(blocks, w_uv):
    heads, width, value_width = w_uv.shape
    rows = (blocks[0].shape[0] - LOG_ROWS) * LANES // width
    tokens = rows // heads
    return pl.pallas_call(
        functools.partial(combine_kernel, len(blocks)),
        out_shape=jax.ShapeDtypeStruct((tokens, heads * value_width), jnp.bfloat16),
        in_specs=[VMEM] * (len(blocks) + 1),
        out_specs=VMEM,
        compiler_params=pltpu.CompilerParams(vmem_limit_bytes=4 * MIB),
        cost_estimate=pl.CostEstimate(
            flops=2 * rows * w_uv.size, bytes_accessed=2 * w_uv.size, transcendentals=0
        ),
        name="combine",
    )(*blocks, w_uv)


def one_hot(shape, target):
    at = lax.broadcasted_iota(jnp.int32, shape, 1)
    return jnp.where(at == target(lax.broadcasted_iota(jnp.int32, shape, 0)), 1.0, 0.0).astype(
        jnp.bfloat16
    )


def out_proj_kernel(order, *refs):
    n_blocks = len(order)
    blocks, (w_o, residual, out) = refs[:n_blocks], refs[n_blocks:]
    blocks = [blocks[order.index(s)] for s in range(n_blocks)]
    per = blocks[0].shape[0]
    tokens = n_blocks * per
    stacked = stack_rows([b[...] for b in blocks])
    at_ctx, at_req = lax.axis_index("ctx"), lax.axis_index("req")
    order = one_hot((tokens, tokens), lambda row: (row // per ^ at_req) * per + row % per)
    ordered = jnp.dot(order, stacked, preferred_element_type=jnp.float32).astype(jnp.bfloat16)
    total = jnp.dot(ordered, w_o[...], preferred_element_type=jnp.float32)
    own = residual.shape[0]
    row = lax.broadcasted_iota(jnp.int32, total.shape, 0) - at_ctx * own
    rows = residual[...].astype(jnp.float32)
    for i in range(own):
        total += jnp.where(row == i, rows[i : i + 1], 0.0)
    out[...] = total.astype(out.dtype)


def out_proj(order, blocks, w_o, residual):
    n = len(blocks)
    tokens = n * blocks[0].shape[0]
    return pl.pallas_call(
        functools.partial(out_proj_kernel, order),
        out_shape=jax.ShapeDtypeStruct((tokens, w_o.shape[1]), jnp.bfloat16),
        in_specs=[VMEM] * (n + 2),
        out_specs=VMEM,
        compiler_params=pltpu.CompilerParams(vmem_limit_bytes=4 * MIB),
        cost_estimate=pl.CostEstimate(
            flops=2 * tokens * w_o.size, bytes_accessed=2 * w_o.size, transcendentals=0
        ),
        name="out_proj",
    )(*blocks, w_o, residual)


def add_products(totals, steps, blocks, gain, gate, up):
    n_exp = gate.shape[0]
    width = blocks[0].shape[1]
    for step, block in zip(steps, blocks):
        columns = pl.ds(0, width)
        if width < gate.shape[2]:
            columns = pl.ds(pl.multiple_of((lax.axis_index("req") ^ step) * width, LANES), width)
        rows = block[...].astype(jnp.float32) * gain[:, columns].astype(jnp.float32)
        rows = rows.astype(jnp.bfloat16)
        for m, weights in enumerate((gate, up)):
            for e in range(n_exp):
                product = lax.dot_general(
                    weights[e, :, columns], rows, NT, preferred_element_type=jnp.float32
                )
                at = m * n_exp + e
                totals[at] = product if totals[at] is None else totals[at] + product
    return totals


def part_kernel(steps, block, gain, gate, up, *refs):
    out = refs[-1]
    totals = add_products([None] * out.shape[0], steps, [block], gain, gate, up)
    for at, total in enumerate(totals):
        out[at] = total


def part(step, block, gain, w_gate, w_up, *held):
    n_exp, units, _ = w_gate.shape
    tokens, width = block.shape
    return pl.pallas_call(
        functools.partial(part_kernel, [step]),
        out_shape=pltpu.VMEM((2 * n_exp, units, tokens), jnp.float32),
        in_specs=[VMEM] * (4 + len(held)),
        out_specs=VMEM,
        compiler_params=pltpu.CompilerParams(vmem_limit_bytes=4 * MIB),
        cost_estimate=pl.CostEstimate(
            flops=4 * tokens * n_exp * units * width,
            bytes_accessed=4 * n_exp * units * width,
            transcendentals=0,
        ),
        name="part",
    )(block, gain, w_gate, w_up, *held)


def experts_kernel(order, n_parts, *refs):
    n_blocks = len(order)
    blocks, refs = refs[:n_blocks], refs[n_blocks:]
    parts, refs = refs[:n_parts], refs[n_parts:]
    gain, routes, weights, gate, up, down, out, kept, hidden, rows = refs
    at_ctx, at_req = lax.axis_index("ctx"), lax.axis_index("req")
    n_exp, units, model = gate.shape
    tokens = rows.shape[0]
    width = blocks[0].shape[1]
    totals = [None] * (2 * n_exp)
    for done in parts:
        totals = [done[at] if t is None else t + done[at] for at, t in enumerate(totals)]
    totals = add_products(totals, order[n_parts:], blocks[n_parts:], gain, gate, up)
    totals = [t.T for t in totals]
    for s, block in zip(order, blocks):
        if n_blocks == 1:
            rows[...] = block[...]
        else:
            offset = pl.multiple_of((at_req ^ s) * width, LANES)
            rows[:, pl.ds(offset, width)] = block[...]
    squares = sum(
        jnp.sum(jnp.square(b[...].astype(jnp.float32)), axis=-1, keepdims=True) for b in blocks
    )
    scale = lax.rsqrt(squares / model + NORM_EPS)
    eye = lax.broadcasted_iota(jnp.int32, (tokens, tokens), 0) == lax.broadcasted_iota(
        jnp.int32, (tokens, tokens), 1
    )
    for e in range(n_exp):
        named = jnp.where(routes[...] == at_req * n_exp + e, weights[...], 0.0)
        coef = jnp.sum(named, axis=0, keepdims=True)
        coef = jnp.sum(jnp.where(eye, coef, 0.0), axis=1, keepdims=True)
        active = jax.nn.silu(totals[e] * scale) * (totals[n_exp + e] * scale) * coef
        hidden[:, e * units : (e + 1) * units] = active.astype(jnp.bfloat16)
    sliced = len(out.shape) == 4
    if sliced:
        per, chunk = out.shape[2:]
        columns = pl.ds(pl.multiple_of(at_ctx * chunk, LANES), chunk)
        own = one_hot((per, tokens), lambda row: row + at_req * per)
        kept[...] = jnp.dot(own, rows[:, columns], preferred_element_type=jnp.float32)
        down_products(out, hidden, down, 1 - at_ctx % CORES)
    else:
        chunk = model // 8
        kept[...] = rows[...].astype(jnp.float32)
        for j in range(8):
            columns = slice(j * chunk, (j + 1) * chunk)
            part_down = down[:, :, columns].reshape(n_exp * units, chunk)
            total = jnp.dot(hidden[...], part_down, preferred_element_type=jnp.float32)
            out[:, columns] = total.astype(out.dtype)


def down_products(out, hidden, down, core):
    n_exp, units, _ = down.shape
    n_req, n_chips, per, chunk = out.shape
    for p in range(n_chips):
        columns = pl.ds(pl.multiple_of((p * CORES + core) * chunk, LANES), chunk)
        part_down = down[:, :, columns].reshape(n_exp * units, chunk)
        total = jnp.dot(hidden[...], part_down, preferred_element_type=jnp.float32)
        total = total.astype(out.dtype)
        for q in range(n_req):
            out[q, p] = total[q * per : (q + 1) * per]


def own_down_kernel(hidden, down, *refs):
    out = refs[-1]
    down_products(out, hidden, down, lax.axis_index("ctx") % CORES)


def own_down(hidden, w_down, shape, *held):
    weights = [pltpu.with_memory_space_constraint(w, pltpu.VMEM) for w in (w_down, *held)]
    return pl.pallas_call(
        own_down_kernel,
        out_shape=jax.ShapeDtypeStruct(shape, jnp.float32),
        in_specs=[VMEM] * (1 + len(weights)),
        out_specs=VMEM,
        compiler_params=pltpu.CompilerParams(vmem_limit_bytes=4 * MIB),
        cost_estimate=pl.CostEstimate(
            flops=hidden.shape[0] * w_down.size, bytes_accessed=w_down.size, transcendentals=0
        ),
        name="own_down",
    )(hidden, *weights)


def experts(order, blocks, gain, routes, route_weight, w_gate, w_up, w_down, n_req, n_ctx):
    n_exp, units, model = w_gate.shape
    tokens = blocks[0].shape[0]
    slice_width = model // n_ctx
    aligned = slice_width % LANES == 0
    w_gate, w_up, w_down = [
        pltpu.with_memory_space_constraint(w, pltpu.VMEM) for w in (w_gate, w_up, w_down)
    ]
    parts = []
    if len(blocks) > 2:
        parts = [part(order[i], blocks[i], gain, w_gate, w_up, w_down) for i in range(2)]
    shape = (n_req, n_ctx // CORES, tokens // n_req, slice_width) if aligned else (tokens, model)
    kept = (tokens // n_req, slice_width) if aligned else (tokens, model)
    return pl.pallas_call(
        functools.partial(experts_kernel, order, len(parts)),
        out_shape=[
            jax.ShapeDtypeStruct(shape, jnp.bfloat16),
            jax.ShapeDtypeStruct(kept, jnp.float32),
            jax.ShapeDtypeStruct((tokens, n_exp * units), jnp.bfloat16),
        ],
        in_specs=[VMEM] * (len(blocks) + len(parts) + 6),
        out_specs=[VMEM] * 3,
        scratch_shapes=[
            pltpu.VMEM((tokens, model), jnp.bfloat16),
        ],
        compiler_params=pltpu.CompilerParams(vmem_limit_bytes=4 * MIB),
        cost_estimate=pl.CostEstimate(
            flops=6 * tokens * w_gate.size,
            bytes_accessed=6 * w_gate.size,
            transcendentals=n_exp * units * tokens,
        ),
        name="experts",
    )(*blocks, *parts, gain, routes, route_weight, w_gate, w_up, w_down)


def local(
    residual,
    query,
    latent_cache,
    lengths,
    w_uv,
    w_o,
    norm_gain,
    routes,
    route_weight,
    w_gate,
    w_up,
    w_down,
):
    n_ctx = lax.axis_size("ctx")
    n_req = lax.axis_size("req")
    chip_steps = list(range(CORES, n_ctx, CORES))[::-1]
    order = [0] + sorted(range(1, n_req), key=lambda s: (s != n_req // 2, -s))
    req_local = latent_cache.shape[0]
    heads_local, lat_width, _ = w_uv.shape
    tok_local = query.shape[0]
    q_tokens = tok_local // req_local

    cache = jnp.swapaxes(latent_cache, 1, 2)
    other_cache = swap(cache, "ctx", 1, n_ctx)
    query = query.reshape(req_local, q_tokens * heads_local, query.shape[2])
    received = [swap(query, "ctx", s, n_ctx) for s in chip_steps]
    cache, query, w_uv, w_o = stage([cache, query, w_uv, w_o])
    blocks = [query] + received
    outs = attend(blocks, (cache, other_cache), lengths, lat_width, q_tokens)
    outs = [outs[0]] + [swap(o, "ctx", s, n_ctx) for o, s in zip(outs[1:], chip_steps)]

    head_values = combine(outs, w_uv)
    blocks = [head_values] + [swap(head_values, "req", s, n_req) for s in order[1:]]
    partial_mid = out_proj(order, blocks, w_o, residual)

    pieces = [partial_mid] + [swap(partial_mid, "ctx", s, n_ctx) for s in chip_steps]
    core_mid = sum(p.astype(jnp.float32) for p in pieces).astype(jnp.bfloat16)
    other = swap(core_mid, "ctx", 1, n_ctx)
    mid = (core_mid.astype(jnp.float32) + other.astype(jnp.float32)).astype(jnp.bfloat16)
    if mid.shape[1] % LANES == 0:
        blocks = [mid] + [swap(mid, "req", s, n_req) for s in order[1:]]
    else:
        order = [0]
        blocks = [lax.all_gather(mid, "req", axis=1, tiled=True)]

    partial_sum, kept, hidden = experts(
        order,
        blocks,
        norm_gain.reshape(1, -1),
        routes.T,
        route_weight.T,
        w_gate,
        w_up,
        w_down,
        n_req,
        n_ctx,
    )
    tokens = mid.shape[0]
    model_width = w_gate.shape[2]
    rows_out = tokens // n_req
    slice_width = model_width // n_ctx
    groups = None
    if partial_sum.ndim == 2:
        partial_sum = partial_sum.reshape(n_req, rows_out, n_ctx, slice_width)
        partial_sum = jnp.swapaxes(partial_sum, 1, 2)
        kept = lax.dynamic_slice(
            kept,
            (lax.axis_index("req") * rows_out, lax.axis_index("ctx") * slice_width),
            (rows_out, slice_width),
        )
    else:
        other = swap(partial_sum, "ctx", 1, n_ctx)
        own = own_down(hidden, w_down, partial_sum.shape, w_gate, w_up)
        partial_sum = (own + other.astype(jnp.float32)).astype(jnp.bfloat16)
        groups = [list(range(core, n_req * n_ctx, CORES)) for core in range(CORES)]
    partial_sum = partial_sum.reshape(-1, rows_out, slice_width)
    landed = lax.all_to_all(
        partial_sum,
        ("req", "ctx"),
        split_axis=0,
        concat_axis=0,
        axis_index_groups=groups,
        tiled=True,
    )
    return (kept + jnp.sum(landed.astype(jnp.float32), axis=0)).astype(jnp.bfloat16)


def solution(mesh):
    in_specs = (
        P("ctx", "req"),
        P("req", "ctx", None),
        P("req", "ctx", None),
        P("req"),
        P("ctx", None, None),
        P("ctx", "req"),
        P(),
        P(),
        P(),
        P("req", "ctx", None),
        P("req", "ctx", None),
        P("req", "ctx", None),
    )
    out_specs = P("req", "ctx")
    return jax.shard_map(local, mesh=mesh, in_specs=in_specs, out_specs=out_specs, check_vma=False)
```

```python
import functools

import jax
import jax.numpy as jnp
from jax import lax
from jax.experimental import pallas as pl
from jax.experimental.pallas import tpu as pltpu
from jax.sharding import PartitionSpec as P

SOFTMAX_SCALE = 192.0 ** (-0.5)
NEG_FILL = -1e30
NORM_EPS = 1e-06
CORES = 2
OVERLAP = 60
LANES = 128
LOG_ROWS = 16
MIB = 1 << 20
NT = (((1,), (1,)), ((), ()))
VMEM = pl.BlockSpec(memory_space=pltpu.VMEM)
HBM = pl.BlockSpec(memory_space=pltpu.HBM)


def swap(x, axis, step, size):
    return lax.ppermute(x, axis, [(i, i ^ step) for i in range(size)])


def stack_rows(blocks):
    if len(blocks) == 1:
        return blocks[0]
    if all(b.shape[0] % 16 == 0 for b in blocks):
        return jnp.concatenate(blocks, axis=0)
    return jnp.concatenate([b.astype(jnp.float32) for b in blocks], axis=0).astype(blocks[0].dtype)


def attend_kernel(n_blocks, q_tokens, width, lengths, *refs):
    queries, caches, outs = refs[:n_blocks], refs[n_blocks : n_blocks + 2], refs[n_blocks + 2 :]
    req_local, rows, _ = queries[0].shape
    ctx_local = caches[0].shape[2]
    total_rows = n_blocks * rows
    heads_local = rows // q_tokens
    row = lax.broadcasted_iota(jnp.int32, (total_rows, ctx_local), 0)
    column = lax.broadcasted_iota(jnp.int32, (total_rows, ctx_local), 1)
    token = (row // heads_local) % q_tokens
    means, log_rows = [], [jnp.zeros((1, LANES), jnp.float32)] * n_blocks
    for r in range(req_local):
        grouped = stack_rows([q[r] for q in queries])
        limit = lengths[:, r : r + 1] - q_tokens + token
        masked = []
        for half, cache in enumerate(caches):
            score = jnp.dot(grouped, cache[r], preferred_element_type=jnp.float32)
            visible = column + (lax.axis_index("ctx") ^ half) * ctx_local <= limit
            masked.append(jnp.where(visible, score * SOFTMAX_SCALE, -jnp.inf))
        peak = jnp.maximum(
            jnp.max(masked[0], axis=-1, keepdims=True), jnp.max(masked[1], axis=-1, keepdims=True)
        )
        peak = jnp.where(peak > -jnp.inf, peak, 0.0)
        total = jnp.zeros((total_rows, 1), jnp.float32)
        mixed = jnp.zeros((total_rows, width), jnp.float32)
        for scores, cache in zip(masked, caches):
            raised = jnp.exp(scores - peak)
            total += jnp.sum(raised, axis=-1, keepdims=True)
            mixed += lax.dot_general(
                raised.astype(jnp.bfloat16),
                cache[r, :width, :],
                NT,
                preferred_element_type=jnp.float32,
            )
        filled = total > 0.0
        safe = jnp.where(filled, total, 1.0)
        mean = jnp.where(filled, mixed / safe, 0.0).astype(jnp.bfloat16)
        log = jnp.where(filled, peak + jnp.log(safe), NEG_FILL)
        high = log.astype(jnp.bfloat16).astype(jnp.float32)
        means.append(mean)
        for s in range(n_blocks):
            block = slice(s * rows, (s + 1) * rows)
            logs = log_lanes(
                lambda where_high, where_low: jnp.where(
                    where_high, high[block], jnp.where(where_low, (log - high)[block], 0.0)
                ),
                rows,
                r * rows,
            )
            log_rows[s] += jnp.sum(logs, axis=0, keepdims=True)
    packed = req_local * rows
    for s, (row, out) in enumerate(zip(log_rows, outs)):
        for i in range(width // LANES):
            columns = slice(i * LANES, (i + 1) * LANES)
            out[i * packed : (i + 1) * packed] = stack_rows(
                [mean[s * rows : (s + 1) * rows, columns] for mean in means]
            )
        spread = jnp.broadcast_to(row, (LOG_ROWS, LANES))
        out[out.shape[0] - LOG_ROWS :] = spread.astype(jnp.bfloat16)


def log_lanes(pick, rows, start):
    row = start + lax.broadcasted_iota(jnp.int32, (rows, LANES), 0)
    lane = lax.broadcasted_iota(jnp.int32, (rows, LANES), 1)
    return pick(lane == row, lane == row + LANES // 2)


def attend(blocks, caches, lengths, width, q_tokens):
    req_local, rows, lat = blocks[0].shape
    n = len(blocks)
    ctx_local = caches[0].shape[2]
    packed = req_local * rows * width // LANES + LOG_ROWS
    shape = jax.ShapeDtypeStruct((packed, LANES), jnp.bfloat16)
    return pl.pallas_call(
        functools.partial(attend_kernel, n, q_tokens, width),
        out_shape=[shape] * n,
        in_specs=[VMEM] * (n + 3),
        out_specs=[VMEM] * n,
        compiler_params=pltpu.CompilerParams(vmem_limit_bytes=4 * MIB),
        cost_estimate=pl.CostEstimate(
            flops=OVERLAP * 4 * req_local * n * rows * ctx_local * (lat + width),
            bytes_accessed=4 * req_local * ctx_local * lat,
            transcendentals=2 * req_local * n * rows * ctx_local,
        ),
        name="attend",
    )(lengths.reshape(1, -1), *blocks, *caches)


def stage_kernel(*refs):
    n = len(refs) // 2
    sems = refs[-1]
    copies = [
        pltpu.make_async_copy(source, target, sems.at[i])
        for i, (source, target) in enumerate(zip(refs[:n], refs[n : 2 * n]))
    ]
    for copy in copies:
        copy.start()
    for copy in copies:
        copy.wait()


def stage(arrays):
    return pl.pallas_call(
        stage_kernel,
        out_shape=[pltpu.VMEM(x.shape, x.dtype) for x in arrays],
        in_specs=[HBM] * len(arrays),
        out_specs=[VMEM] * len(arrays),
        scratch_shapes=[pltpu.SemaphoreType.DMA((len(arrays),))],
        compiler_params=pltpu.CompilerParams(vmem_limit_bytes=4 * MIB),
        cost_estimate=pl.CostEstimate(
            flops=0, bytes_accessed=sum(x.size * 2 for x in arrays), transcendentals=0
        ),
        name="stage",
    )(*[pltpu.with_memory_space_constraint(x, pltpu.HBM) for x in arrays])


def combine_kernel(n_blocks, *refs):
    blocks, (w_uv, out) = refs[:n_blocks], refs[n_blocks:]
    heads, width, value_width = w_uv.shape
    total_rows = (blocks[0].shape[0] - LOG_ROWS) * LANES // width
    parts, logs = [], []
    for block in blocks:
        columns = [
            block[i * total_rows : (i + 1) * total_rows].astype(jnp.float32)
            for i in range(width // LANES)
        ]
        parts.append(jnp.concatenate(columns, axis=1))
        row = block[block.shape[0] - LOG_ROWS :].astype(jnp.float32)[:1]
        lanes = log_lanes(lambda high, low: jnp.where(high | low, row, 0.0), total_rows, 0)
        logs.append(jnp.sum(lanes, axis=1, keepdims=True))
    top = functools.reduce(jnp.maximum, logs)
    factors = [jnp.exp(log - top) for log in logs]
    numer = sum(f * p for f, p in zip(factors, parts))
    latent = (numer / sum(factors)).astype(jnp.bfloat16)
    head = lax.broadcasted_iota(jnp.int32, (total_rows, value_width), 0) % heads
    values = []
    for h in range(heads):
        value = jnp.dot(latent, w_uv[h], preferred_element_type=jnp.float32)
        values.append(jnp.where(head == h, value, 0.0).astype(jnp.bfloat16))
    values = jnp.concatenate(values, axis=1)
    tokens = total_rows // heads
    token = lax.broadcasted_iota(jnp.int32, (tokens, total_rows), 0)
    at = lax.broadcasted_iota(jnp.int32, (tokens, total_rows), 1)
    fold = jnp.where(at // heads == token, 1.0, 0.0).astype(jnp.bfloat16)
    out[...] = jnp.dot(fold, values, preferred_element_type=jnp.float32).astype(out.dtype)


def combine(blocks, w_uv):
    heads, width, value_width = w_uv.shape
    rows = (blocks[0].shape[0] - LOG_ROWS) * LANES // width
    tokens = rows // heads
    return pl.pallas_call(
        functools.partial(combine_kernel, len(blocks)),
        out_shape=jax.ShapeDtypeStruct((tokens, heads * value_width), jnp.bfloat16),
        in_specs=[VMEM] * (len(blocks) + 1),
        out_specs=VMEM,
        compiler_params=pltpu.CompilerParams(vmem_limit_bytes=4 * MIB),
        cost_estimate=pl.CostEstimate(
            flops=2 * rows * w_uv.size, bytes_accessed=2 * w_uv.size, transcendentals=0
        ),
        name="combine",
    )(*blocks, w_uv)


def one_hot(shape, target):
    at = lax.broadcasted_iota(jnp.int32, shape, 1)
    return jnp.where(at == target(lax.broadcasted_iota(jnp.int32, shape, 0)), 1.0, 0.0).astype(
        jnp.bfloat16
    )


def out_proj_kernel(order, *refs):
    n_blocks = len(order)
    blocks, (w_o, residual, out) = refs[:n_blocks], refs[n_blocks:]
    blocks = [blocks[order.index(s)] for s in range(n_blocks)]
    per = blocks[0].shape[0]
    tokens = n_blocks * per
    stacked = stack_rows([b[...] for b in blocks])
    at_ctx, at_req = lax.axis_index("ctx"), lax.axis_index("req")
    order = one_hot((tokens, tokens), lambda row: (row // per ^ at_req) * per + row % per)
    ordered = jnp.dot(order, stacked, preferred_element_type=jnp.float32).astype(jnp.bfloat16)
    total = jnp.dot(ordered, w_o[...], preferred_element_type=jnp.float32)
    own = residual.shape[0]
    row = lax.broadcasted_iota(jnp.int32, total.shape, 0) - at_ctx * own
    rows = residual[...].astype(jnp.float32)
    for i in range(own):
        total += jnp.where(row == i, rows[i : i + 1], 0.0)
    out[...] = total.astype(out.dtype)


def out_proj(order, blocks, w_o, residual):
    n = len(blocks)
    tokens = n * blocks[0].shape[0]
    return pl.pallas_call(
        functools.partial(out_proj_kernel, order),
        out_shape=jax.ShapeDtypeStruct((tokens, w_o.shape[1]), jnp.bfloat16),
        in_specs=[VMEM] * (n + 2),
        out_specs=VMEM,
        compiler_params=pltpu.CompilerParams(vmem_limit_bytes=4 * MIB),
        cost_estimate=pl.CostEstimate(
            flops=2 * tokens * w_o.size, bytes_accessed=2 * w_o.size, transcendentals=0
        ),
        name="out_proj",
    )(*blocks, w_o, residual)


def add_products(totals, steps, blocks, gain, gate, up):
    n_exp = gate.shape[0]
    width = blocks[0].shape[1]
    for step, block in zip(steps, blocks):
        columns = pl.ds(0, width)
        if width < gate.shape[2]:
            columns = pl.ds(pl.multiple_of((lax.axis_index("req") ^ step) * width, LANES), width)
        rows = block[...].astype(jnp.float32) * gain[:, columns].astype(jnp.float32)
        rows = rows.astype(jnp.bfloat16)
        for m, weights in enumerate((gate, up)):
            for e in range(n_exp):
                product = lax.dot_general(
                    weights[e, :, columns], rows, NT, preferred_element_type=jnp.float32
                )
                at = m * n_exp + e
                totals[at] = product if totals[at] is None else totals[at] + product
    return totals


def part_kernel(steps, block, gain, gate, up, *refs):
    out = refs[-1]
    totals = add_products([None] * out.shape[0], steps, [block], gain, gate, up)
    for at, total in enumerate(totals):
        out[at] = total


def part(step, block, gain, w_gate, w_up, *held):
    n_exp, units, _ = w_gate.shape
    tokens, width = block.shape
    return pl.pallas_call(
        functools.partial(part_kernel, [step]),
        out_shape=pltpu.VMEM((2 * n_exp, units, tokens), jnp.float32),
        in_specs=[VMEM] * (4 + len(held)),
        out_specs=VMEM,
        compiler_params=pltpu.CompilerParams(vmem_limit_bytes=4 * MIB),
        cost_estimate=pl.CostEstimate(
            flops=4 * tokens * n_exp * units * width,
            bytes_accessed=4 * n_exp * units * width,
            transcendentals=0,
        ),
        name="part",
    )(block, gain, w_gate, w_up, *held)


def experts_kernel(order, n_parts, *refs):
    n_blocks = len(order)
    blocks, refs = refs[:n_blocks], refs[n_blocks:]
    parts, refs = refs[:n_parts], refs[n_parts:]
    gain, routes, weights, gate, up, down, out, kept, hidden, rows = refs
    at_ctx, at_req = lax.axis_index("ctx"), lax.axis_index("req")
    n_exp, units, model = gate.shape
    tokens = rows.shape[0]
    width = blocks[0].shape[1]
    totals = [None] * (2 * n_exp)
    for done in parts:
        totals = [done[at] if t is None else t + done[at] for at, t in enumerate(totals)]
    totals = add_products(totals, order[n_parts:], blocks[n_parts:], gain, gate, up)
    totals = [t.T for t in totals]
    for s, block in zip(order, blocks):
        if n_blocks == 1:
            rows[...] = block[...]
        else:
            offset = pl.multiple_of((at_req ^ s) * width, LANES)
            rows[:, pl.ds(offset, width)] = block[...]
    squares = sum(
        jnp.sum(jnp.square(b[...].astype(jnp.float32)), axis=-1, keepdims=True) for b in blocks
    )
    scale = lax.rsqrt(squares / model + NORM_EPS)
    eye = lax.broadcasted_iota(jnp.int32, (tokens, tokens), 0) == lax.broadcasted_iota(
        jnp.int32, (tokens, tokens), 1
    )
    for e in range(n_exp):
        named = jnp.where(routes[...] == at_req * n_exp + e, weights[...], 0.0)
        coef = jnp.sum(named, axis=0, keepdims=True)
        coef = jnp.sum(jnp.where(eye, coef, 0.0), axis=1, keepdims=True)
        active = jax.nn.silu(totals[e] * scale) * (totals[n_exp + e] * scale) * coef
        hidden[:, e * units : (e + 1) * units] = active.astype(jnp.bfloat16)
    sliced = len(out.shape) == 4
    if sliced:
        per, chunk = out.shape[2:]
        columns = pl.ds(pl.multiple_of(at_ctx * chunk, LANES), chunk)
        own = one_hot((per, tokens), lambda row: row + at_req * per)
        kept[...] = jnp.dot(own, rows[:, columns], preferred_element_type=jnp.float32)
        down_products(out, hidden, down, 1 - at_ctx % CORES)
    else:
        chunk = model // 8
        kept[...] = rows[...].astype(jnp.float32)
        for j in range(8):
            columns = slice(j * chunk, (j + 1) * chunk)
            part_down = down[:, :, columns].reshape(n_exp * units, chunk)
            total = jnp.dot(hidden[...], part_down, preferred_element_type=jnp.float32)
            out[:, columns] = total.astype(out.dtype)


def down_products(out, hidden, down, core):
    n_exp, units, _ = down.shape
    n_req, n_chips, per, chunk = out.shape
    for p in range(n_chips):
        columns = pl.ds(pl.multiple_of((p * CORES + core) * chunk, LANES), chunk)
        part_down = down[:, :, columns].reshape(n_exp * units, chunk)
        total = jnp.dot(hidden[...], part_down, preferred_element_type=jnp.float32)
        total = total.astype(out.dtype)
        for q in range(n_req):
            out[q, p] = total[q * per : (q + 1) * per]


def own_down_kernel(hidden, down, *refs):
    out = refs[-1]
    down_products(out, hidden, down, lax.axis_index("ctx") % CORES)


def own_down(hidden, w_down, shape, *held):
    weights = [pltpu.with_memory_space_constraint(w, pltpu.VMEM) for w in (w_down, *held)]
    return pl.pallas_call(
        own_down_kernel,
        out_shape=jax.ShapeDtypeStruct(shape, jnp.float32),
        in_specs=[VMEM] * (1 + len(weights)),
        out_specs=VMEM,
        compiler_params=pltpu.CompilerParams(vmem_limit_bytes=4 * MIB),
        cost_estimate=pl.CostEstimate(
            flops=hidden.shape[0] * w_down.size, bytes_accessed=w_down.size, transcendentals=0
        ),
        name="own_down",
    )(hidden, *weights)


def experts(order, blocks, gain, routes, route_weight, w_gate, w_up, w_down, n_req, n_ctx):
    n_exp, units, model = w_gate.shape
    tokens = blocks[0].shape[0]
    slice_width = model // n_ctx
    aligned = slice_width % LANES == 0
    w_gate, w_up, w_down = [
        pltpu.with_memory_space_constraint(w, pltpu.VMEM) for w in (w_gate, w_up, w_down)
    ]
    parts = []
    if len(blocks) > 2:
        parts = [part(order[i], blocks[i], gain, w_gate, w_up, w_down) for i in range(2)]
    shape = (n_req, n_ctx // CORES, tokens // n_req, slice_width) if aligned else (tokens, model)
    kept = (tokens // n_req, slice_width) if aligned else (tokens, model)
    return pl.pallas_call(
        functools.partial(experts_kernel, order, len(parts)),
        out_shape=[
            jax.ShapeDtypeStruct(shape, jnp.bfloat16),
            jax.ShapeDtypeStruct(kept, jnp.float32),
            jax.ShapeDtypeStruct((tokens, n_exp * units), jnp.bfloat16),
        ],
        in_specs=[VMEM] * (len(blocks) + len(parts) + 6),
        out_specs=[VMEM] * 3,
        scratch_shapes=[
            pltpu.VMEM((tokens, model), jnp.bfloat16),
        ],
        compiler_params=pltpu.CompilerParams(vmem_limit_bytes=4 * MIB),
        cost_estimate=pl.CostEstimate(
            flops=6 * tokens * w_gate.size,
            bytes_accessed=6 * w_gate.size,
            transcendentals=n_exp * units * tokens,
        ),
        name="experts",
    )(*blocks, *parts, gain, routes, route_weight, w_gate, w_up, w_down)


def local(
    residual,
    query,
    latent_cache,
    lengths,
    w_uv,
    w_o,
    norm_gain,
    routes,
    route_weight,
    w_gate,
    w_up,
    w_down,
):
    n_ctx = lax.axis_size("ctx")
    n_req = lax.axis_size("req")
    chip_steps = list(range(CORES, n_ctx, CORES))[::-1]
    order = [0] + sorted(range(1, n_req), key=lambda s: (s != n_req // 2, -s))
    req_local = latent_cache.shape[0]
    heads_local, lat_width, _ = w_uv.shape
    tok_local = query.shape[0]
    q_tokens = tok_local // req_local

    cache = jnp.swapaxes(latent_cache, 1, 2)
    other_cache = swap(cache, "ctx", 1, n_ctx)
    query = query.reshape(req_local, q_tokens * heads_local, query.shape[2])
    received = [swap(query, "ctx", s, n_ctx) for s in chip_steps]
    cache, query, w_uv, w_o = stage([cache, query, w_uv, w_o])
    blocks = [query] + received
    outs = attend(blocks, (cache, other_cache), lengths, lat_width, q_tokens)
    outs = [outs[0]] + [swap(o, "ctx", s, n_ctx) for o, s in zip(outs[1:], chip_steps)]

    head_values = combine(outs, w_uv)
    blocks = [head_values] + [swap(head_values, "req", s, n_req) for s in order[1:]]
    partial_mid = out_proj(order, blocks, w_o, residual)

    other = swap(partial_mid, "ctx", 1, n_ctx)
    chip_mid = (partial_mid.astype(jnp.float32) + other.astype(jnp.float32)).astype(jnp.bfloat16)
    pieces = [chip_mid] + [swap(chip_mid, "ctx", s, n_ctx) for s in chip_steps]
    mid = sum(p.astype(jnp.float32) for p in pieces).astype(jnp.bfloat16)
    if mid.shape[1] % LANES == 0:
        order = [0, 1, *range(n_req - 1, 1, -1)]
        blocks = [mid] + [swap(mid, "req", s, n_req) for s in order[1:]]
    else:
        order = [0]
        blocks = [lax.all_gather(mid, "req", axis=1, tiled=True)]

    partial_sum, kept, hidden = experts(
        order,
        blocks,
        norm_gain.reshape(1, -1),
        routes.T,
        route_weight.T,
        w_gate,
        w_up,
        w_down,
        n_req,
        n_ctx,
    )
    tokens = mid.shape[0]
    model_width = w_gate.shape[2]
    rows_out = tokens // n_req
    slice_width = model_width // n_ctx
    groups = None
    if partial_sum.ndim == 2:
        partial_sum = partial_sum.reshape(n_req, rows_out, n_ctx, slice_width)
        partial_sum = jnp.swapaxes(partial_sum, 1, 2)
        kept = lax.dynamic_slice(
            kept,
            (lax.axis_index("req") * rows_out, lax.axis_index("ctx") * slice_width),
            (rows_out, slice_width),
        )
    else:
        other = swap(partial_sum, "ctx", 1, n_ctx)
        own = own_down(hidden, w_down, partial_sum.shape, w_gate, w_up)
        partial_sum = (own + other.astype(jnp.float32)).astype(jnp.bfloat16)
        groups = [list(range(core, n_req * n_ctx, CORES)) for core in range(CORES)]
    partial_sum = partial_sum.reshape(-1, rows_out, slice_width)
    landed = lax.all_to_all(
        partial_sum,
        ("req", "ctx"),
        split_axis=0,
        concat_axis=0,
        axis_index_groups=groups,
        tiled=True,
    )
    return (kept + jnp.sum(landed.astype(jnp.float32), axis=0)).astype(jnp.bfloat16)


def solution(mesh):
    in_specs = (
        P("ctx", "req"),
        P("req", "ctx", None),
        P("req", "ctx", None),
        P("req"),
        P("ctx", None, None),
        P("ctx", "req"),
        P(),
        P(),
        P(),
        P("req", "ctx", None),
        P("req", "ctx", None),
        P("req", "ctx", None),
    )
    out_specs = P("req", "ctx")
    return jax.shard_map(local, mesh=mesh, in_specs=in_specs, out_specs=out_specs, check_vma=False)
```
